32 devices in a mesh: gx: 8 (over z, y), gy: 4 (over x, core).
Axes of the slice: x: 2, y: 2, z: 4, core: 2. Of those that a mesh axis runs over, the one named last changes fastest.
Arguments:
- populations: float32 [4, 16, 19, 4096], P('gy', 'gx'), may hold values from 0 to 0.67
- solid_mask: int32 [4, 16, 4096], P('gy', 'gx'), may hold values from 0 to 1, as said below
- slot_blocks: int32 [4, 16], P('gy', 'gx'), may hold values from 0 to 15, as said below
- swap_slots: int32 [4, 8, 3, 2], P('gy', 'gx'), may hold values from 0 to 1, as said below
Outputs:
- moved_populations: float32 [4, 16, 19, 4096], P('gy', 'gx')
The draws below stay inside these ranges and needn't reach their ends.
Inputs may be any that keep to these rules, and one draw needn't show every extreme that they name: `slot_blocks`: each slab's row is a permutation of its 16 block numbers. `swap_slots`: for each slab, owner and round, 2 distinct slot numbers of that owner. `solid_mask`: every block is either rock throughout or holds fluid cells.
All inputs are finite; a program needn't handle non-finite values.
Results may differ from the reference program's by a relative error of at most 0.0003.
Values sent between devices are 32-bit elements; how exact they have to be, the bound alone decides.
No kernel may reach another device: no remote copies, remote signals or barrier semaphores. Data moves between devices by JAX's collectives and lax.ppermute only.
A program may use at most 64 MiB of HBM per device.

```python
import jax
import jax.numpy as jnp
import numpy as np
from jax import lax

B = 16
NB = 2
MOVE = 2
STEPS = 2
N_GX = 8
N_GY = 4


WEIGHTS = (1.0 / 3.0,) + (1.0 / 18.0,) * 6 + (1.0 / 36.0,) * 12


def arrangement(key):
    group_size = N_GX * NB
    order_key, device_key, swap_key = jax.random.split(key, 3)
    orders = jax.vmap(lambda subkey: jax.random.permutation(subkey, group_size))(jax.random.split(order_key, N_GY))
    device_rows = jax.vmap(lambda subkey: jax.random.permutation(subkey, N_GX))(jax.random.split(device_key, N_GY))
    rows_of = orders.reshape(N_GY, N_GX, NB)
    placed = jax.vmap(lambda rows_here, picked: rows_here[picked])(rows_of, device_rows)
    position = device_rows[:, :, None] * NB + jnp.arange(NB)[None, None, :]
    bearing = (position < group_size // 4).astype(jnp.int32)
    slab_index = jnp.arange(N_GY)[:, None, None]
    owner_index = jnp.arange(N_GX)[None, :, None]
    state_now = bearing
    swap_lists = []
    for round_bit in range(3):
        partner = jnp.bitwise_xor(jnp.arange(N_GX), 1 << round_bit)
        load_now = jnp.sum(state_now, axis=2)
        busier = load_now > load_now[:, partner]
        primary = jnp.where(busier[:, :, None], 1 - state_now, state_now)
        shuffle = jax.vmap(lambda subkey: jax.random.permutation(subkey, NB))(jax.random.split(jax.random.fold_in(swap_key, round_bit), N_GY * N_GX)).reshape(N_GY, N_GX, NB)
        ranking = jnp.argsort(primary * NB + shuffle, axis=2)
        chosen = ranking[:, :, :MOVE]
        leaving = jnp.take_along_axis(state_now, chosen, axis=2)
        state_now = state_now.at[slab_index, owner_index, chosen].set(leaving[:, partner, :])
        swap_lists.append(chosen)
    return (placed.reshape(N_GY, group_size), bearing.reshape(N_GY, group_size), jnp.stack(swap_lists, axis=2))


def draw_slot_blocks(key, part):
    placed, bearing, swap_lists = arrangement(key)
    return placed.astype(jnp.int32)


def draw_swap_slots(key, part):
    placed, bearing, swap_lists = arrangement(key)
    return swap_lists.astype(jnp.int32)


def draw_solid_mask(key, part):
    placed, bearing, swap_lists = arrangement(key)
    key = jax.random.fold_in(key, 7)
    porosity_key, cell_key = jax.random.split(key)
    porosity = jax.random.randint(porosity_key, (N_GY, N_GX * NB, 1), 30, 90)
    chance = jax.random.randint(cell_key, (N_GY, N_GX * NB, B * B * B), 0, 100)
    return ((chance < porosity).astype(jnp.int32) * bearing[:, :, None]).astype(jnp.int32)


def draw_populations(key, part):
    key = jax.random.fold_in(key, 11)
    shape_full = (N_GY, N_GX * NB, 19, B * B * B)
    noise_term = jnp.clip(0.35 * jax.random.normal(key, shape_full, jnp.float32), -1.0, 1.0)
    weights = jnp.asarray(WEIGHTS, dtype=jnp.float32)
    return (weights[None, None, :, None] * (1.0 + noise_term)).astype(jnp.float32)


def setup_inputs(seed: int = 0) -> dict:
    streams_of = jax.random.split(jax.random.key(seed), 5)
    return {
        "populations": draw_populations(jax.random.fold_in(streams_of[4], 71), 0),
        "solid_mask": draw_solid_mask(jax.random.fold_in(streams_of[4], 71), 0),
        "slot_blocks": draw_slot_blocks(jax.random.fold_in(streams_of[4], 71), 0),
        "swap_slots": draw_swap_slots(jax.random.fold_in(streams_of[4], 71), 0),
    }


VELOCITIES = ((0, 0, 0), (1, 0, 0), (-1, 0, 0), (0, 1, 0), (0, -1, 0), (0, 0, 1), (0, 0, -1), (1, 1, 0), (-1, -1, 0), (1, -1, 0), (-1, 1, 0), (1, 0, 1), (-1, 0, -1), (1, 0, -1), (-1, 0, 1), (0, 1, 1), (0, -1, -1), (0, 1, -1), (0, -1, 1))
OPPOSITE = (0, 2, 1, 4, 3, 6, 5, 8, 7, 10, 9, 12, 11, 14, 13, 16, 15, 18, 17)
WEIGHTS = (1.0 / 3.0,) + (1.0 / 18.0,) * 6 + (1.0 / 36.0,) * 12
RATES = (0.0, 0.0, 0.0, 0.0) + (1.25,) * 6 + (1.5,) * 6 + (1.3,) * 3

def device_tables():
    velocity = jnp.asarray(VELOCITIES, dtype=jnp.float32)
    x_part = velocity[:, 0]
    y_part = velocity[:, 1]
    z_part = velocity[:, 2]
    polynomials = jnp.stack([jnp.ones((19,), jnp.float32), x_part, y_part, z_part, x_part * x_part, y_part * y_part, z_part * z_part, x_part * y_part, x_part * z_part, y_part * z_part, x_part * x_part * y_part, x_part * x_part * z_part, y_part * y_part * x_part, y_part * y_part * z_part, z_part * z_part * x_part, z_part * z_part * y_part, x_part * x_part * y_part * y_part, x_part * x_part * z_part * z_part, y_part * y_part * z_part * z_part])
    rates = jnp.asarray(RATES, dtype=jnp.float32)
    scaled = rates[:, None] * polynomials
    gram = jnp.dot(polynomials, polynomials.T, precision=lax.Precision.HIGHEST)
    lower = jnp.linalg.cholesky(gram)
    solved = jax.scipy.linalg.cho_solve((lower, True), scaled)
    relaxation = jnp.dot(polynomials.T, solved, precision=lax.Precision.HIGHEST)
    weights = jnp.asarray(WEIGHTS, dtype=jnp.float32)
    return (relaxation, velocity, weights)

def collide(current, fluid_cells, tables):
    relaxation, velocity, weights = tables
    density = jnp.sum(current, axis=-2)
    momentum = jnp.einsum('iv,...ic->...vc', velocity, current, precision=lax.Precision.HIGHEST)
    projected = jnp.einsum('iv,...vc->...ic', velocity, momentum, precision=lax.Precision.HIGHEST)
    squared = jnp.sum(momentum * momentum, axis=-2)
    equilibrium = weights[:, None] * (density[..., None, :] + 3.0 * projected + 4.5 * projected * projected - 1.5 * squared[..., None, :])
    relaxed = current - jnp.einsum('ij,...jc->...ic', relaxation, current - equilibrium, precision=lax.Precision.HIGHEST)
    bounced = current[..., np.array(OPPOSITE, dtype=np.int32), :]
    return jnp.where(fluid_cells[..., None, :] > 0, relaxed, bounced)

def reference(populations, solid_mask, slot_blocks, swap_slots):
    tables = device_tables()
    slab_count = N_GY
    group_size = N_GX * NB
    inverse = jnp.argsort(slot_blocks, axis=1).astype(jnp.int32)
    pick_rows = jax.vmap(lambda rows_here, picked: jnp.take(rows_here, picked, axis=0))
    block_pops = pick_rows(populations, inverse)
    block_fluid = pick_rows(solid_mask, inverse)
    lattice = block_pops.reshape(slab_count, N_GX, NB, 19, B, B, B).transpose(0, 4, 3, 1, 5, 2, 6)
    lattice = lattice.reshape(slab_count * B, 19, N_GX * B * NB * B)
    fluid_lattice = block_fluid.reshape(slab_count, N_GX, NB, B, B, B).transpose(0, 3, 1, 4, 2, 5)
    fluid_lattice = fluid_lattice.reshape(slab_count * B, N_GX * B * NB * B)
    for step_index in range(STEPS):
        collided = lax.map(lambda row_pair: collide(row_pair[0], row_pair[1], tables), (lattice, fluid_lattice))
        collided = collided.reshape(slab_count * B, 19, N_GX * B, NB * B)
        passed = []
        for direction in range(19):
            shift_by = VELOCITIES[direction]
            passed.append(jnp.roll(collided[:, direction], shift_by, axis=(0, 1, 2)))
        lattice = jnp.stack(passed, axis=1).reshape(slab_count * B, 19, N_GX * B * NB * B)
    final_blocks = lattice.reshape(slab_count, B, 19, N_GX, B, NB, B).transpose(0, 3, 5, 2, 1, 4, 6)
    final_blocks = final_blocks.reshape(slab_count, group_size, 19, B * B * B)
    placement = slot_blocks.reshape(slab_count, N_GX, NB)
    slab_index = jnp.arange(slab_count).astype(jnp.int32)[:, None, None]
    owner_index = jnp.arange(N_GX).astype(jnp.int32)[None, :, None]
    for round_bit in range(3):
        partner = jnp.bitwise_xor(jnp.arange(N_GX).astype(jnp.int32), 1 << round_bit)
        chosen = swap_slots[:, :, round_bit, :]
        leaving = jnp.take_along_axis(placement, chosen, axis=2)
        arriving = leaving[:, partner, :]
        placement = placement.at[slab_index, owner_index, chosen].set(arriving)
    return pick_rows(final_blocks, placement.reshape(slab_count, group_size))
```

```python
import jax
import jax.numpy as jnp
from jax import lax
from jax.experimental import pallas as pl
from jax.experimental.pallas import tpu as pltpu
from jax.sharding import PartitionSpec as P

B = 16
NB = 2
LANES = 128
PLANE_ROWS = B * B // LANES
HALF = LANES // B

VELOCITIES = (
    (0, 0, 0),
    (1, 0, 0),
    (-1, 0, 0),
    (0, 1, 0),
    (0, -1, 0),
    (0, 0, 1),
    (0, 0, -1),
    (1, 1, 0),
    (-1, -1, 0),
    (1, -1, 0),
    (-1, 1, 0),
    (1, 0, 1),
    (-1, 0, -1),
    (1, 0, -1),
    (-1, 0, 1),
    (0, 1, 1),
    (0, -1, -1),
    (0, 1, -1),
    (0, -1, 1),
)
OPPOSITE = (0, 2, 1, 4, 3, 6, 5, 8, 7, 10, 9, 12, 11, 14, 13, 16, 15, 18, 17)
Q = len(VELOCITIES)
UPWARD = tuple(p for p in range(Q) if VELOCITIES[p][0] == 1)
DOWNWARD = tuple(p for p in range(Q) if VELOCITIES[p][0] == -1)

VMEM_SPEC = pl.BlockSpec(memory_space=pltpu.VMEM)
SMEM_SPEC = pl.BlockSpec(memory_space=pltpu.SMEM)
PARAMS = pltpu.CompilerParams(vmem_limit_bytes=40 * 1024 * 1024)


def snake(place):
    pair = place // 2
    return 2 * pair + (place % 2 if pair % 2 == 0 else 1 - place % 2)


def owner_at(place, slab, owners):
    return snake(place if slab % 2 == 0 else owners - 1 - place)


def dynamic_owner(place, odd_slab, owners):
    return jnp.where(odd_slab == 1, snake(owners - 1 - place), snake(place))


def ring_pairs(owners, slabs, step):
    pairs = []
    for slab in range(slabs):
        for place in range(owners):
            target = slab * owners + place + step
            there, seat = (target // owners) % slabs, target % owners
            pairs.append(
                (
                    owner_at(place, slab, owners) * slabs + slab,
                    owner_at(seat, there, owners) * slabs + there,
                )
            )
    return pairs


def collide(f, fluid):
    def pair(p):
        return f[p] + f[p + 1], f[p] - f[p + 1]

    sx, dx = pair(1)
    sy, dy = pair(3)
    sz, dz = pair(5)
    sxy_a, dxy_a = pair(7)
    sxy_b, dxy_b = pair(9)
    sxz_a, dxz_a = pair(11)
    sxz_b, dxz_b = pair(13)
    syz_a, dyz_a = pair(15)
    syz_b, dyz_b = pair(17)
    axy, bxy = sxy_a + sxy_b, sxy_a - sxy_b
    axz, bxz = sxz_a + sxz_b, sxz_a - sxz_b
    ayz, byz = syz_a + syz_b, syz_a - syz_b
    rho = f[0] + sx + sy + sz + axy + axz + ayz
    ox = dxy_a + dxy_b + dxz_a + dxz_b
    oy = dxy_a - dxy_b + dyz_a + dyz_b
    oz = dxz_a - dxz_b + dyz_a - dyz_b
    jx, jy, jz = dx + ox, dy + oy, dz + oz
    jxx, jyy, jzz = jx * jx, jy * jy, jz * jz
    base = rho * (1.3 / 9.0)
    wide = 1.3 / 3.0
    thin = 1.3 / 6.0
    axy1 = base - 0.3 * axy + wide * (jxx + jyy) - thin * jzz
    axz1 = base - 0.3 * axz + wide * (jxx + jzz) - thin * jyy
    ayz1 = base - 0.3 * ayz + wide * (jyy + jzz) - thin * jxx
    bxy1 = 1.25 * (jx * jy) - 0.25 * bxy
    bxz1 = 1.25 * (jx * jz) - 0.25 * bxz
    byz1 = 1.25 * (jy * jz) - 0.25 * byz
    third = rho * (1.25 / 3.0)
    sx1 = third + 1.25 * jxx - 0.25 * (sx + axy + axz) - axy1 - axz1
    sy1 = third + 1.25 * jyy - 0.25 * (sy + axy + ayz) - axy1 - ayz1
    sz1 = third + 1.25 * jzz - 0.25 * (sz + axz + ayz) - axz1 - ayz1
    rest = rho - sx1 - sy1 - sz1 - axy1 - axz1 - ayz1

    def split(even, odd):
        return 0.5 * (even + odd), 0.5 * (even - odd)

    def diagonal(a1, b1, d_a, d_b, j_first, j_second):
        plus = 0.25 * (j_first + j_second) - 0.5 * d_a
        minus = 0.25 * (j_first - j_second) - 0.5 * d_b
        return split(0.5 * (a1 + b1), plus) + split(0.5 * (a1 - b1), minus)

    relaxed = (
        (rest,)
        + split(sx1, 0.5 * ox)
        + split(sy1, 0.5 * oy)
        + split(sz1, 0.5 * oz)
        + diagonal(axy1, bxy1, dxy_a, dxy_b, jx, jy)
        + diagonal(axz1, bxz1, dxz_a, dxz_b, jx, jz)
        + diagonal(ayz1, byz1, dyz_a, dyz_b, jy, jz)
    )
    return [jnp.where(fluid, relaxed[p], f[OPPOSITE[p]]) for p in range(Q)]


def shift_y(value, step, lane):
    rows = value.shape[0]
    if step == 1:
        turned = pltpu.roll(value, B, 1)
        return jnp.where(lane < B, pltpu.roll(turned, 1, 0), turned)
    turned = pltpu.roll(value, LANES - B, 1)
    return jnp.where(lane >= LANES - B, pltpu.roll(turned, rows - 1, 0), turned)


def shift_z(value, other, step, lane):
    if step == 1:
        return jnp.where(
            lane % B == 0, pltpu.roll(other, LANES - (B - 1), 1), pltpu.roll(value, 1, 1)
        )
    return jnp.where(
        lane % B == B - 1, pltpu.roll(other, B - 1, 1), pltpu.roll(value, LANES - 1, 1)
    )


def collide_and_pass(take, fluid_at, planes, rows, post, body, high, low):
    for i in range(planes):
        for kz in range(NB):
            after = collide([take(p, i, kz) for p in range(Q)], fluid_at(i, kz))
            for p in range(Q):
                post[p, i, kz] = after[p]
    lane = lax.broadcasted_iota(jnp.int32, (rows, LANES), 1)
    for i in range(planes):
        for p in range(Q):
            cx, cy, cz = VELOCITIES[p]
            pair = [post[p, i, kz] for kz in range(NB)]
            if cy:
                pair = [shift_y(value, cy, lane) for value in pair]
            if cz:
                pair = [shift_z(pair[kz], pair[1 - kz], cz, lane) for kz in range(NB)]
            for kz in range(NB):
                if cx == 1 and i == planes - 1:
                    high[UPWARD.index(p), kz] = pair[kz]
                elif cx == -1 and i == 0:
                    low[DOWNWARD.index(p), kz] = pair[kz]
                else:
                    body[p, i + cx, kz] = pair[kz]


def taker(planes, body, from_below, from_above):
    def take(p, i, kz, rows=slice(None)):
        cx = VELOCITIES[p][0]
        if cx == 1 and i == 0:
            return from_below[UPWARD.index(p), kz, rows]
        if cx == -1 and i == planes - 1:
            return from_above[DOWNWARD.index(p), kz, rows]
        return body[p, i, kz, rows]

    return take


def build(mesh):
    owners, slabs = mesh.shape["gx"], mesh.shape["gy"]
    planes = B // owners
    count = planes * PLANE_ROWS
    rows = owners * PLANE_ROWS
    slot_rows_in = (Q + 1) * count
    head = NB * slot_rows_in
    rows_in = head + 8
    slot_rows_out = Q * count
    rows_out = NB * slot_rows_out
    blocks = NB * owners
    f32 = jnp.float32

    def pack_kernel(odd_ref, pops, mask, slots, swaps, out):
        odd = odd_ref[0]
        lane = lax.broadcasted_iota(jnp.int32, (8, LANES), 1)
        header = jnp.zeros((8, LANES), jnp.int32)
        for t in range(NB):
            header = jnp.where(lane == t, slots[0, t], header)
        for r in range(3):
            header = jnp.where(lane == NB + r, swaps[0, 0, r, 0], header)
        header = header.astype(f32)
        for place in range(owners):
            d = dynamic_owner(place, odd, owners)
            for t in range(NB):
                for c in range(count):
                    cells = pl.ds((place * count + c) * LANES, LANES)
                    for p0 in range(0, Q, 8):
                        n = min(8, Q - p0)
                        out[d, pl.ds(t * slot_rows_in + p0 * count + c, n, stride=count), :] = pops[
                            t, p0 : p0 + n, cells
                        ]
                    out[d, pl.ds(t * slot_rows_in + Q * count + c, 1), :] = mask[
                        t : t + 1, cells
                    ].astype(f32)
            out[d, pl.ds(head, 8), :] = header

    def first_kernel(got, body, fluid, high, low, final, lattice, post, table, inverse, sem):
        copies = [
            pltpu.make_async_copy(got.at[g, pl.ds(head, 1), :], table.at[pl.ds(g, 1), :], sem.at[g])
            for g in range(owners)
        ]
        for copy in copies:
            copy.start()
        for copy in copies:
            copy.wait()
        held = [
            [table[g, t].astype(jnp.int32) for t in range(NB)] for g in range(owners)
        ]
        first = [
            [table[g, NB + r].astype(jnp.int32) for r in range(3)] for g in range(owners)
        ]
        for g in range(owners):
            for t in range(NB):
                inverse[held[g][t]] = g * NB + t
        for g in range(owners):
            flip = first[g][2] + first[g ^ 4][2] + first[g ^ 4][1]
            flip = flip + first[g ^ 6][1] + first[g ^ 6][0] + first[g ^ 7][0]
            crossed = flip % 2 == 1
            one, two = held[g ^ 7]
            final[g * NB] = jnp.where(crossed, two, one)
            final[g * NB + 1] = jnp.where(crossed, one, two)
        for b in range(blocks):
            ky, kz = b // NB, b % NB
            q = inverse[b]
            g, t = q // NB, q % NB
            for v in range(slot_rows_in // 8):
                start = pl.multiple_of(t * slot_rows_in + 8 * v, 8)
                chunk = got[g, pl.ds(start, 8), :]
                for r in range(0, 8, PLANE_ROWS):
                    p, c = (8 * v + r) // count, (8 * v + r) % count
                    lattice[p, c // PLANE_ROWS, kz, pl.ds(ky * PLANE_ROWS, PLANE_ROWS), :] = chunk[
                        r : r + PLANE_ROWS
                    ]
        fluid[...] = lattice[Q]
        collide_and_pass(
            lambda p, i, kz: lattice[p, i, kz],
            lambda i, kz: lattice[Q, i, kz] > 0.5,
            planes,
            rows,
            post,
            body,
            high,
            low,
        )

    def second_kernel(body_in, fluid, from_below, from_above, body, high, low, post):
        collide_and_pass(
            taker(planes, body_in, from_below, from_above),
            lambda i, kz: fluid[i, kz] > 0.5,
            planes,
            rows,
            post,
            body,
            high,
            low,
        )

    def sort_kernel(final, body, from_below, from_above, out):
        take = taker(planes, body, from_below, from_above)
        for g in range(owners):
            for t in range(NB):
                b = final[g * NB + t]
                kz = b % NB
                place = pl.ds(pl.multiple_of((b // NB) * PLANE_ROWS, PLANE_ROWS), PLANE_ROWS)
                for p in range(Q):
                    for i in range(planes):
                        at = t * slot_rows_out + p * count + i * PLANE_ROWS
                        out[g, pl.ds(at, PLANE_ROWS), :] = take(p, i, kz, place)

    def unpack_kernel(odd_ref, got, out):
        odd = odd_ref[0]
        for place in range(owners):
            g = dynamic_owner(place, odd, owners)
            for t in range(NB):
                for c in range(count):
                    cells = pl.ds((place * count + c) * LANES, LANES)
                    for p0 in range(0, Q, 8):
                        n = min(8, Q - p0)
                        out[0, t, p0 : p0 + n, cells] = got[
                            g, pl.ds(t * slot_rows_out + p0 * count + c, n, stride=count), :
                        ]

    def shape(*dims, dtype=f32):
        return jax.ShapeDtypeStruct(dims, dtype)

    body_shape = shape(Q, planes, NB, rows, LANES)
    face_shape = shape(len(UPWARD), NB, rows, LANES)
    post_scratch = pltpu.VMEM((Q, planes, NB, rows, LANES), f32)
    up_pairs = ring_pairs(owners, slabs, 1)
    down_pairs = ring_pairs(owners, slabs, -1)

    def shards(populations, solid_mask, slot_blocks, swap_slots):
        odd = (lax.axis_index("gy") % 2).astype(jnp.int32).reshape(1)
        packed = pl.pallas_call(
            pack_kernel,
            out_shape=shape(owners, rows_in, LANES),
            in_specs=[SMEM_SPEC, VMEM_SPEC, VMEM_SPEC, SMEM_SPEC, SMEM_SPEC],
            out_specs=VMEM_SPEC,
            compiler_params=PARAMS,
            name="pack",
        )(odd, populations[0], solid_mask[0], slot_blocks, swap_slots)
        got = lax.all_to_all(packed, "gx", 0, 0, tiled=True)
        body, fluid, high, low, final = pl.pallas_call(
            first_kernel,
            out_shape=(
                body_shape,
                shape(planes, NB, rows, LANES),
                face_shape,
                face_shape,
                shape(blocks, dtype=jnp.int32),
            ),
            in_specs=[VMEM_SPEC],
            out_specs=(VMEM_SPEC, VMEM_SPEC, VMEM_SPEC, VMEM_SPEC, SMEM_SPEC),
            scratch_shapes=[
                pltpu.VMEM((Q + 1, planes, NB, rows, LANES), f32),
                post_scratch,
                pltpu.SMEM((owners, LANES), f32),
                pltpu.SMEM((blocks,), jnp.int32),
                pltpu.SemaphoreType.DMA((owners,)),
            ],
            compiler_params=PARAMS,
            name="first_step",
        )(got)
        from_below = lax.ppermute(high, ("gx", "gy"), up_pairs)
        from_above = lax.ppermute(low, ("gx", "gy"), down_pairs)
        body, high, low = pl.pallas_call(
            second_kernel,
            out_shape=(body_shape, face_shape, face_shape),
            in_specs=[VMEM_SPEC] * 4,
            out_specs=(VMEM_SPEC,) * 3,
            scratch_shapes=[post_scratch],
            compiler_params=PARAMS,
            name="second_step",
        )(body, fluid, from_below, from_above)
        from_below = lax.ppermute(high, ("gx", "gy"), up_pairs)
        from_above = lax.ppermute(low, ("gx", "gy"), down_pairs)
        sorted_pieces = pl.pallas_call(
            sort_kernel,
            out_shape=shape(owners, rows_out, LANES),
            in_specs=[SMEM_SPEC, VMEM_SPEC, VMEM_SPEC, VMEM_SPEC],
            out_specs=VMEM_SPEC,
            compiler_params=PARAMS,
            name="sort_blocks",
        )(final, body, from_below, from_above)
        home = lax.all_to_all(sorted_pieces, "gx", 0, 0, tiled=True)
        return pl.pallas_call(
            unpack_kernel,
            out_shape=shape(1, NB, Q, B * B * B),
            in_specs=[SMEM_SPEC, VMEM_SPEC],
            out_specs=VMEM_SPEC,
            compiler_params=PARAMS,
            name="unpack",
        )(odd, home)

    return shards


def solution(mesh):
    return jax.shard_map(
        build(mesh),
        mesh=mesh,
        in_specs=(
            P("gy", "gx", None, None),
            P("gy", "gx", None),
            P("gy", "gx"),
            P("gy", "gx", None, None),
        ),
        out_specs=P("gy", "gx", None, None),
        check_vma=False,
    )
```

```python
import jax
import jax.numpy as jnp
from jax import lax
from jax.experimental import pallas as pl
from jax.experimental.pallas import tpu as pltpu
from jax.sharding import PartitionSpec as P

B = 16
NB = 2
LANES = 128
PLANE_ROWS = B * B // LANES
PLANE = PLANE_ROWS * NB
WHOLE = B * PLANE

VELOCITIES = (
    (0, 0, 0),
    (1, 0, 0),
    (-1, 0, 0),
    (0, 1, 0),
    (0, -1, 0),
    (0, 0, 1),
    (0, 0, -1),
    (1, 1, 0),
    (-1, -1, 0),
    (1, -1, 0),
    (-1, 1, 0),
    (1, 0, 1),
    (-1, 0, -1),
    (1, 0, -1),
    (-1, 0, 1),
    (0, 1, 1),
    (0, -1, -1),
    (0, 1, -1),
    (0, -1, 1),
)
OPPOSITE = (0, 2, 1, 4, 3, 6, 5, 8, 7, 10, 9, 12, 11, 14, 13, 16, 15, 18, 17)
Q = len(VELOCITIES)
UPWARD = tuple(p for p in range(Q) if VELOCITIES[p][0] == 1)
DOWNWARD = tuple(p for p in range(Q) if VELOCITIES[p][0] == -1)

VMEM_SPEC = pl.BlockSpec(memory_space=pltpu.VMEM)
PARAMS = pltpu.CompilerParams(vmem_limit_bytes=40 * 1024 * 1024)


def dynamic_place(owner, odd_slab, owners):
    pair, core = owner // 2, owner % 2
    forward = 2 * pair + jnp.where(pair % 2 == 0, core, 1 - core)
    return jnp.where(odd_slab == 1, owners - 1 - forward, forward)


def collide(f, fluid):
    def pair(p):
        return f[p] + f[p + 1], f[p] - f[p + 1]

    sx, dx = pair(1)
    sy, dy = pair(3)
    sz, dz = pair(5)
    sxy_a, dxy_a = pair(7)
    sxy_b, dxy_b = pair(9)
    sxz_a, dxz_a = pair(11)
    sxz_b, dxz_b = pair(13)
    syz_a, dyz_a = pair(15)
    syz_b, dyz_b = pair(17)
    axy, bxy = sxy_a + sxy_b, sxy_a - sxy_b
    axz, bxz = sxz_a + sxz_b, sxz_a - sxz_b
    ayz, byz = syz_a + syz_b, syz_a - syz_b
    rho = f[0] + sx + sy + sz + axy + axz + ayz
    ox = dxy_a + dxy_b + dxz_a + dxz_b
    oy = dxy_a - dxy_b + dyz_a + dyz_b
    oz = dxz_a - dxz_b + dyz_a - dyz_b
    jx, jy, jz = dx + ox, dy + oy, dz + oz
    jxx, jyy, jzz = jx * jx, jy * jy, jz * jz
    base = rho * (1.3 / 9.0)
    wide = 1.3 / 3.0
    thin = 1.3 / 6.0
    axy1 = base - 0.3 * axy + wide * (jxx + jyy) - thin * jzz
    axz1 = base - 0.3 * axz + wide * (jxx + jzz) - thin * jyy
    ayz1 = base - 0.3 * ayz + wide * (jyy + jzz) - thin * jxx
    bxy1 = 1.25 * (jx * jy) - 0.25 * bxy
    bxz1 = 1.25 * (jx * jz) - 0.25 * bxz
    byz1 = 1.25 * (jy * jz) - 0.25 * byz
    third = rho * (1.25 / 3.0)
    sx1 = third + 1.25 * jxx - 0.25 * (sx + axy + axz) - axy1 - axz1
    sy1 = third + 1.25 * jyy - 0.25 * (sy + axy + ayz) - axy1 - ayz1
    sz1 = third + 1.25 * jzz - 0.25 * (sz + axz + ayz) - axz1 - ayz1
    rest = rho - sx1 - sy1 - sz1 - axy1 - axz1 - ayz1

    def split(even, odd):
        return 0.5 * (even + odd), 0.5 * (even - odd)

    def diagonal(a1, b1, d_a, d_b, j_first, j_second):
        plus = 0.25 * (j_first + j_second) - 0.5 * d_a
        minus = 0.25 * (j_first - j_second) - 0.5 * d_b
        return split(0.5 * (a1 + b1), plus) + split(0.5 * (a1 - b1), minus)

    relaxed = (
        (rest,)
        + split(sx1, 0.5 * ox)
        + split(sy1, 0.5 * oy)
        + split(sz1, 0.5 * oz)
        + diagonal(axy1, bxy1, dxy_a, dxy_b, jx, jy)
        + diagonal(axz1, bxz1, dxz_a, dxz_b, jx, jz)
        + diagonal(ayz1, byz1, dyz_a, dyz_b, jy, jz)
    )
    return [jnp.where(fluid, relaxed[p], f[OPPOSITE[p]]) for p in range(Q)]


def shift_y(value, step, lane):
    rows = value.shape[0]
    if step == 1:
        turned = pltpu.roll(value, B, 1)
        return jnp.where(lane < B, pltpu.roll(turned, 1, 0), turned)
    turned = pltpu.roll(value, LANES - B, 1)
    return jnp.where(lane >= LANES - B, pltpu.roll(turned, rows - 1, 0), turned)


def shift_z(value, other, step, lane):
    if step == 1:
        return jnp.where(
            lane % B == 0, pltpu.roll(other, LANES - (B - 1), 1), pltpu.roll(value, 1, 1)
        )
    return jnp.where(
        lane % B == B - 1, pltpu.roll(other, B - 1, 1), pltpu.roll(value, LANES - 1, 1)
    )


def build(mesh):
    owners, slabs = mesh.shape["gx"], mesh.shape["gy"]
    planes = B // owners
    share = planes * PLANE
    rows = owners * PLANE_ROWS
    head = (Q + 1) * share
    rows_in = head + 8
    rows_out = Q * share
    faces = len(UPWARD) * PLANE
    rows_hop = faces + 4
    f32 = jnp.float32

    def position():
        me = lax.axis_index("gx")
        return me, lax.axis_index("gy") % 2

    def edge_kernel(pops, mask, slots, swaps, up, down):
        for start, out, chosen, inside in (
            (WHOLE - 8, up, UPWARD, 8 - PLANE),
            (0, down, DOWNWARD, 0),
        ):
            f = [pops[pl.ds(p * WHOLE + start, 8), :] for p in range(Q)]
            after = collide(f, mask[pl.ds(start, 8), :] > 0)
            for n, p in enumerate(chosen):
                out[pl.ds(n * PLANE, PLANE), :] = after[p][inside : inside + PLANE]
            out[pl.ds(faces, 4), :] = jnp.zeros((4, LANES), f32)
            out[pl.ds(faces, 1), 0:NB] = slots[...].astype(f32)
            out[pl.ds(faces + 1, 1), 0:3] = swaps[0:1].astype(f32)

    def collide_kernel(pops, mask, post):
        for start in range(0, WHOLE, 8):
            f = [pops[pl.ds(p * WHOLE + start, 8), :] for p in range(Q)]
            after = collide(f, mask[pl.ds(start, 8), :] > 0)
            for p in range(Q):
                post[p, pl.ds(8 + start, 8), :] = after[p]

    def pack_kernel(post, mask, slots, swaps, below, above, *outs):
        me, odd = position()
        own = jnp.zeros((4, LANES), f32)
        for d in range(owners):
            out = outs[d]
            place = dynamic_place(me ^ d, odd, owners)
            here = pl.multiple_of(place * share, min(share, 8))
            for p in range(Q):
                cx = VELOCITIES[p][0]
                out[pl.ds(p * share, share), :] = post[p, pl.ds(8 + here - cx * PLANE, share), :]
            out[pl.ds(Q * share, share), :] = mask[pl.ds(here, share), :].astype(f32)
            out[pl.ds(head, 4), :] = own
            out[pl.ds(head, 1), 0:NB] = slots[...].astype(f32)
            out[pl.ds(head + 1, 1), 0:3] = swaps[0:1].astype(f32)
            out[pl.ds(head + 2, 2), :] = below[pl.ds(faces, 2), :]
            out[pl.ds(head + 4, 2), :] = above[pl.ds(faces, 2), :]
            out[pl.ds(head + 6, 2), :] = own[0:2]

            @pl.when(place == 0)
            def _():
                for n, p in enumerate(UPWARD):
                    out[pl.ds(p * share, PLANE), :] = below[pl.ds(n * PLANE, PLANE), :]

            @pl.when(place == owners - 1)
            def _():
                for n, p in enumerate(DOWNWARD):
                    out[pl.ds(p * share + share - PLANE, PLANE), :] = above[
                        pl.ds(n * PLANE, PLANE), :
                    ]

    def middle_kernel(*refs):
        got, outs = refs[:owners], refs[owners : 2 * owners]
        lattice, ready, table, sem = refs[2 * owners :]
        me, odd = position()
        place = dynamic_place(me, odd, owners)
        first, last = place == 0, place == owners - 1
        copies = [
            pltpu.make_async_copy(got[d].at[pl.ds(head, 8), :], table.at[d], sem.at[d])
            for d in range(owners)
        ]
        for copy in copies:
            copy.start()
        for copy in copies:
            copy.wait()

        def number(d, row, column):
            return table[d, row, column].astype(jnp.int32)

        def held(d, t, which):
            return number(d, 2 * which, t)

        def final(d, t, which):
            def lead(e, r):
                return number(d ^ e, 2 * which + 1, r)

            flip = lead(0, 2) + lead(4, 2) + lead(4, 1) + lead(6, 1) + lead(6, 0) + lead(7, 0)
            one, two = held(d ^ 7, t, which), held(d ^ 7, 1 - t, which)
            return jnp.where(flip % 2 == 1, two, one)

        def seat(b):
            return b % NB, pl.multiple_of((b // NB) * PLANE_ROWS, PLANE_ROWS)

        for d in range(owners):
            for t in range(NB):
                usual = held(d, t, 0)
                at_usual = seat(usual)
                at_below = seat(jnp.where(first, held(d, t, 1), usual))
                at_above = seat(jnp.where(last, held(d, t, 2), usual))
                for p in range(Q + 1):
                    cx = VELOCITIES[p][0] if p < Q else 0
                    for i in range(planes):
                        kz, y = at_usual
                        if cx == 1 and i == 0:
                            kz, y = at_below
                        if cx == -1 and i == planes - 1:
                            kz, y = at_above
                        lattice[p, i, kz, pl.ds(y, PLANE_ROWS), :] = got[d][
                            pl.ds(p * share + i * PLANE + t, PLANE_ROWS, stride=NB), :
                        ]
        lane = lax.broadcasted_iota(jnp.int32, (rows, LANES), 1)

        def passed(pair, p):
            cx, cy, cz = VELOCITIES[p]
            if cy:
                pair = [shift_y(value, cy, lane) for value in pair]
            if cz:
                pair = [shift_z(pair[kz], pair[1 - kz], cz, lane) for kz in range(NB)]
            return pair

        for i in range(planes):
            for p in range(Q):
                pair = passed([lattice[p, i, kz] for kz in range(NB)], p)
                for kz in range(NB):
                    ready[p, i, kz] = pair[kz]
            for kz in range(NB):
                after = collide([ready[p, i, kz] for p in range(Q)], lattice[Q, i, kz] > 0.5)
                for p in range(Q):
                    lattice[p, i, kz] = after[p]
            for p in range(Q):
                pair = passed([lattice[p, i, kz] for kz in range(NB)], p)
                for kz in range(NB):
                    ready[p, i, kz] = pair[kz]
        for d in range(owners):
            for t in range(NB):
                usual = final(d, t, 0)
                at_usual = seat(usual)
                at_below = seat(jnp.where(first, final(d, t, 1), usual))
                at_above = seat(jnp.where(last, final(d, t, 2), usual))
                for p in range(Q):
                    cx = VELOCITIES[p][0]
                    for i in range(planes):
                        kz, y = at_usual
                        if cx == 1 and i == planes - 1:
                            kz, y = at_above
                        if cx == -1 and i == 0:
                            kz, y = at_below
                        outs[d][pl.ds(p * share + i * PLANE + t, PLANE_ROWS, stride=NB), :] = ready[
                            p, i, kz, pl.ds(y, PLANE_ROWS), :
                        ]

    def crossing_kernel(*refs):
        got, up, down = refs[:owners], refs[owners], refs[owners + 1]
        me, odd = position()
        for d in range(owners):
            place = dynamic_place(me ^ d, odd, owners)

            @pl.when(place == owners - 1)
            def _():
                for n, p in enumerate(UPWARD):
                    up[pl.ds(n * PLANE, PLANE), :] = got[d][
                        pl.ds(p * share + share - PLANE, PLANE), :
                    ]

            @pl.when(place == 0)
            def _():
                for n, p in enumerate(DOWNWARD):
                    down[pl.ds(n * PLANE, PLANE), :] = got[d][pl.ds(p * share, PLANE), :]

        for out in (up, down):
            out[pl.ds(faces, 4), :] = jnp.zeros((4, LANES), f32)

    def unpack_kernel(*refs):
        got, main = refs[:owners], refs[owners]
        me, odd = position()
        for d in range(owners):
            place = dynamic_place(me ^ d, odd, owners)
            here = pl.multiple_of(place * share, min(share, 8))
            for p in range(Q):
                cx = VELOCITIES[p][0]
                main[p, pl.ds(8 + here + cx * PLANE, share), :] = got[d][
                    pl.ds(p * share, share), :
                ]

    def finish_kernel(main, below, above, out):
        for p in range(Q):
            out[pl.ds(p * WHOLE, WHOLE), :] = main[p, pl.ds(8, WHOLE), :]
        for n, p in enumerate(UPWARD):
            out[pl.ds(p * WHOLE, PLANE), :] = below[pl.ds(n * PLANE, PLANE), :]
        for n, p in enumerate(DOWNWARD):
            out[pl.ds(p * WHOLE + WHOLE - PLANE, PLANE), :] = above[pl.ds(n * PLANE, PLANE), :]

    def shape(*dims):
        return jax.ShapeDtypeStruct(dims, f32)

    def call(kernel, name, out_shape, inputs, cost, scratch=()):
        outs = jax.tree.map(lambda _: VMEM_SPEC, out_shape)
        return pl.pallas_call(
            kernel,
            out_shape=out_shape,
            in_specs=[VMEM_SPEC] * len(inputs),
            out_specs=outs,
            scratch_shapes=list(scratch),
            compiler_params=PARAMS,
            cost_estimate=pl.CostEstimate(flops=cost, bytes_accessed=cost, transcendentals=0),
            name=name,
        )(*inputs)

    def exchange(parts):
        here = [parts[0]]
        for d in range(1, owners):
            here.append(lax.ppermute(parts[d], "gx", [(g, g ^ d) for g in range(owners)]))
        return here

    def hop(up, down):
        return (
            lax.ppermute(up, "gy", [(s, (s + 1) % slabs) for s in range(slabs)]),
            lax.ppermute(down, "gy", [(s, (s - 1) % slabs) for s in range(slabs)]),
        )

    padded = shape(Q, 8 + WHOLE + 8, LANES)
    work = pltpu.VMEM((Q + 1, planes, NB, rows, LANES), f32)
    small, large = 100_000, 4_000_000

    def shards(populations, solid_mask, slot_blocks, swap_slots):
        tiles = B * B * B // LANES
        pops = populations[0].transpose(1, 0, 2).reshape(Q, NB, tiles, LANES)
        pops = pops.transpose(0, 2, 1, 3).reshape(Q * WHOLE, LANES)
        mask = solid_mask[0].reshape(NB, tiles, LANES).transpose(1, 0, 2).reshape(WHOLE, LANES)
        swaps = swap_slots[0, 0].T
        up, down = call(
            edge_kernel,
            "edge_planes",
            (shape(rows_hop, LANES),) * 2,
            (pops, mask, slot_blocks, swaps),
            small,
        )
        below, above = hop(up, down)
        post = call(collide_kernel, "first_collision", padded, (pops, mask), large)
        parts = call(
            pack_kernel,
            "pack_planes",
            (shape(rows_in, LANES),) * owners,
            (post, mask, slot_blocks, swaps, below, above),
            large,
        )
        got = exchange(parts)
        parts = call(
            middle_kernel,
            "second_step",
            (shape(rows_out, LANES),) * owners,
            got,
            large,
            (
                work,
                work,
                pltpu.SMEM((owners, 8, LANES), f32),
                pltpu.SemaphoreType.DMA((owners,)),
            ),
        )
        home = exchange(parts)
        up, down = call(crossing_kernel, "crossing_planes", (shape(rows_hop, LANES),) * 2, home, small)
        below, above = hop(up, down)
        main = call(unpack_kernel, "unpack_planes", padded, home, large)
        out = call(
            finish_kernel, "finish", shape(Q * WHOLE, LANES), (main, below, above), small
        )
        out = out.reshape(Q, tiles, NB, LANES).transpose(0, 2, 1, 3)
        return out.reshape(Q, NB, B * B * B).transpose(1, 0, 2)[None]

    return shards


def solution(mesh):
    return jax.shard_map(
        build(mesh),
        mesh=mesh,
        in_specs=(
            P("gy", "gx", None, None),
            P("gy", "gx", None),
            P("gy", "gx"),
            P("gy", "gx", None, None),
        ),
        out_specs=P("gy", "gx", None, None),
        check_vma=False,
    )
```

```python
import jax
import jax.numpy as jnp
from jax import lax
from jax.experimental import pallas as pl
from jax.experimental.pallas import tpu as pltpu
from jax.sharding import PartitionSpec as P

B = 16
NB = 2
LANES = 128
PLANE_ROWS = B * B // LANES
PLANE = PLANE_ROWS * NB
WHOLE = B * PLANE

VELOCITIES = (
    (0, 0, 0),
    (1, 0, 0),
    (-1, 0, 0),
    (0, 1, 0),
    (0, -1, 0),
    (0, 0, 1),
    (0, 0, -1),
    (1, 1, 0),
    (-1, -1, 0),
    (1, -1, 0),
    (-1, 1, 0),
    (1, 0, 1),
    (-1, 0, -1),
    (1, 0, -1),
    (-1, 0, 1),
    (0, 1, 1),
    (0, -1, -1),
    (0, 1, -1),
    (0, -1, 1),
)
OPPOSITE = (0, 2, 1, 4, 3, 6, 5, 8, 7, 10, 9, 12, 11, 14, 13, 16, 15, 18, 17)
Q = len(VELOCITIES)
UPWARD = tuple(p for p in range(Q) if VELOCITIES[p][0] == 1)
DOWNWARD = tuple(p for p in range(Q) if VELOCITIES[p][0] == -1)

VMEM_SPEC = pl.BlockSpec(memory_space=pltpu.VMEM)
PARAMS = pltpu.CompilerParams(vmem_limit_bytes=40 * 1024 * 1024)


def dynamic_place(owner, odd_slab, owners):
    pair, core = owner // 2, owner % 2
    forward = 2 * pair + jnp.where(pair % 2 == 0, core, 1 - core)
    return jnp.where(odd_slab == 1, owners - 1 - forward, forward)


def collide(f, fluid):
    def pair(p):
        return f[p] + f[p + 1], f[p] - f[p + 1]

    sx, dx = pair(1)
    sy, dy = pair(3)
    sz, dz = pair(5)
    sxy_a, dxy_a = pair(7)
    sxy_b, dxy_b = pair(9)
    sxz_a, dxz_a = pair(11)
    sxz_b, dxz_b = pair(13)
    syz_a, dyz_a = pair(15)
    syz_b, dyz_b = pair(17)
    axy, bxy = sxy_a + sxy_b, sxy_a - sxy_b
    axz, bxz = sxz_a + sxz_b, sxz_a - sxz_b
    ayz, byz = syz_a + syz_b, syz_a - syz_b
    rho = f[0] + sx + sy + sz + axy + axz + ayz
    ox = dxy_a + dxy_b + dxz_a + dxz_b
    oy = dxy_a - dxy_b + dyz_a + dyz_b
    oz = dxz_a - dxz_b + dyz_a - dyz_b
    jx, jy, jz = dx + ox, dy + oy, dz + oz
    jxx, jyy, jzz = jx * jx, jy * jy, jz * jz
    base = rho * (1.3 / 9.0)
    wide = 1.3 / 3.0
    thin = 1.3 / 6.0
    axy1 = base - 0.3 * axy + wide * (jxx + jyy) - thin * jzz
    axz1 = base - 0.3 * axz + wide * (jxx + jzz) - thin * jyy
    ayz1 = base - 0.3 * ayz + wide * (jyy + jzz) - thin * jxx
    bxy1 = 1.25 * (jx * jy) - 0.25 * bxy
    bxz1 = 1.25 * (jx * jz) - 0.25 * bxz
    byz1 = 1.25 * (jy * jz) - 0.25 * byz
    third = rho * (1.25 / 3.0)
    sx1 = third + 1.25 * jxx - 0.25 * (sx + axy + axz) - axy1 - axz1
    sy1 = third + 1.25 * jyy - 0.25 * (sy + axy + ayz) - axy1 - ayz1
    sz1 = third + 1.25 * jzz - 0.25 * (sz + axz + ayz) - axz1 - ayz1
    rest = rho - sx1 - sy1 - sz1 - axy1 - axz1 - ayz1

    def split(even, odd):
        return 0.5 * (even + odd), 0.5 * (even - odd)

    def diagonal(a1, b1, d_a, d_b, j_first, j_second):
        plus = 0.25 * (j_first + j_second) - 0.5 * d_a
        minus = 0.25 * (j_first - j_second) - 0.5 * d_b
        return split(0.5 * (a1 + b1), plus) + split(0.5 * (a1 - b1), minus)

    relaxed = (
        (rest,)
        + split(sx1, 0.5 * ox)
        + split(sy1, 0.5 * oy)
        + split(sz1, 0.5 * oz)
        + diagonal(axy1, bxy1, dxy_a, dxy_b, jx, jy)
        + diagonal(axz1, bxz1, dxz_a, dxz_b, jx, jz)
        + diagonal(ayz1, byz1, dyz_a, dyz_b, jy, jz)
    )
    return [jnp.where(fluid, relaxed[p], f[OPPOSITE[p]]) for p in range(Q)]


def shift_y(value, step, lane):
    rows = value.shape[0]
    if step == 1:
        turned = pltpu.roll(value, B, 1)
        return jnp.where(lane < B, pltpu.roll(turned, 1, 0), turned)
    turned = pltpu.roll(value, LANES - B, 1)
    return jnp.where(lane >= LANES - B, pltpu.roll(turned, rows - 1, 0), turned)


def shift_z(value, other, step, lane):
    if step == 1:
        return jnp.where(
            lane % B == 0, pltpu.roll(other, LANES - (B - 1), 1), pltpu.roll(value, 1, 1)
        )
    return jnp.where(
        lane % B == B - 1, pltpu.roll(other, B - 1, 1), pltpu.roll(value, LANES - 1, 1)
    )


def build(mesh):
    owners, slabs = mesh.shape["gx"], mesh.shape["gy"]
    planes = B // owners
    share = planes * PLANE
    rows = owners * PLANE_ROWS
    head = (Q + 1) * share
    rows_in = head + 8
    rows_out = Q * share
    faces = len(UPWARD) * PLANE
    rows_hop = faces + 4
    f32 = jnp.float32

    def position():
        me = lax.axis_index("gx")
        return me, lax.axis_index("gy") % 2

    def edge_kernel(pops, mask, slots, swaps, up, down, own, cells, solid, held, given, sem):
        ends = (WHOLE - 8, 0)
        copies = []
        for n, start in enumerate(ends):
            copies.append((pops.at[:, pl.ds(start, 8), :], cells.at[n]))
            copies.append((mask.at[pl.ds(start, 8), :], solid.at[n]))
        copies += [(slots, held), (swaps, given)]
        copies = [
            pltpu.make_async_copy(source, target, sem.at[n])
            for n, (source, target) in enumerate(copies)
        ]
        for copy in copies:
            copy.start()
        for copy in copies:
            copy.wait()
        own[...] = jnp.zeros((8, LANES), f32)
        own[0:1, 0:NB] = held[...].astype(f32)
        own[1:2, 0:3] = given[0:1].astype(f32)
        for n, (out, chosen, inside) in enumerate(((up, UPWARD, 8 - PLANE), (down, DOWNWARD, 0))):
            after = collide([cells[n, p] for p in range(Q)], solid[n] > 0)
            for m, p in enumerate(chosen):
                out[pl.ds(m * PLANE, PLANE), :] = after[p][inside : inside + PLANE]
            out[pl.ds(faces, 4), :] = own[0:4]

    def collide_kernel(pops, mask, post, cells, solid, sem):
        copies = (
            pltpu.make_async_copy(pops, cells, sem.at[0]),
            pltpu.make_async_copy(mask, solid, sem.at[1]),
        )
        for copy in copies:
            copy.start()
        for copy in copies:
            copy.wait()
        for start in range(0, WHOLE, 8):
            here = pl.ds(start, 8)
            after = collide([cells[p, here, :] for p in range(Q)], solid[here, :] > 0)
            for p in range(Q):
                post[p, pl.ds(8 + start, 8), :] = after[p]
            post[Q, pl.ds(8 + start, 8), :] = solid[here, :].astype(f32)

    def pack_kernel(post, own, below, above, *outs):
        me, odd = position()
        for d in range(owners):
            out = outs[d]
            place = dynamic_place(me ^ d, odd, owners)
            here = pl.multiple_of(place * share, min(share, 8))
            for p in range(Q + 1):
                cx = VELOCITIES[p][0] if p < Q else 0
                out[pl.ds(p * share, share), :] = post[p, pl.ds(8 + here - cx * PLANE, share), :]
            out[pl.ds(head, 2), :] = own[0:2]
            out[pl.ds(head + 2, 2), :] = below[pl.ds(faces, 2), :]
            out[pl.ds(head + 4, 2), :] = above[pl.ds(faces, 2), :]
            out[pl.ds(head + 6, 2), :] = own[2:4]

            @pl.when(place == 0)
            def _():
                for n, p in enumerate(UPWARD):
                    out[pl.ds(p * share, PLANE), :] = below[pl.ds(n * PLANE, PLANE), :]

            @pl.when(place == owners - 1)
            def _():
                for n, p in enumerate(DOWNWARD):
                    out[pl.ds(p * share + share - PLANE, PLANE), :] = above[
                        pl.ds(n * PLANE, PLANE), :
                    ]

    def middle_kernel(*refs):
        got, outs = refs[:owners], refs[owners : 2 * owners]
        lattice, ready, table, sem = refs[2 * owners :]
        me, odd = position()
        place = dynamic_place(me, odd, owners)
        first, last = place == 0, place == owners - 1
        copies = [
            pltpu.make_async_copy(got[d].at[pl.ds(head, 8), :], table.at[d], sem.at[d])
            for d in range(owners)
        ]
        for copy in copies:
            copy.start()
        for copy in copies:
            copy.wait()

        def number(d, row, column):
            return table[d, row, column].astype(jnp.int32)

        def held(d, t, which):
            return number(d, 2 * which, t)

        def final(d, t, which):
            def lead(e, r):
                return number(d ^ e, 2 * which + 1, r)

            flip = lead(0, 2) + lead(4, 2) + lead(4, 1) + lead(6, 1) + lead(6, 0) + lead(7, 0)
            one, two = held(d ^ 7, t, which), held(d ^ 7, 1 - t, which)
            return jnp.where(flip % 2 == 1, two, one)

        def seat(b):
            return b % NB, pl.multiple_of((b // NB) * PLANE_ROWS, PLANE_ROWS)

        for d in range(owners):
            for t in range(NB):
                usual = held(d, t, 0)
                at_usual = seat(usual)
                at_below = seat(jnp.where(first, held(d, t, 1), usual))
                at_above = seat(jnp.where(last, held(d, t, 2), usual))
                for p in range(Q + 1):
                    cx = VELOCITIES[p][0] if p < Q else 0
                    for i in range(planes):
                        kz, y = at_usual
                        if cx == 1 and i == 0:
                            kz, y = at_below
                        if cx == -1 and i == planes - 1:
                            kz, y = at_above
                        lattice[p, i, kz, pl.ds(y, PLANE_ROWS), :] = got[d][
                            pl.ds(p * share + i * PLANE + t, PLANE_ROWS, stride=NB), :
                        ]
        lane = lax.broadcasted_iota(jnp.int32, (rows, LANES), 1)

        def passed(pair, p):
            cx, cy, cz = VELOCITIES[p]
            if cy:
                pair = [shift_y(value, cy, lane) for value in pair]
            if cz:
                pair = [shift_z(pair[kz], pair[1 - kz], cz, lane) for kz in range(NB)]
            return pair

        for i in range(planes):
            for p in range(Q):
                pair = passed([lattice[p, i, kz] for kz in range(NB)], p)
                for kz in range(NB):
                    ready[p, i, kz] = pair[kz]
            for kz in range(NB):
                after = collide([ready[p, i, kz] for p in range(Q)], lattice[Q, i, kz] > 0.5)
                for p in range(Q):
                    lattice[p, i, kz] = after[p]
            for p in range(Q):
                pair = passed([lattice[p, i, kz] for kz in range(NB)], p)
                for kz in range(NB):
                    ready[p, i, kz] = pair[kz]
        for d in range(owners):
            for t in range(NB):
                usual = final(d, t, 0)
                at_usual = seat(usual)
                at_below = seat(jnp.where(first, final(d, t, 1), usual))
                at_above = seat(jnp.where(last, final(d, t, 2), usual))
                for p in range(Q):
                    cx = VELOCITIES[p][0]
                    for i in range(planes):
                        kz, y = at_usual
                        if cx == 1 and i == planes - 1:
                            kz, y = at_above
                        if cx == -1 and i == 0:
                            kz, y = at_below
                        outs[d][pl.ds(p * share + i * PLANE + t, PLANE_ROWS, stride=NB), :] = ready[
                            p, i, kz, pl.ds(y, PLANE_ROWS), :
                        ]

    def crossing_kernel(*refs):
        got, up, down = refs[:owners], refs[owners], refs[owners + 1]
        me, odd = position()
        for d in range(owners):
            place = dynamic_place(me ^ d, odd, owners)

            @pl.when(place == owners - 1)
            def _():
                for n, p in enumerate(UPWARD):
                    up[pl.ds(n * PLANE, PLANE), :] = got[d][
                        pl.ds(p * share + share - PLANE, PLANE), :
                    ]

            @pl.when(place == 0)
            def _():
                for n, p in enumerate(DOWNWARD):
                    down[pl.ds(n * PLANE, PLANE), :] = got[d][pl.ds(p * share, PLANE), :]

        for out in (up, down):
            out[pl.ds(faces, 4), :] = jnp.zeros((4, LANES), f32)

    def unpack_kernel(*refs):
        got, main = refs[:owners], refs[owners]
        me, odd = position()
        for d in range(owners):
            place = dynamic_place(me ^ d, odd, owners)
            here = pl.multiple_of(place * share, min(share, 8))
            for p in range(Q):
                cx = VELOCITIES[p][0]
                main[p, pl.ds(8 + here + cx * PLANE, share), :] = got[d][
                    pl.ds(p * share, share), :
                ]

    def finish_kernel(main, below, above, out):
        for p in range(Q):
            out[pl.ds(p * WHOLE, WHOLE), :] = main[p, pl.ds(8, WHOLE), :]
        for n, p in enumerate(UPWARD):
            out[pl.ds(p * WHOLE, PLANE), :] = below[pl.ds(n * PLANE, PLANE), :]
        for n, p in enumerate(DOWNWARD):
            out[pl.ds(p * WHOLE + WHOLE - PLANE, PLANE), :] = above[pl.ds(n * PLANE, PLANE), :]

    def shape(*dims):
        return jax.ShapeDtypeStruct(dims, f32)

    def call(kernel, name, out_shape, inputs, cost, scratch=(), spec=VMEM_SPEC):
        outs = jax.tree.map(lambda _: VMEM_SPEC, out_shape)
        return pl.pallas_call(
            kernel,
            out_shape=out_shape,
            in_specs=[spec] * len(inputs),
            out_specs=outs,
            scratch_shapes=list(scratch),
            compiler_params=PARAMS,
            cost_estimate=pl.CostEstimate(flops=cost, bytes_accessed=cost, transcendentals=0),
            name=name,
        )(*inputs)

    def exchange(parts):
        here = list(parts)
        for d in reversed(range(1, owners)):
            here[d] = lax.ppermute(parts[d], "gx", [(g, g ^ d) for g in range(owners)])
        return here

    def hop(up, down):
        return (
            lax.ppermute(up, "gy", [(s, (s + 1) % slabs) for s in range(slabs)]),
            lax.ppermute(down, "gy", [(s, (s - 1) % slabs) for s in range(slabs)]),
        )

    def padded(count):
        return shape(count, 8 + WHOLE + 8, LANES)

    work = pltpu.VMEM((Q + 1, planes, NB, rows, LANES), f32)
    small, large = 100_000, 4_000_000

    def shards(populations, solid_mask, slot_blocks, swap_slots):
        tiles = B * B * B // LANES
        pops = populations[0].transpose(1, 0, 2).reshape(Q, NB, tiles, LANES)
        pops = pops.transpose(0, 2, 1, 3).reshape(Q, WHOLE, LANES)
        mask = solid_mask[0].reshape(NB, tiles, LANES).transpose(1, 0, 2).reshape(WHOLE, LANES)
        swaps = swap_slots[0, 0].T
        in_place = pl.BlockSpec(memory_space=pl.ANY)
        up, down, own = call(
            edge_kernel,
            "edge_planes",
            (shape(rows_hop, LANES), shape(rows_hop, LANES), shape(8, LANES)),
            (pops, mask, slot_blocks, swaps),
            small,
            (
                pltpu.VMEM((2, Q, 8, LANES), f32),
                pltpu.VMEM((2, 8, LANES), jnp.int32),
                pltpu.VMEM(slot_blocks.shape, jnp.int32),
                pltpu.VMEM(swaps.shape, jnp.int32),
                pltpu.SemaphoreType.DMA((6,)),
            ),
            in_place,
        )
        below, above = hop(up, down)
        post = call(
            collide_kernel,
            "first_collision",
            padded(Q + 1),
            (pops, mask),
            large,
            (
                pltpu.VMEM(pops.shape, f32),
                pltpu.VMEM(mask.shape, jnp.int32),
                pltpu.SemaphoreType.DMA((2,)),
            ),
            in_place,
        )
        parts = call(
            pack_kernel,
            "pack_planes",
            (shape(rows_in, LANES),) * owners,
            (post, own, below, above),
            large,
        )
        got = exchange(parts)
        parts = call(
            middle_kernel,
            "second_step",
            (shape(rows_out, LANES),) * owners,
            got,
            large,
            (
                work,
                work,
                pltpu.SMEM((owners, 8, LANES), f32),
                pltpu.SemaphoreType.DMA((owners,)),
            ),
        )
        home = exchange(parts)
        up, down = call(crossing_kernel, "crossing_planes", (shape(rows_hop, LANES),) * 2, home, small)
        below, above = hop(up, down)
        main = call(unpack_kernel, "unpack_planes", padded(Q), home, large)
        out = call(
            finish_kernel, "finish", shape(Q * WHOLE, LANES), (main, below, above), small
        )
        out = out.reshape(Q, tiles, NB, LANES).transpose(0, 2, 1, 3)
        return out.reshape(Q, NB, B * B * B).transpose(1, 0, 2)[None]

    return shards


def solution(mesh):
    return jax.shard_map(
        build(mesh),
        mesh=mesh,
        in_specs=(
            P("gy", "gx", None, None),
            P("gy", "gx", None),
            P("gy", "gx"),
            P("gy", "gx", None, None),
        ),
        out_specs=P("gy", "gx", None, None),
        check_vma=False,
    )
```

```python
import jax
import jax.numpy as jnp
from jax import lax
from jax.experimental import pallas as pl
from jax.experimental.pallas import tpu as pltpu
from jax.sharding import PartitionSpec as P

B = 16
NB = 2
LANES = 128
PLANE_ROWS = B * B // LANES
PLANE = PLANE_ROWS * NB
WHOLE = B * PLANE

VELOCITIES = (
    (0, 0, 0),
    (1, 0, 0),
    (-1, 0, 0),
    (0, 1, 0),
    (0, -1, 0),
    (0, 0, 1),
    (0, 0, -1),
    (1, 1, 0),
    (-1, -1, 0),
    (1, -1, 0),
    (-1, 1, 0),
    (1, 0, 1),
    (-1, 0, -1),
    (1, 0, -1),
    (-1, 0, 1),
    (0, 1, 1),
    (0, -1, -1),
    (0, 1, -1),
    (0, -1, 1),
)
OPPOSITE = (0, 2, 1, 4, 3, 6, 5, 8, 7, 10, 9, 12, 11, 14, 13, 16, 15, 18, 17)
Q = len(VELOCITIES)
UPWARD = tuple(p for p in range(Q) if VELOCITIES[p][0] == 1)
DOWNWARD = tuple(p for p in range(Q) if VELOCITIES[p][0] == -1)

VMEM_SPEC = pl.BlockSpec(memory_space=pltpu.VMEM)


def dynamic_place(owner, odd_slab, owners):
    pair, core = owner // 2, owner % 2
    forward = 2 * pair + jnp.where(pair % 2 == 0, core, 1 - core)
    return jnp.where(odd_slab == 1, owners - 1 - forward, forward)


def collide(f, fluid):
    def pair(p):
        return f[p] + f[p + 1], f[p] - f[p + 1]

    sx, dx = pair(1)
    sy, dy = pair(3)
    sz, dz = pair(5)
    sxy_a, dxy_a = pair(7)
    sxy_b, dxy_b = pair(9)
    sxz_a, dxz_a = pair(11)
    sxz_b, dxz_b = pair(13)
    syz_a, dyz_a = pair(15)
    syz_b, dyz_b = pair(17)
    axy, bxy = sxy_a + sxy_b, sxy_a - sxy_b
    axz, bxz = sxz_a + sxz_b, sxz_a - sxz_b
    ayz, byz = syz_a + syz_b, syz_a - syz_b
    rho = f[0] + sx + sy + sz + axy + axz + ayz
    ox = dxy_a + dxy_b + dxz_a + dxz_b
    oy = dxy_a - dxy_b + dyz_a + dyz_b
    oz = dxz_a - dxz_b + dyz_a - dyz_b
    jx, jy, jz = dx + ox, dy + oy, dz + oz
    jxx, jyy, jzz = jx * jx, jy * jy, jz * jz
    base = rho * (1.3 / 9.0)
    wide = 1.3 / 3.0
    thin = 1.3 / 6.0
    axy1 = base - 0.3 * axy + wide * (jxx + jyy) - thin * jzz
    axz1 = base - 0.3 * axz + wide * (jxx + jzz) - thin * jyy
    ayz1 = base - 0.3 * ayz + wide * (jyy + jzz) - thin * jxx
    bxy1 = 1.25 * (jx * jy) - 0.25 * bxy
    bxz1 = 1.25 * (jx * jz) - 0.25 * bxz
    byz1 = 1.25 * (jy * jz) - 0.25 * byz
    third = rho * (1.25 / 3.0)
    sx1 = third + 1.25 * jxx - 0.25 * (sx + axy + axz) - axy1 - axz1
    sy1 = third + 1.25 * jyy - 0.25 * (sy + axy + ayz) - axy1 - ayz1
    sz1 = third + 1.25 * jzz - 0.25 * (sz + axz + ayz) - axz1 - ayz1
    rest = rho - sx1 - sy1 - sz1 - axy1 - axz1 - ayz1

    def split(even, odd):
        return 0.5 * (even + odd), 0.5 * (even - odd)

    def diagonal(a1, b1, d_a, d_b, j_first, j_second):
        plus = 0.25 * (j_first + j_second) - 0.5 * d_a
        minus = 0.25 * (j_first - j_second) - 0.5 * d_b
        return split(0.5 * (a1 + b1), plus) + split(0.5 * (a1 - b1), minus)

    relaxed = (
        (rest,)
        + split(sx1, 0.5 * ox)
        + split(sy1, 0.5 * oy)
        + split(sz1, 0.5 * oz)
        + diagonal(axy1, bxy1, dxy_a, dxy_b, jx, jy)
        + diagonal(axz1, bxz1, dxz_a, dxz_b, jx, jz)
        + diagonal(ayz1, byz1, dyz_a, dyz_b, jy, jz)
    )
    return [jnp.where(fluid, relaxed[p], f[OPPOSITE[p]]) for p in range(Q)]


def shift_y(value, step, lane):
    rows = value.shape[0]
    if step == 1:
        turned = pltpu.roll(value, B, 1)
        return jnp.where(lane < B, pltpu.roll(turned, 1, 0), turned)
    turned = pltpu.roll(value, LANES - B, 1)
    return jnp.where(lane >= LANES - B, pltpu.roll(turned, rows - 1, 0), turned)


def shift_z(value, other, step, lane):
    if step == 1:
        return jnp.where(
            lane % B == 0, pltpu.roll(other, LANES - (B - 1), 1), pltpu.roll(value, 1, 1)
        )
    return jnp.where(
        lane % B == B - 1, pltpu.roll(other, B - 1, 1), pltpu.roll(value, LANES - 1, 1)
    )


def build(mesh):
    owners, slabs = mesh.shape["gx"], mesh.shape["gy"]
    planes = B // owners
    share = planes * PLANE
    rows = owners * PLANE_ROWS
    head = (Q + 1) * share
    rows_in = head + 8
    rows_out = Q * share
    faces = len(UPWARD) * PLANE
    rows_hop = faces + 4
    f32 = jnp.float32

    order = [0]
    for bit in reversed(range(owners.bit_length() - 1)):
        order += range(1 << bit, 2 << bit)
    slot_of = [order.index(d) for d in range(owners)]

    def position():
        me = lax.axis_index("gx")
        return me, lax.axis_index("gy") % 2

    def sides(odd, near, far):
        return (
            jnp.where(odd == 1, near[...], far[...]),
            jnp.where(odd == 1, far[...], near[...]),
        )

    def send_sides(odd, up, down, near, far):
        near[...] = jnp.where(odd == 1, down[...], up[...])
        far[...] = jnp.where(odd == 1, up[...], down[...])

    def edge_kernel(pops, mask, slots, swaps, near, far, own, up, down, cells, solid, held, given, sem):
        ends = (WHOLE - 8, 0)
        copies = []
        for n, start in enumerate(ends):
            copies.append((pops.at[:, pl.ds(start, 8), :], cells.at[n]))
            copies.append((mask.at[pl.ds(start, 8), :], solid.at[n]))
        copies += [(slots, held), (swaps, given)]
        copies = [
            pltpu.make_async_copy(source, target, sem.at[n])
            for n, (source, target) in enumerate(copies)
        ]
        for copy in copies:
            copy.start()
        for copy in copies:
            copy.wait()
        own[...] = jnp.zeros((8, LANES), f32)
        own[0:1, 0:NB] = held[...].astype(f32)
        own[1:2, 0:3] = given[0:1].astype(f32)
        for n, (out, chosen, inside) in enumerate(((up, UPWARD, 8 - PLANE), (down, DOWNWARD, 0))):
            after = collide([cells[n, p] for p in range(Q)], solid[n] > 0)
            for m, p in enumerate(chosen):
                out[pl.ds(m * PLANE, PLANE), :] = after[p][inside : inside + PLANE]
            out[pl.ds(faces, 4), :] = own[0:4]
        send_sides(position()[1], up, down, near, far)

    def collide_kernel(cells, solid, post):
        for start in range(0, WHOLE, 8):
            here = pl.ds(start, 8)
            after = collide([cells[p, here, :] for p in range(Q)], solid[here, :] > 0)
            for p in range(Q):
                post[p, pl.ds(8 + start, 8), :] = after[p]
            post[Q, pl.ds(8 + start, 8), :] = solid[here, :].astype(f32)

    def pack_kernel(post, own, near, far, *outs):
        me, odd = position()
        below, above = sides(odd, near, far)
        for d in range(owners):
            out = outs[slot_of[d]]
            place = dynamic_place(me ^ d, odd, owners)
            here = pl.multiple_of(place * share, min(share, 8))
            for p in range(Q + 1):
                cx = VELOCITIES[p][0] if p < Q else 0
                out[pl.ds(p * share, share), :] = post[p, pl.ds(8 + here - cx * PLANE, share), :]
            out[pl.ds(head, 2), :] = own[0:2]
            out[pl.ds(head + 2, 2), :] = below[faces : faces + 2]
            out[pl.ds(head + 4, 2), :] = above[faces : faces + 2]
            out[pl.ds(head + 6, 2), :] = own[2:4]

            @pl.when(place == 0)
            def _():
                for n, p in enumerate(UPWARD):
                    out[pl.ds(p * share, PLANE), :] = below[n * PLANE : (n + 1) * PLANE]

            @pl.when(place == owners - 1)
            def _():
                for n, p in enumerate(DOWNWARD):
                    out[pl.ds(p * share + share - PLANE, PLANE), :] = above[
                        n * PLANE : (n + 1) * PLANE
                    ]

    def middle_kernel(*refs):
        got = [refs[slot_of[d]] for d in range(owners)]
        outs = [refs[owners + slot_of[d]] for d in range(owners)]
        lattice, ready, table, sem = refs[2 * owners :]
        me, odd = position()
        place = dynamic_place(me, odd, owners)
        first, last = place == 0, place == owners - 1
        copies = [
            pltpu.make_async_copy(got[d].at[pl.ds(head, 8), :], table.at[d], sem.at[d])
            for d in range(owners)
        ]
        for copy in copies:
            copy.start()
        for copy in copies:
            copy.wait()

        def number(d, row, column):
            return table[d, row, column].astype(jnp.int32)

        def held(d, t, which):
            return number(d, 2 * which, t)

        def final(d, t, which):
            def lead(e, r):
                return number(d ^ e, 2 * which + 1, r)

            flip = lead(0, 2) + lead(4, 2) + lead(4, 1) + lead(6, 1) + lead(6, 0) + lead(7, 0)
            one, two = held(d ^ 7, t, which), held(d ^ 7, 1 - t, which)
            return jnp.where(flip % 2 == 1, two, one)

        def seat(b):
            return b % NB, pl.multiple_of((b // NB) * PLANE_ROWS, PLANE_ROWS)

        for d in range(owners):
            for t in range(NB):
                usual = held(d, t, 0)
                at_usual = seat(usual)
                at_below = seat(jnp.where(first, held(d, t, 1), usual))
                at_above = seat(jnp.where(last, held(d, t, 2), usual))
                for p in range(Q + 1):
                    cx = VELOCITIES[p][0] if p < Q else 0
                    for i in range(planes):
                        kz, y = at_usual
                        if cx == 1 and i == 0:
                            kz, y = at_below
                        if cx == -1 and i == planes - 1:
                            kz, y = at_above
                        lattice[p, i, kz, pl.ds(y, PLANE_ROWS), :] = got[d][
                            pl.ds(p * share + i * PLANE + t, PLANE_ROWS, stride=NB), :
                        ]
        lane = lax.broadcasted_iota(jnp.int32, (rows, LANES), 1)

        def passed(pair, p):
            cx, cy, cz = VELOCITIES[p]
            if cy:
                pair = [shift_y(value, cy, lane) for value in pair]
            if cz:
                pair = [shift_z(pair[kz], pair[1 - kz], cz, lane) for kz in range(NB)]
            return pair

        for i in range(planes):
            for p in range(Q):
                pair = passed([lattice[p, i, kz] for kz in range(NB)], p)
                for kz in range(NB):
                    ready[p, i, kz] = pair[kz]
            for kz in range(NB):
                after = collide([ready[p, i, kz] for p in range(Q)], lattice[Q, i, kz] > 0.5)
                for p in range(Q):
                    lattice[p, i, kz] = after[p]
            for p in range(Q):
                pair = passed([lattice[p, i, kz] for kz in range(NB)], p)
                for kz in range(NB):
                    ready[p, i, kz] = pair[kz]
        for d in range(owners):
            for t in range(NB):
                usual = final(d, t, 0)
                at_usual = seat(usual)
                at_below = seat(jnp.where(first, final(d, t, 1), usual))
                at_above = seat(jnp.where(last, final(d, t, 2), usual))
                for p in range(Q):
                    cx = VELOCITIES[p][0]
                    for i in range(planes):
                        kz, y = at_usual
                        if cx == 1 and i == planes - 1:
                            kz, y = at_above
                        if cx == -1 and i == 0:
                            kz, y = at_below
                        outs[d][pl.ds(p * share + i * PLANE + t, PLANE_ROWS, stride=NB), :] = ready[
                            p, i, kz, pl.ds(y, PLANE_ROWS), :
                        ]

    def crossing_kernel(*refs):
        got = [refs[slot_of[d]] for d in range(owners)]
        near, far, up, down = refs[owners:]
        me, odd = position()
        for d in range(owners):
            place = dynamic_place(me ^ d, odd, owners)

            @pl.when(place == owners - 1)
            def _():
                for n, p in enumerate(UPWARD):
                    up[pl.ds(n * PLANE, PLANE), :] = got[d][
                        pl.ds(p * share + share - PLANE, PLANE), :
                    ]

            @pl.when(place == 0)
            def _():
                for n, p in enumerate(DOWNWARD):
                    down[pl.ds(n * PLANE, PLANE), :] = got[d][pl.ds(p * share, PLANE), :]

        for out in (up, down):
            out[pl.ds(faces, 4), :] = jnp.zeros((4, LANES), f32)
        send_sides(odd, up, down, near, far)

    def unpack_kernel(*refs):
        got, main = [refs[slot_of[d]] for d in range(owners)], refs[owners]
        me, odd = position()
        for d in range(owners):
            place = dynamic_place(me ^ d, odd, owners)
            here = pl.multiple_of(place * share, min(share, 8))
            for p in range(Q):
                cx = VELOCITIES[p][0]
                main[p, pl.ds(8 + here + cx * PLANE, share), :] = got[d][
                    pl.ds(p * share, share), :
                ]

    def finish_kernel(main, near, far, out):
        below, above = sides(position()[1], near, far)
        for p in range(Q):
            out[pl.ds(p * WHOLE, WHOLE), :] = main[p, pl.ds(8, WHOLE), :]
        for n, p in enumerate(UPWARD):
            out[pl.ds(p * WHOLE, PLANE), :] = below[n * PLANE : (n + 1) * PLANE]
        for n, p in enumerate(DOWNWARD):
            out[pl.ds(p * WHOLE + WHOLE - PLANE, PLANE), :] = above[n * PLANE : (n + 1) * PLANE]

    def shape(*dims):
        return jax.ShapeDtypeStruct(dims, f32)

    def call(kernel, name, out_shape, inputs, cost, scratch=(), spec=VMEM_SPEC, limit=40):
        outs = jax.tree.map(lambda _: VMEM_SPEC, out_shape)
        return pl.pallas_call(
            kernel,
            out_shape=out_shape,
            in_specs=[spec] * len(inputs),
            out_specs=outs,
            scratch_shapes=list(scratch),
            compiler_params=pltpu.CompilerParams(vmem_limit_bytes=limit * 1024 * 1024),
            cost_estimate=pl.CostEstimate(flops=cost, bytes_accessed=cost, transcendentals=0),
            name=name,
        )(*inputs)

    def exchange(parts):
        return [parts[0]] + [
            lax.ppermute(parts[n], "gx", [(g, g ^ order[n]) for g in range(owners)])
            for n in range(1, owners)
        ]

    def hop(near, far):
        ahead = [(s + 1) % slabs if s % 2 == 0 else (s - 1) % slabs for s in range(slabs)]
        behind = [(s - 1) % slabs if s % 2 == 0 else (s + 1) % slabs for s in range(slabs)]
        return (
            lax.ppermute(near, "gy", list(enumerate(ahead))),
            lax.ppermute(far, "gy", list(enumerate(behind))),
        )

    def padded(count):
        return shape(count, 8 + WHOLE + 8, LANES)

    work = pltpu.VMEM((Q + 1, planes, NB, rows, LANES), f32)
    small, large = 100_000, 4_000_000

    def shards(populations, solid_mask, slot_blocks, swap_slots):
        tiles = B * B * B // LANES
        pops = populations[0].transpose(1, 0, 2).reshape(Q, NB, tiles, LANES)
        pops = pops.transpose(0, 2, 1, 3).reshape(Q, WHOLE, LANES)
        mask = solid_mask[0].reshape(NB, tiles, LANES).transpose(1, 0, 2).reshape(WHOLE, LANES)
        swaps = swap_slots[0, 0].T
        in_place = pl.BlockSpec(memory_space=pltpu.HBM)
        near, far, own = call(
            edge_kernel,
            "edge_planes",
            (shape(rows_hop, LANES), shape(rows_hop, LANES), shape(8, LANES)),
            (pops, mask, slot_blocks, swaps),
            small,
            (
                pltpu.VMEM((rows_hop, LANES), f32),
                pltpu.VMEM((rows_hop, LANES), f32),
                pltpu.VMEM((2, Q, 8, LANES), f32),
                pltpu.VMEM((2, 8, LANES), jnp.int32),
                pltpu.VMEM(slot_blocks.shape, jnp.int32),
                pltpu.VMEM(swaps.shape, jnp.int32),
                pltpu.SemaphoreType.DMA((6,)),
            ),
            in_place,
            62,
        )
        near, far = hop(near, far)
        post = call(
            collide_kernel,
            "first_collision",
            padded(Q + 1),
            (pops, mask),
            large,
        )
        parts = call(
            pack_kernel,
            "pack_planes",
            (shape(rows_in, LANES),) * owners,
            (post, own, near, far),
            large,
        )
        got = exchange(parts)
        parts = call(
            middle_kernel,
            "second_step",
            (shape(rows_out, LANES),) * owners,
            got,
            large,
            (
                work,
                work,
                pltpu.SMEM((owners, 8, LANES), f32),
                pltpu.SemaphoreType.DMA((owners,)),
            ),
        )
        home = exchange(parts)
        near, far = call(
            crossing_kernel,
            "crossing_planes",
            (shape(rows_hop, LANES),) * 2,
            home,
            small,
            (pltpu.VMEM((rows_hop, LANES), f32),) * 2,
        )
        near, far = hop(near, far)
        main = call(unpack_kernel, "unpack_planes", padded(Q), home, large)
        out = call(
            finish_kernel, "finish", shape(Q * WHOLE, LANES), (main, near, far), small
        )
        out = out.reshape(Q, tiles, NB, LANES).transpose(0, 2, 1, 3)
        return out.reshape(Q, NB, B * B * B).transpose(1, 0, 2)[None]

    return shards


def solution(mesh):
    return jax.shard_map(
        build(mesh),
        mesh=mesh,
        in_specs=(
            P("gy", "gx", None, None),
            P("gy", "gx", None),
            P("gy", "gx"),
            P("gy", "gx", None, None),
        ),
        out_specs=P("gy", "gx", None, None),
        check_vma=False,
    )
```

```python
import jax
import jax.numpy as jnp
from jax import lax
from jax.experimental import pallas as pl
from jax.experimental.pallas import tpu as pltpu
from jax.sharding import PartitionSpec as P

B = 16
NB = 2
LANES = 128
PLANE_ROWS = B * B // LANES
PLANE = PLANE_ROWS * NB
WHOLE = B * PLANE

VELOCITIES = (
    (0, 0, 0),
    (1, 0, 0),
    (-1, 0, 0),
    (0, 1, 0),
    (0, -1, 0),
    (0, 0, 1),
    (0, 0, -1),
    (1, 1, 0),
    (-1, -1, 0),
    (1, -1, 0),
    (-1, 1, 0),
    (1, 0, 1),
    (-1, 0, -1),
    (1, 0, -1),
    (-1, 0, 1),
    (0, 1, 1),
    (0, -1, -1),
    (0, 1, -1),
    (0, -1, 1),
)
OPPOSITE = (0, 2, 1, 4, 3, 6, 5, 8, 7, 10, 9, 12, 11, 14, 13, 16, 15, 18, 17)
Q = len(VELOCITIES)
UPWARD = tuple(p for p in range(Q) if VELOCITIES[p][0] == 1)
DOWNWARD = tuple(p for p in range(Q) if VELOCITIES[p][0] == -1)

VMEM_SPEC = pl.BlockSpec(memory_space=pltpu.VMEM)


def dynamic_place(owner, odd_slab, owners):
    pair, core = owner // 2, owner % 2
    forward = 2 * pair + jnp.where(pair % 2 == 0, core, 1 - core)
    return jnp.where(odd_slab == 1, owners - 1 - forward, forward)


def collide(f, fluid):
    def pair(p):
        return f[p] + f[p + 1], f[p] - f[p + 1]

    sx, dx = pair(1)
    sy, dy = pair(3)
    sz, dz = pair(5)
    sxy_a, dxy_a = pair(7)
    sxy_b, dxy_b = pair(9)
    sxz_a, dxz_a = pair(11)
    sxz_b, dxz_b = pair(13)
    syz_a, dyz_a = pair(15)
    syz_b, dyz_b = pair(17)
    axy, bxy = sxy_a + sxy_b, sxy_a - sxy_b
    axz, bxz = sxz_a + sxz_b, sxz_a - sxz_b
    ayz, byz = syz_a + syz_b, syz_a - syz_b
    rho = f[0] + sx + sy + sz + axy + axz + ayz
    ox = dxy_a + dxy_b + dxz_a + dxz_b
    oy = dxy_a - dxy_b + dyz_a + dyz_b
    oz = dxz_a - dxz_b + dyz_a - dyz_b
    jx, jy, jz = dx + ox, dy + oy, dz + oz
    jxx, jyy, jzz = jx * jx, jy * jy, jz * jz
    base = rho * (1.3 / 9.0)
    wide = 1.3 / 3.0
    thin = 1.3 / 6.0
    axy1 = base - 0.3 * axy + wide * (jxx + jyy) - thin * jzz
    axz1 = base - 0.3 * axz + wide * (jxx + jzz) - thin * jyy
    ayz1 = base - 0.3 * ayz + wide * (jyy + jzz) - thin * jxx
    bxy1 = 1.25 * (jx * jy) - 0.25 * bxy
    bxz1 = 1.25 * (jx * jz) - 0.25 * bxz
    byz1 = 1.25 * (jy * jz) - 0.25 * byz
    third = rho * (1.25 / 3.0)
    sx1 = third + 1.25 * jxx - 0.25 * (sx + axy + axz) - axy1 - axz1
    sy1 = third + 1.25 * jyy - 0.25 * (sy + axy + ayz) - axy1 - ayz1
    sz1 = third + 1.25 * jzz - 0.25 * (sz + axz + ayz) - axz1 - ayz1
    rest = rho - sx1 - sy1 - sz1 - axy1 - axz1 - ayz1

    def split(even, odd):
        return 0.5 * (even + odd), 0.5 * (even - odd)

    def diagonal(a1, b1, d_a, d_b, j_first, j_second):
        plus = 0.25 * (j_first + j_second) - 0.5 * d_a
        minus = 0.25 * (j_first - j_second) - 0.5 * d_b
        return split(0.5 * (a1 + b1), plus) + split(0.5 * (a1 - b1), minus)

    relaxed = (
        (rest,)
        + split(sx1, 0.5 * ox)
        + split(sy1, 0.5 * oy)
        + split(sz1, 0.5 * oz)
        + diagonal(axy1, bxy1, dxy_a, dxy_b, jx, jy)
        + diagonal(axz1, bxz1, dxz_a, dxz_b, jx, jz)
        + diagonal(ayz1, byz1, dyz_a, dyz_b, jy, jz)
    )
    return [jnp.where(fluid, relaxed[p], f[OPPOSITE[p]]) for p in range(Q)]


def shift_y(value, step, lane):
    rows = value.shape[0]
    if step == 1:
        turned = pltpu.roll(value, B, 1)
        return jnp.where(lane < B, pltpu.roll(turned, 1, 0), turned)
    turned = pltpu.roll(value, LANES - B, 1)
    return jnp.where(lane >= LANES - B, pltpu.roll(turned, rows - 1, 0), turned)


def shift_z(value, other, step, lane):
    if step == 1:
        return jnp.where(
            lane % B == 0, pltpu.roll(other, LANES - (B - 1), 1), pltpu.roll(value, 1, 1)
        )
    return jnp.where(
        lane % B == B - 1, pltpu.roll(other, B - 1, 1), pltpu.roll(value, LANES - 1, 1)
    )


def build(mesh):
    owners, slabs = mesh.shape["gx"], mesh.shape["gy"]
    planes = B // owners
    share = planes * PLANE
    rows = owners * PLANE_ROWS
    head = (Q + 1) * share
    rows_in = head + 8
    rows_out = Q * share
    faces = len(UPWARD) * PLANE
    rows_hop = faces + 4
    f32 = jnp.float32

    half = owners // 2
    near_group = range(2, half)

    def sent(d, size):
        if d < half:
            return d, 0
        e = d - half
        return (half, (e - 2) * size) if e in near_group else (half + 1, e * size)

    def arrived(d, size):
        if d < half:
            return d, 0
        e = d - half
        return (e, size) if e in near_group else (half + e, 0)

    def pieces(refs, where, size):
        found = [where(d, size) for d in range(owners)]
        return [refs[which].at[pl.ds(base, size), :] for which, base in found]

    def position():
        me = lax.axis_index("gx")
        return me, lax.axis_index("gy") % 2

    def sides(odd, near, far):
        return (
            jnp.where(odd == 1, near[...], far[...]),
            jnp.where(odd == 1, far[...], near[...]),
        )

    def send_sides(odd, up, down, near, far):
        near[...] = jnp.where(odd == 1, down[...], up[...])
        far[...] = jnp.where(odd == 1, up[...], down[...])

    def edge_kernel(pops, mask, slots, swaps, near, far, own, up, down, cells, solid, held, given, sem):
        ends = (WHOLE - 8, 0)
        copies = []
        for n, start in enumerate(ends):
            copies.append((pops.at[:, pl.ds(start, 8), :], cells.at[n]))
            copies.append((mask.at[pl.ds(start, 8), :], solid.at[n]))
        copies += [(slots, held), (swaps, given)]
        copies = [
            pltpu.make_async_copy(source, target, sem.at[n])
            for n, (source, target) in enumerate(copies)
        ]
        for copy in copies:
            copy.start()
        for copy in copies:
            copy.wait()
        own[...] = jnp.zeros((8, LANES), f32)
        own[0:1, 0:NB] = held[...].astype(f32)
        own[1:2, 0:3] = given[0:1].astype(f32)
        for n, (out, chosen, inside) in enumerate(((up, UPWARD, 8 - PLANE), (down, DOWNWARD, 0))):
            after = collide([cells[n, p] for p in range(Q)], solid[n] > 0)
            for m, p in enumerate(chosen):
                out[pl.ds(m * PLANE, PLANE), :] = after[p][inside : inside + PLANE]
            out[pl.ds(faces, 4), :] = own[0:4]
        send_sides(position()[1], up, down, near, far)

    def collide_kernel(cells, solid, post):
        for start in range(0, WHOLE, 8):
            here = pl.ds(start, 8)
            after = collide([cells[p, here, :] for p in range(Q)], solid[here, :] > 0)
            for p in range(Q):
                post[p, pl.ds(8 + start, 8), :] = after[p]
            post[Q, pl.ds(8 + start, 8), :] = solid[here, :].astype(f32)

    def pack_kernel(post, own, near, far, *outs):
        me, odd = position()
        below, above = sides(odd, near, far)
        outs = pieces(outs, sent, rows_in)
        for d in range(owners):
            out = outs[d]
            place = dynamic_place(me ^ d, odd, owners)
            here = pl.multiple_of(place * share, min(share, 8))
            for p in range(Q + 1):
                cx = VELOCITIES[p][0] if p < Q else 0
                out[pl.ds(p * share, share), :] = post[p, pl.ds(8 + here - cx * PLANE, share), :]
            out[pl.ds(head, 2), :] = own[0:2]
            out[pl.ds(head + 2, 2), :] = below[faces : faces + 2]
            out[pl.ds(head + 4, 2), :] = above[faces : faces + 2]
            out[pl.ds(head + 6, 2), :] = own[2:4]

            @pl.when(place == 0)
            def _():
                for n, p in enumerate(UPWARD):
                    out[pl.ds(p * share, PLANE), :] = below[n * PLANE : (n + 1) * PLANE]

            @pl.when(place == owners - 1)
            def _():
                for n, p in enumerate(DOWNWARD):
                    out[pl.ds(p * share + share - PLANE, PLANE), :] = above[
                        n * PLANE : (n + 1) * PLANE
                    ]

    def relay_kernel(*refs):
        own, far, outs = refs[: half - 2], refs[half - 2], refs[half - 1 :]
        size = own[0].shape[0]
        for e in near_group:
            outs[e - 2][pl.ds(0, size), :] = own[e - 2][...]
            outs[e - 2][pl.ds(size, size), :] = far[pl.ds((e - 2) * size, size), :]

    def middle_kernel(*refs):
        inputs, outputs = half + 2, half + 2
        got = pieces(refs[:inputs], arrived, rows_in)
        outs = pieces(refs[inputs : inputs + outputs], sent, rows_out)
        lattice, ready, table, sem = refs[inputs + outputs :]
        me, odd = position()
        place = dynamic_place(me, odd, owners)
        first, last = place == 0, place == owners - 1
        copies = [
            pltpu.make_async_copy(got[d].at[pl.ds(head, 8), :], table.at[d], sem.at[d])
            for d in range(owners)
        ]
        for copy in copies:
            copy.start()
        for copy in copies:
            copy.wait()

        def number(d, row, column):
            return table[d, row, column].astype(jnp.int32)

        def held(d, t, which):
            return number(d, 2 * which, t)

        def final(d, t, which):
            def lead(e, r):
                return number(d ^ e, 2 * which + 1, r)

            flip = lead(0, 2) + lead(4, 2) + lead(4, 1) + lead(6, 1) + lead(6, 0) + lead(7, 0)
            one, two = held(d ^ 7, t, which), held(d ^ 7, 1 - t, which)
            return jnp.where(flip % 2 == 1, two, one)

        def seat(b):
            return b % NB, pl.multiple_of((b // NB) * PLANE_ROWS, PLANE_ROWS)

        for d in range(owners):
            for t in range(NB):
                usual = held(d, t, 0)
                at_usual = seat(usual)
                at_below = seat(jnp.where(first, held(d, t, 1), usual))
                at_above = seat(jnp.where(last, held(d, t, 2), usual))
                for p in range(Q + 1):
                    cx = VELOCITIES[p][0] if p < Q else 0
                    for i in range(planes):
                        kz, y = at_usual
                        if cx == 1 and i == 0:
                            kz, y = at_below
                        if cx == -1 and i == planes - 1:
                            kz, y = at_above
                        lattice[p, i, kz, pl.ds(y, PLANE_ROWS), :] = got[d][
                            pl.ds(p * share + i * PLANE + t, PLANE_ROWS, stride=NB), :
                        ]
        lane = lax.broadcasted_iota(jnp.int32, (rows, LANES), 1)

        def passed(pair, p):
            cx, cy, cz = VELOCITIES[p]
            if cy:
                pair = [shift_y(value, cy, lane) for value in pair]
            if cz:
                pair = [shift_z(pair[kz], pair[1 - kz], cz, lane) for kz in range(NB)]
            return pair

        for i in range(planes):
            for p in range(Q):
                pair = passed([lattice[p, i, kz] for kz in range(NB)], p)
                for kz in range(NB):
                    ready[p, i, kz] = pair[kz]
            for kz in range(NB):
                after = collide([ready[p, i, kz] for p in range(Q)], lattice[Q, i, kz] > 0.5)
                for p in range(Q):
                    lattice[p, i, kz] = after[p]
            for p in range(Q):
                pair = passed([lattice[p, i, kz] for kz in range(NB)], p)
                for kz in range(NB):
                    ready[p, i, kz] = pair[kz]
        for d in range(owners):
            for t in range(NB):
                usual = final(d, t, 0)
                at_usual = seat(usual)
                at_below = seat(jnp.where(first, final(d, t, 1), usual))
                at_above = seat(jnp.where(last, final(d, t, 2), usual))
                for p in range(Q):
                    cx = VELOCITIES[p][0]
                    for i in range(planes):
                        kz, y = at_usual
                        if cx == 1 and i == planes - 1:
                            kz, y = at_above
                        if cx == -1 and i == 0:
                            kz, y = at_below
                        outs[d][pl.ds(p * share + i * PLANE + t, PLANE_ROWS, stride=NB), :] = ready[
                            p, i, kz, pl.ds(y, PLANE_ROWS), :
                        ]

    def crossing_kernel(*refs):
        got = pieces(refs[: half + 2], arrived, rows_out)
        near, far, up, down = refs[half + 2 :]
        me, odd = position()
        for d in range(owners):
            place = dynamic_place(me ^ d, odd, owners)

            @pl.when(place == owners - 1)
            def _():
                for n, p in enumerate(UPWARD):
                    up[pl.ds(n * PLANE, PLANE), :] = got[d][
                        pl.ds(p * share + share - PLANE, PLANE), :
                    ]

            @pl.when(place == 0)
            def _():
                for n, p in enumerate(DOWNWARD):
                    down[pl.ds(n * PLANE, PLANE), :] = got[d][pl.ds(p * share, PLANE), :]

        for out in (up, down):
            out[pl.ds(faces, 4), :] = jnp.zeros((4, LANES), f32)
        send_sides(odd, up, down, near, far)

    def unpack_kernel(*refs):
        got, main = pieces(refs[: half + 2], arrived, rows_out), refs[half + 2]
        me, odd = position()
        for d in range(owners):
            place = dynamic_place(me ^ d, odd, owners)
            here = pl.multiple_of(place * share, min(share, 8))
            for p in range(Q):
                cx = VELOCITIES[p][0]
                main[p, pl.ds(8 + here + cx * PLANE, share), :] = got[d][
                    pl.ds(p * share, share), :
                ]

    def finish_kernel(main, near, far, out):
        below, above = sides(position()[1], near, far)
        for p in range(Q):
            out[pl.ds(p * WHOLE, WHOLE), :] = main[p, pl.ds(8, WHOLE), :]
        for n, p in enumerate(UPWARD):
            out[pl.ds(p * WHOLE, PLANE), :] = below[n * PLANE : (n + 1) * PLANE]
        for n, p in enumerate(DOWNWARD):
            out[pl.ds(p * WHOLE + WHOLE - PLANE, PLANE), :] = above[n * PLANE : (n + 1) * PLANE]

    def shape(*dims):
        return jax.ShapeDtypeStruct(dims, f32)

    def call(kernel, name, out_shape, inputs, cost, scratch=(), spec=VMEM_SPEC, limit=40):
        outs = jax.tree.map(lambda _: VMEM_SPEC, out_shape)
        return pl.pallas_call(
            kernel,
            out_shape=out_shape,
            in_specs=[spec] * len(inputs),
            out_specs=outs,
            scratch_shapes=list(scratch),
            compiler_params=pltpu.CompilerParams(vmem_limit_bytes=limit * 1024 * 1024),
            cost_estimate=pl.CostEstimate(flops=cost, bytes_accessed=cost, transcendentals=0),
            name=name,
        )(*inputs)

    def part_shapes(size):
        return (
            (shape(size, LANES),) * half
            + (shape((half - 2) * size, LANES), shape(2 * size, LANES))
        )

    def swapped(value, d):
        return lax.ppermute(value, "gx", [(g, g ^ d) for g in range(owners)])

    def exchange(parts):
        size = parts[0].shape[0]
        relayed = swapped(parts[half], half)
        direct = swapped(parts[half + 1], half)
        beside = swapped(parts[1], 1)
        doubled = call(
            relay_kernel,
            "relay",
            (shape(2 * size, LANES),) * (half - 2),
            (*parts[2:half], relayed),
            small,
        )
        doubled = [swapped(doubled[e - 2], e) for e in near_group]
        last = swapped(direct[size:], 1)
        return (parts[0], beside, *doubled, direct, last)

    def hop(near, far):
        ahead = [(s + 1) % slabs if s % 2 == 0 else (s - 1) % slabs for s in range(slabs)]
        behind = [(s - 1) % slabs if s % 2 == 0 else (s + 1) % slabs for s in range(slabs)]
        return (
            lax.ppermute(near, "gy", list(enumerate(ahead))),
            lax.ppermute(far, "gy", list(enumerate(behind))),
        )

    def padded(count):
        return shape(count, 8 + WHOLE + 8, LANES)

    small, large = 100_000, 4_000_000
    work = pltpu.VMEM((Q + 1, planes, NB, rows, LANES), f32)

    def shards(populations, solid_mask, slot_blocks, swap_slots):
        tiles = B * B * B // LANES
        pops = populations[0].transpose(1, 0, 2).reshape(Q, NB, tiles, LANES)
        pops = pops.transpose(0, 2, 1, 3).reshape(Q, WHOLE, LANES)
        mask = solid_mask[0].reshape(NB, tiles, LANES).transpose(1, 0, 2).reshape(WHOLE, LANES)
        swaps = swap_slots[0, 0].T
        in_place = pl.BlockSpec(memory_space=pltpu.HBM)
        near, far, own = call(
            edge_kernel,
            "edge_planes",
            (shape(rows_hop, LANES), shape(rows_hop, LANES), shape(8, LANES)),
            (pops, mask, slot_blocks, swaps),
            small,
            (
                pltpu.VMEM((rows_hop, LANES), f32),
                pltpu.VMEM((rows_hop, LANES), f32),
                pltpu.VMEM((2, Q, 8, LANES), f32),
                pltpu.VMEM((2, 8, LANES), jnp.int32),
                pltpu.VMEM(slot_blocks.shape, jnp.int32),
                pltpu.VMEM(swaps.shape, jnp.int32),
                pltpu.SemaphoreType.DMA((6,)),
            ),
            in_place,
            62,
        )
        near, far = hop(near, far)
        post = call(
            collide_kernel,
            "first_collision",
            padded(Q + 1),
            (pops, mask),
            large,
        )
        parts = call(
            pack_kernel,
            "pack_planes",
            part_shapes(rows_in),
            (post, own, near, far),
            large,
        )
        got = exchange(parts)
        parts = call(
            middle_kernel,
            "second_step",
            part_shapes(rows_out),
            got,
            large,
            (
                work,
                work,
                pltpu.SMEM((owners, 8, LANES), f32),
                pltpu.SemaphoreType.DMA((owners,)),
            ),
        )
        home = exchange(parts)
        near, far = call(
            crossing_kernel,
            "crossing_planes",
            (shape(rows_hop, LANES),) * 2,
            home,
            small,
            (pltpu.VMEM((rows_hop, LANES), f32),) * 2,
        )
        near, far = hop(near, far)
        main = call(unpack_kernel, "unpack_planes", padded(Q), home, large)
        out = call(
            finish_kernel, "finish", shape(Q * WHOLE, LANES), (main, near, far), small
        )
        out = out.reshape(Q, tiles, NB, LANES).transpose(0, 2, 1, 3)
        return out.reshape(Q, NB, B * B * B).transpose(1, 0, 2)[None]

    return shards


def solution(mesh):
    return jax.shard_map(
        build(mesh),
        mesh=mesh,
        in_specs=(
            P("gy", "gx", None, None),
            P("gy", "gx", None),
            P("gy", "gx"),
            P("gy", "gx", None, None),
        ),
        out_specs=P("gy", "gx", None, None),
        check_vma=False,
    )
```

```python
import jax
import jax.numpy as jnp
from jax import lax
from jax.experimental import pallas as pl
from jax.experimental.pallas import tpu as pltpu
from jax.sharding import PartitionSpec as P

B = 16
NB = 2
LANES = 128
PLANE_ROWS = B * B // LANES
PLANE = PLANE_ROWS * NB
WHOLE = B * PLANE

VELOCITIES = (
    (0, 0, 0),
    (1, 0, 0),
    (-1, 0, 0),
    (0, 1, 0),
    (0, -1, 0),
    (0, 0, 1),
    (0, 0, -1),
    (1, 1, 0),
    (-1, -1, 0),
    (1, -1, 0),
    (-1, 1, 0),
    (1, 0, 1),
    (-1, 0, -1),
    (1, 0, -1),
    (-1, 0, 1),
    (0, 1, 1),
    (0, -1, -1),
    (0, 1, -1),
    (0, -1, 1),
)
OPPOSITE = (0, 2, 1, 4, 3, 6, 5, 8, 7, 10, 9, 12, 11, 14, 13, 16, 15, 18, 17)
Q = len(VELOCITIES)
UPWARD = tuple(p for p in range(Q) if VELOCITIES[p][0] == 1)
DOWNWARD = tuple(p for p in range(Q) if VELOCITIES[p][0] == -1)

VMEM_SPEC = pl.BlockSpec(memory_space=pltpu.VMEM)


def dynamic_place(owner, odd_slab, owners):
    pair, core = owner // 2, owner % 2
    forward = 2 * pair + jnp.where(pair % 2 == 0, core, 1 - core)
    return jnp.where(odd_slab == 1, owners - 1 - forward, forward)


def collide(f, fluid):
    def pair(p):
        return f[p] + f[p + 1], f[p] - f[p + 1]

    sx, dx = pair(1)
    sy, dy = pair(3)
    sz, dz = pair(5)
    sxy_a, dxy_a = pair(7)
    sxy_b, dxy_b = pair(9)
    sxz_a, dxz_a = pair(11)
    sxz_b, dxz_b = pair(13)
    syz_a, dyz_a = pair(15)
    syz_b, dyz_b = pair(17)
    axy, bxy = sxy_a + sxy_b, sxy_a - sxy_b
    axz, bxz = sxz_a + sxz_b, sxz_a - sxz_b
    ayz, byz = syz_a + syz_b, syz_a - syz_b
    rho = f[0] + sx + sy + sz + axy + axz + ayz
    ox = dxy_a + dxy_b + dxz_a + dxz_b
    oy = dxy_a - dxy_b + dyz_a + dyz_b
    oz = dxz_a - dxz_b + dyz_a - dyz_b
    jx, jy, jz = dx + ox, dy + oy, dz + oz
    jxx, jyy, jzz = jx * jx, jy * jy, jz * jz
    base = rho * (1.3 / 9.0)
    wide = 1.3 / 3.0
    thin = 1.3 / 6.0
    axy1 = base - 0.3 * axy + wide * (jxx + jyy) - thin * jzz
    axz1 = base - 0.3 * axz + wide * (jxx + jzz) - thin * jyy
    ayz1 = base - 0.3 * ayz + wide * (jyy + jzz) - thin * jxx
    bxy1 = 1.25 * (jx * jy) - 0.25 * bxy
    bxz1 = 1.25 * (jx * jz) - 0.25 * bxz
    byz1 = 1.25 * (jy * jz) - 0.25 * byz
    third = rho * (1.25 / 3.0)
    sx1 = third + 1.25 * jxx - 0.25 * (sx + axy + axz) - axy1 - axz1
    sy1 = third + 1.25 * jyy - 0.25 * (sy + axy + ayz) - axy1 - ayz1
    sz1 = third + 1.25 * jzz - 0.25 * (sz + axz + ayz) - axz1 - ayz1
    rest = rho - sx1 - sy1 - sz1 - axy1 - axz1 - ayz1

    def split(even, odd):
        return 0.5 * (even + odd), 0.5 * (even - odd)

    def diagonal(a1, b1, d_a, d_b, j_first, j_second):
        plus = 0.25 * (j_first + j_second) - 0.5 * d_a
        minus = 0.25 * (j_first - j_second) - 0.5 * d_b
        return split(0.5 * (a1 + b1), plus) + split(0.5 * (a1 - b1), minus)

    relaxed = (
        (rest,)
        + split(sx1, 0.5 * ox)
        + split(sy1, 0.5 * oy)
        + split(sz1, 0.5 * oz)
        + diagonal(axy1, bxy1, dxy_a, dxy_b, jx, jy)
        + diagonal(axz1, bxz1, dxz_a, dxz_b, jx, jz)
        + diagonal(ayz1, byz1, dyz_a, dyz_b, jy, jz)
    )
    return [jnp.where(fluid, relaxed[p], f[OPPOSITE[p]]) for p in range(Q)]


def shift_y(value, step, lane):
    rows = value.shape[0]
    if step == 1:
        turned = pltpu.roll(value, B, 1)
        return jnp.where(lane < B, pltpu.roll(turned, 1, 0), turned)
    turned = pltpu.roll(value, LANES - B, 1)
    return jnp.where(lane >= LANES - B, pltpu.roll(turned, rows - 1, 0), turned)


def shift_z(value, other, step, lane):
    if step == 1:
        return jnp.where(
            lane % B == 0, pltpu.roll(other, LANES - (B - 1), 1), pltpu.roll(value, 1, 1)
        )
    return jnp.where(
        lane % B == B - 1, pltpu.roll(other, B - 1, 1), pltpu.roll(value, LANES - 1, 1)
    )


def build(mesh):
    owners, slabs = mesh.shape["gx"], mesh.shape["gy"]
    planes = B // owners
    share = planes * PLANE
    rows = owners * PLANE_ROWS
    head = (Q + 1) * share
    rows_in = head + 8
    rows_out = Q * share
    faces = len(UPWARD) * PLANE
    rows_hop = faces + 4
    f32 = jnp.float32

    half = owners // 2
    near_group = range(1, half)

    def sent(d, size):
        return (d, 0) if d < half else (half, (d - half) * size)

    def arrived(d, size):
        if d < half:
            return d, 0
        return (half, 0) if d == half else (d - half, size)

    def pieces(refs, where, size):
        found = [where(d, size) for d in range(owners)]
        return [refs[which].at[pl.ds(base, size), :] for which, base in found]

    def position():
        me = lax.axis_index("gx")
        return me, lax.axis_index("gy") % 2

    def sides(odd, near, far):
        return (
            jnp.where(odd == 1, near[...], far[...]),
            jnp.where(odd == 1, far[...], near[...]),
        )

    def send_sides(odd, up, down, near, far):
        near[...] = jnp.where(odd == 1, down[...], up[...])
        far[...] = jnp.where(odd == 1, up[...], down[...])

    def edge_kernel(pops, mask, slots, swaps, near, far, own, up, down, cells, solid, held, given, sem):
        ends = (WHOLE - 8, 0)
        copies = []
        for n, start in enumerate(ends):
            copies.append((pops.at[:, pl.ds(start, 8), :], cells.at[n]))
            copies.append((mask.at[pl.ds(start, 8), :], solid.at[n]))
        copies += [(slots, held), (swaps, given)]
        copies = [
            pltpu.make_async_copy(source, target, sem.at[n])
            for n, (source, target) in enumerate(copies)
        ]
        for copy in copies:
            copy.start()
        for copy in copies:
            copy.wait()
        own[...] = jnp.zeros((8, LANES), f32)
        own[0:1, 0:NB] = held[...].astype(f32)
        own[1:2, 0:3] = given[0:1].astype(f32)
        for n, (out, chosen, inside) in enumerate(((up, UPWARD, 8 - PLANE), (down, DOWNWARD, 0))):
            after = collide([cells[n, p] for p in range(Q)], solid[n] > 0)
            for m, p in enumerate(chosen):
                out[pl.ds(m * PLANE, PLANE), :] = after[p][inside : inside + PLANE]
            out[pl.ds(faces, 4), :] = own[0:4]
        send_sides(position()[1], up, down, near, far)

    def collide_kernel(cells, solid, post):
        for start in range(0, WHOLE, 8):
            here = pl.ds(start, 8)
            after = collide([cells[p, here, :] for p in range(Q)], solid[here, :] > 0)
            for p in range(Q):
                post[p, pl.ds(8 + start, 8), :] = after[p]
            post[Q, pl.ds(8 + start, 8), :] = solid[here, :].astype(f32)

    def pack_kernel(post, own, near, far, *outs):
        me, odd = position()
        below, above = sides(odd, near, far)
        outs = pieces(outs, sent, rows_in)
        for d in range(owners):
            out = outs[d]
            place = dynamic_place(me ^ d, odd, owners)
            here = pl.multiple_of(place * share, min(share, 8))
            for p in range(Q + 1):
                cx = VELOCITIES[p][0] if p < Q else 0
                out[pl.ds(p * share, share), :] = post[p, pl.ds(8 + here - cx * PLANE, share), :]
            out[pl.ds(head, 2), :] = own[0:2]
            out[pl.ds(head + 2, 2), :] = below[faces : faces + 2]
            out[pl.ds(head + 4, 2), :] = above[faces : faces + 2]
            out[pl.ds(head + 6, 2), :] = own[2:4]

            @pl.when(place == 0)
            def _():
                for n, p in enumerate(UPWARD):
                    out[pl.ds(p * share, PLANE), :] = below[n * PLANE : (n + 1) * PLANE]

            @pl.when(place == owners - 1)
            def _():
                for n, p in enumerate(DOWNWARD):
                    out[pl.ds(p * share + share - PLANE, PLANE), :] = above[
                        n * PLANE : (n + 1) * PLANE
                    ]

    def relay_kernel(*refs):
        own, far, outs = refs[: half - 1], refs[half - 1], refs[half:]
        size = own[0].shape[0]
        for e in near_group:
            outs[e - 1][pl.ds(0, size), :] = own[e - 1][...]
            outs[e - 1][pl.ds(size, size), :] = far[pl.ds(e * size, size), :]

    def middle_kernel(*refs):
        inputs, outputs = half + 1, half + 1
        got = pieces(refs[:inputs], arrived, rows_in)
        outs = pieces(refs[inputs : inputs + outputs], sent, rows_out)
        lattice, ready, table, sem = refs[inputs + outputs :]
        me, odd = position()
        place = dynamic_place(me, odd, owners)
        first, last = place == 0, place == owners - 1
        copies = [
            pltpu.make_async_copy(got[d].at[pl.ds(head, 8), :], table.at[d], sem.at[d])
            for d in range(owners)
        ]
        for copy in copies:
            copy.start()
        for copy in copies:
            copy.wait()

        def number(d, row, column):
            return table[d, row, column].astype(jnp.int32)

        def held(d, t, which):
            return number(d, 2 * which, t)

        def final(d, t, which):
            def lead(e, r):
                return number(d ^ e, 2 * which + 1, r)

            flip = lead(0, 2) + lead(4, 2) + lead(4, 1) + lead(6, 1) + lead(6, 0) + lead(7, 0)
            one, two = held(d ^ 7, t, which), held(d ^ 7, 1 - t, which)
            return jnp.where(flip % 2 == 1, two, one)

        def seat(b):
            return b % NB, pl.multiple_of((b // NB) * PLANE_ROWS, PLANE_ROWS)

        for d in range(owners):
            for t in range(NB):
                usual = held(d, t, 0)
                at_usual = seat(usual)
                at_below = seat(jnp.where(first, held(d, t, 1), usual))
                at_above = seat(jnp.where(last, held(d, t, 2), usual))
                for p in range(Q + 1):
                    cx = VELOCITIES[p][0] if p < Q else 0
                    for i in range(planes):
                        kz, y = at_usual
                        if cx == 1 and i == 0:
                            kz, y = at_below
                        if cx == -1 and i == planes - 1:
                            kz, y = at_above
                        lattice[p, i, kz, pl.ds(y, PLANE_ROWS), :] = got[d][
                            pl.ds(p * share + i * PLANE + t, PLANE_ROWS, stride=NB), :
                        ]
        lane = lax.broadcasted_iota(jnp.int32, (rows, LANES), 1)

        def passed(pair, p):
            cx, cy, cz = VELOCITIES[p]
            if cy:
                pair = [shift_y(value, cy, lane) for value in pair]
            if cz:
                pair = [shift_z(pair[kz], pair[1 - kz], cz, lane) for kz in range(NB)]
            return pair

        for i in range(planes):
            for p in range(Q):
                pair = passed([lattice[p, i, kz] for kz in range(NB)], p)
                for kz in range(NB):
                    ready[p, i, kz] = pair[kz]
            for kz in range(NB):
                after = collide([ready[p, i, kz] for p in range(Q)], lattice[Q, i, kz] > 0.5)
                for p in range(Q):
                    lattice[p, i, kz] = after[p]
            for p in range(Q):
                pair = passed([lattice[p, i, kz] for kz in range(NB)], p)
                for kz in range(NB):
                    ready[p, i, kz] = pair[kz]
        for d in range(owners):
            for t in range(NB):
                usual = final(d, t, 0)
                at_usual = seat(usual)
                at_below = seat(jnp.where(first, final(d, t, 1), usual))
                at_above = seat(jnp.where(last, final(d, t, 2), usual))
                for p in range(Q):
                    cx = VELOCITIES[p][0]
                    for i in range(planes):
                        kz, y = at_usual
                        if cx == 1 and i == planes - 1:
                            kz, y = at_above
                        if cx == -1 and i == 0:
                            kz, y = at_below
                        outs[d][pl.ds(p * share + i * PLANE + t, PLANE_ROWS, stride=NB), :] = ready[
                            p, i, kz, pl.ds(y, PLANE_ROWS), :
                        ]

    def crossing_kernel(*refs):
        got = pieces(refs[: half + 1], arrived, rows_out)
        near, far, up, down = refs[half + 1 :]
        me, odd = position()
        for d in range(owners):
            place = dynamic_place(me ^ d, odd, owners)

            @pl.when(place == owners - 1)
            def _():
                for n, p in enumerate(UPWARD):
                    up[pl.ds(n * PLANE, PLANE), :] = got[d][
                        pl.ds(p * share + share - PLANE, PLANE), :
                    ]

            @pl.when(place == 0)
            def _():
                for n, p in enumerate(DOWNWARD):
                    down[pl.ds(n * PLANE, PLANE), :] = got[d][pl.ds(p * share, PLANE), :]

        for out in (up, down):
            out[pl.ds(faces, 4), :] = jnp.zeros((4, LANES), f32)
        send_sides(odd, up, down, near, far)

    def unpack_kernel(*refs):
        got, main = pieces(refs[: half + 1], arrived, rows_out), refs[half + 1]
        me, odd = position()
        for d in range(owners):
            place = dynamic_place(me ^ d, odd, owners)
            here = pl.multiple_of(place * share, min(share, 8))
            for p in range(Q):
                cx = VELOCITIES[p][0]
                main[p, pl.ds(8 + here + cx * PLANE, share), :] = got[d][
                    pl.ds(p * share, share), :
                ]

    def finish_kernel(main, near, far, out):
        below, above = sides(position()[1], near, far)
        for p in range(Q):
            out[pl.ds(p * WHOLE, WHOLE), :] = main[p, pl.ds(8, WHOLE), :]
        for n, p in enumerate(UPWARD):
            out[pl.ds(p * WHOLE, PLANE), :] = below[n * PLANE : (n + 1) * PLANE]
        for n, p in enumerate(DOWNWARD):
            out[pl.ds(p * WHOLE + WHOLE - PLANE, PLANE), :] = above[n * PLANE : (n + 1) * PLANE]

    def shape(*dims):
        return jax.ShapeDtypeStruct(dims, f32)

    def call(kernel, name, out_shape, inputs, cost, scratch=(), spec=VMEM_SPEC, limit=40):
        outs = jax.tree.map(lambda _: VMEM_SPEC, out_shape)
        return pl.pallas_call(
            kernel,
            out_shape=out_shape,
            in_specs=[spec] * len(inputs),
            out_specs=outs,
            scratch_shapes=list(scratch),
            compiler_params=pltpu.CompilerParams(vmem_limit_bytes=limit * 1024 * 1024),
            cost_estimate=pl.CostEstimate(flops=cost, bytes_accessed=cost, transcendentals=0),
            name=name,
        )(*inputs)

    def part_shapes(size):
        return (shape(size, LANES),) * half + (shape(half * size, LANES),)

    def swapped(value, d):
        return lax.ppermute(value, "gx", [(g, g ^ d) for g in range(owners)])

    def exchange(parts):
        size = parts[0].shape[0]
        across = swapped(parts[half], half)
        doubled = call(
            relay_kernel,
            "relay",
            (shape(2 * size, LANES),) * (half - 1),
            (*parts[1:half], across),
            small,
        )
        return (parts[0], *(swapped(doubled[e - 1], e) for e in near_group), across)

    def hop(near, far):
        ahead = [(s + 1) % slabs if s % 2 == 0 else (s - 1) % slabs for s in range(slabs)]
        behind = [(s - 1) % slabs if s % 2 == 0 else (s + 1) % slabs for s in range(slabs)]
        return (
            lax.ppermute(near, "gy", list(enumerate(ahead))),
            lax.ppermute(far, "gy", list(enumerate(behind))),
        )

    def padded(count):
        return shape(count, 8 + WHOLE + 8, LANES)

    small, large = 100_000, 4_000_000
    work = pltpu.VMEM((Q + 1, planes, NB, rows, LANES), f32)

    def shards(populations, solid_mask, slot_blocks, swap_slots):
        tiles = B * B * B // LANES
        pops = populations[0].transpose(1, 0, 2).reshape(Q, NB, tiles, LANES)
        pops = pops.transpose(0, 2, 1, 3).reshape(Q, WHOLE, LANES)
        mask = solid_mask[0].reshape(NB, tiles, LANES).transpose(1, 0, 2).reshape(WHOLE, LANES)
        swaps = swap_slots[0, 0].T
        in_place = pl.BlockSpec(memory_space=pltpu.HBM)
        near, far, own = call(
            edge_kernel,
            "edge_planes",
            (shape(rows_hop, LANES), shape(rows_hop, LANES), shape(8, LANES)),
            (pops, mask, slot_blocks, swaps),
            small,
            (
                pltpu.VMEM((rows_hop, LANES), f32),
                pltpu.VMEM((rows_hop, LANES), f32),
                pltpu.VMEM((2, Q, 8, LANES), f32),
                pltpu.VMEM((2, 8, LANES), jnp.int32),
                pltpu.VMEM(slot_blocks.shape, jnp.int32),
                pltpu.VMEM(swaps.shape, jnp.int32),
                pltpu.SemaphoreType.DMA((6,)),
            ),
            in_place,
            62,
        )
        near, far = hop(near, far)
        post = call(
            collide_kernel,
            "first_collision",
            padded(Q + 1),
            (pops, mask),
            large,
        )
        parts = call(
            pack_kernel,
            "pack_planes",
            part_shapes(rows_in),
            (post, own, near, far),
            large,
        )
        got = exchange(parts)
        parts = call(
            middle_kernel,
            "second_step",
            part_shapes(rows_out),
            got,
            large,
            (
                work,
                work,
                pltpu.SMEM((owners, 8, LANES), f32),
                pltpu.SemaphoreType.DMA((owners,)),
            ),
        )
        home = exchange(parts)
        near, far = call(
            crossing_kernel,
            "crossing_planes",
            (shape(rows_hop, LANES),) * 2,
            home,
            small,
            (pltpu.VMEM((rows_hop, LANES), f32),) * 2,
        )
        near, far = hop(near, far)
        main = call(unpack_kernel, "unpack_planes", padded(Q), home, large)
        out = call(
            finish_kernel, "finish", shape(Q * WHOLE, LANES), (main, near, far), small
        )
        out = out.reshape(Q, tiles, NB, LANES).transpose(0, 2, 1, 3)
        return out.reshape(Q, NB, B * B * B).transpose(1, 0, 2)[None]

    return shards


def solution(mesh):
    return jax.shard_map(
        build(mesh),
        mesh=mesh,
        in_specs=(
            P("gy", "gx", None, None),
            P("gy", "gx", None),
            P("gy", "gx"),
            P("gy", "gx", None, None),
        ),
        out_specs=P("gy", "gx", None, None),
        check_vma=False,
    )
```

```python
import jax
import jax.numpy as jnp
from jax import lax
from jax.experimental import pallas as pl
from jax.experimental.pallas import tpu as pltpu
from jax.sharding import PartitionSpec as P

B = 16
NB = 2
LANES = 128
PLANE_ROWS = B * B // LANES
PLANE = PLANE_ROWS * NB
FLIGHT = 5
WHOLE = B * PLANE

VELOCITIES = (
    (0, 0, 0),
    (1, 0, 0),
    (-1, 0, 0),
    (0, 1, 0),
    (0, -1, 0),
    (0, 0, 1),
    (0, 0, -1),
    (1, 1, 0),
    (-1, -1, 0),
    (1, -1, 0),
    (-1, 1, 0),
    (1, 0, 1),
    (-1, 0, -1),
    (1, 0, -1),
    (-1, 0, 1),
    (0, 1, 1),
    (0, -1, -1),
    (0, 1, -1),
    (0, -1, 1),
)
OPPOSITE = (0, 2, 1, 4, 3, 6, 5, 8, 7, 10, 9, 12, 11, 14, 13, 16, 15, 18, 17)
Q = len(VELOCITIES)
UPWARD = tuple(p for p in range(Q) if VELOCITIES[p][0] == 1)
DOWNWARD = tuple(p for p in range(Q) if VELOCITIES[p][0] == -1)

LEVEL = tuple(p for p in range(Q) if VELOCITIES[p][0] == 0)
SLOPED = UPWARD + DOWNWARD

VMEM_SPEC = pl.BlockSpec(memory_space=pltpu.VMEM)


def dynamic_place(owner, odd_slab, owners):
    pair, core = owner // 2, owner % 2
    forward = 2 * pair + jnp.where(pair % 2 == 0, core, 1 - core)
    return jnp.where(odd_slab == 1, owners - 1 - forward, forward)


def collide(f, fluid):
    def pair(p):
        return f[p] + f[p + 1], f[p] - f[p + 1]

    sx, dx = pair(1)
    sy, dy = pair(3)
    sz, dz = pair(5)
    sxy_a, dxy_a = pair(7)
    sxy_b, dxy_b = pair(9)
    sxz_a, dxz_a = pair(11)
    sxz_b, dxz_b = pair(13)
    syz_a, dyz_a = pair(15)
    syz_b, dyz_b = pair(17)
    axy, bxy = sxy_a + sxy_b, sxy_a - sxy_b
    axz, bxz = sxz_a + sxz_b, sxz_a - sxz_b
    ayz, byz = syz_a + syz_b, syz_a - syz_b
    rho = f[0] + sx + sy + sz + axy + axz + ayz
    ox = dxy_a + dxy_b + dxz_a + dxz_b
    oy = dxy_a - dxy_b + dyz_a + dyz_b
    oz = dxz_a - dxz_b + dyz_a - dyz_b
    jx, jy, jz = dx + ox, dy + oy, dz + oz
    jxx, jyy, jzz = jx * jx, jy * jy, jz * jz
    base = rho * (1.3 / 9.0)
    wide = 1.3 / 3.0
    thin = 1.3 / 6.0
    axy1 = base - 0.3 * axy + wide * (jxx + jyy) - thin * jzz
    axz1 = base - 0.3 * axz + wide * (jxx + jzz) - thin * jyy
    ayz1 = base - 0.3 * ayz + wide * (jyy + jzz) - thin * jxx
    bxy1 = 1.25 * (jx * jy) - 0.25 * bxy
    bxz1 = 1.25 * (jx * jz) - 0.25 * bxz
    byz1 = 1.25 * (jy * jz) - 0.25 * byz
    third = rho * (1.25 / 3.0)
    sx1 = third + 1.25 * jxx - 0.25 * (sx + axy + axz) - axy1 - axz1
    sy1 = third + 1.25 * jyy - 0.25 * (sy + axy + ayz) - axy1 - ayz1
    sz1 = third + 1.25 * jzz - 0.25 * (sz + axz + ayz) - axz1 - ayz1
    rest = rho - sx1 - sy1 - sz1 - axy1 - axz1 - ayz1

    def split(even, odd):
        return 0.5 * (even + odd), 0.5 * (even - odd)

    def diagonal(a1, b1, d_a, d_b, j_first, j_second):
        plus = 0.25 * (j_first + j_second) - 0.5 * d_a
        minus = 0.25 * (j_first - j_second) - 0.5 * d_b
        return split(0.5 * (a1 + b1), plus) + split(0.5 * (a1 - b1), minus)

    relaxed = (
        (rest,)
        + split(sx1, 0.5 * ox)
        + split(sy1, 0.5 * oy)
        + split(sz1, 0.5 * oz)
        + diagonal(axy1, bxy1, dxy_a, dxy_b, jx, jy)
        + diagonal(axz1, bxz1, dxz_a, dxz_b, jx, jz)
        + diagonal(ayz1, byz1, dyz_a, dyz_b, jy, jz)
    )
    return [jnp.where(fluid, relaxed[p], f[OPPOSITE[p]]) for p in range(Q)]


def shift_y(value, step, lane):
    rows = value.shape[0]
    if step == 1:
        turned = pltpu.roll(value, B, 1)
        return jnp.where(lane < B, pltpu.roll(turned, 1, 0), turned)
    turned = pltpu.roll(value, LANES - B, 1)
    return jnp.where(lane >= LANES - B, pltpu.roll(turned, rows - 1, 0), turned)


def shift_z(value, other, step, lane):
    if step == 1:
        return jnp.where(
            lane % B == 0, pltpu.roll(other, LANES - (B - 1), 1), pltpu.roll(value, 1, 1)
        )
    return jnp.where(
        lane % B == B - 1, pltpu.roll(other, B - 1, 1), pltpu.roll(value, LANES - 1, 1)
    )


def build(mesh):
    owners, slabs = mesh.shape["gx"], mesh.shape["gy"]
    planes = B // owners
    share = planes * PLANE
    rows = owners * PLANE_ROWS
    level_in = LEVEL + (Q,)
    head = len(SLOPED) * share
    sizes_in = (len(level_in) * share, head + 8)
    sizes_out = (len(LEVEL) * share, head)
    half = owners // 2
    faces = len(UPWARD) * PLANE
    rows_hop = faces + 4
    f32 = jnp.float32

    def spot(p):
        if p in SLOPED:
            return 1, SLOPED.index(p) * share
        return 0, level_in.index(p) * share

    def pieces(whole, level, sloped, sizes):
        pairs = [
            (ref.at[pl.ds(0, sizes[0]), :], ref.at[pl.ds(sizes[0], sizes[1]), :]) for ref in whole
        ]
        return pairs + list(zip(level, sloped))

    def cut(refs, lengths):
        groups, start = [], 0
        for length in lengths:
            groups.append(refs[start : start + length])
            start += length
        return groups + [refs[start:]]

    def position():
        me = lax.axis_index("gx")
        return me, lax.axis_index("gy") % 2

    def sides(odd, near, far):
        return (
            jnp.where(odd == 1, near[...], far[...]),
            jnp.where(odd == 1, far[...], near[...]),
        )

    def send_sides(odd, up, down, near, far):
        near[...] = jnp.where(odd == 1, down[...], up[...])
        far[...] = jnp.where(odd == 1, up[...], down[...])

    def edge_kernel(pops, mask, slots, swaps, near, far, own, up, down, cells, solid, held, given, sem):
        ends = (WHOLE - 8, 0)
        copies = []
        for n, start in enumerate(ends):
            copies.append((pops.at[:, pl.ds(start, 8), :], cells.at[n]))
            copies.append((mask.at[pl.ds(start, 8), :], solid.at[n]))
        copies += [(slots, held), (swaps, given)]
        copies = [
            pltpu.make_async_copy(source, target, sem.at[n])
            for n, (source, target) in enumerate(copies)
        ]
        for copy in copies:
            copy.start()
        for copy in copies:
            copy.wait()
        own[...] = jnp.zeros((8, LANES), f32)
        own[0:1, 0:NB] = held[...].astype(f32)
        own[1:2, 0:3] = given[0:1].astype(f32)
        for n, (out, chosen, inside) in enumerate(((up, UPWARD, 8 - PLANE), (down, DOWNWARD, 0))):
            after = collide([cells[n, p] for p in range(Q)], solid[n] > 0)
            for m, p in enumerate(chosen):
                out[pl.ds(m * PLANE, PLANE), :] = after[p][inside : inside + PLANE]
            out[pl.ds(faces, 4), :] = own[0:4]
        send_sides(position()[1], up, down, near, far)

    def collide_kernel(cells, solid, post):
        for start in range(0, WHOLE, 8):
            here = pl.ds(start, 8)
            after = collide([cells[p, here, :] for p in range(Q)], solid[here, :] > 0)
            for p in range(Q):
                post[p, pl.ds(8 + start, 8), :] = after[p]
            post[Q, pl.ds(8 + start, 8), :] = solid[here, :].astype(f32)

    def pack_kernel(post, own, near, far, *outs):
        me, odd = position()
        below, above = sides(odd, near, far)
        outs = pieces(outs, (), (), sizes_in)
        for d in range(owners):
            place = dynamic_place(me ^ d, odd, owners)
            here = pl.multiple_of(place * share, min(share, 8))
            for p in range(Q + 1):
                cx = VELOCITIES[p][0] if p < Q else 0
                part, row = spot(p)
                outs[d][part][pl.ds(row, share), :] = post[
                    p, pl.ds(8 + here - cx * PLANE, share), :
                ]
            out = outs[d][1]
            out[pl.ds(head, 2), :] = own[0:2]
            out[pl.ds(head + 2, 2), :] = below[faces : faces + 2]
            out[pl.ds(head + 4, 2), :] = above[faces : faces + 2]
            out[pl.ds(head + 6, 2), :] = own[2:4]

            @pl.when(place == 0)
            def _():
                for n, p in enumerate(UPWARD):
                    out[pl.ds(spot(p)[1], PLANE), :] = below[n * PLANE : (n + 1) * PLANE]

            @pl.when(place == owners - 1)
            def _():
                for n, p in enumerate(DOWNWARD):
                    out[pl.ds(spot(p)[1] + share - PLANE, PLANE), :] = above[
                        n * PLANE : (n + 1) * PLANE
                    ]

    def middle_kernel(*refs):
        got, *groups, rest = cut(refs, (owners, half, half, half))
        got = pieces(got, (), (), sizes_in)
        outs = pieces(*groups, sizes_out)
        lattice, ready, table, sem = rest
        me, odd = position()
        place = dynamic_place(me, odd, owners)
        first, last = place == 0, place == owners - 1
        copies = [
            pltpu.make_async_copy(got[d][1].at[pl.ds(head, 8), :], table.at[d], sem.at[d])
            for d in range(owners)
        ]
        for copy in copies:
            copy.start()
        for copy in copies:
            copy.wait()

        def number(d, row, column):
            return table[d, row, column].astype(jnp.int32)

        def held(d, t, which):
            return number(d, 2 * which, t)

        def final(d, t, which):
            def lead(e, r):
                return number(d ^ e, 2 * which + 1, r)

            flip = lead(0, 2) + lead(4, 2) + lead(4, 1) + lead(6, 1) + lead(6, 0) + lead(7, 0)
            one, two = held(d ^ 7, t, which), held(d ^ 7, 1 - t, which)
            return jnp.where(flip % 2 == 1, two, one)

        def seat(b):
            return b % NB, pl.multiple_of((b // NB) * PLANE_ROWS, PLANE_ROWS)

        for d in range(owners):
            for t in range(NB):
                usual = held(d, t, 0)
                at_usual = seat(usual)
                at_below = seat(jnp.where(first, held(d, t, 1), usual))
                at_above = seat(jnp.where(last, held(d, t, 2), usual))
                for p in range(Q + 1):
                    cx = VELOCITIES[p][0] if p < Q else 0
                    for i in range(planes):
                        kz, y = at_usual
                        if cx == 1 and i == 0:
                            kz, y = at_below
                        if cx == -1 and i == planes - 1:
                            kz, y = at_above
                        part, row = spot(p)
                        lattice[p, i, kz, pl.ds(y, PLANE_ROWS), :] = got[d][part][
                            pl.ds(row + i * PLANE + t, PLANE_ROWS, stride=NB), :
                        ]
        lane = lax.broadcasted_iota(jnp.int32, (rows, LANES), 1)

        def passed(pair, p):
            cx, cy, cz = VELOCITIES[p]
            if cy:
                pair = [shift_y(value, cy, lane) for value in pair]
            if cz:
                pair = [shift_z(pair[kz], pair[1 - kz], cz, lane) for kz in range(NB)]
            return pair

        for i in range(planes):
            for p in range(Q):
                pair = passed([lattice[p, i, kz] for kz in range(NB)], p)
                for kz in range(NB):
                    ready[p, i, kz] = pair[kz]
            for kz in range(NB):
                after = collide([ready[p, i, kz] for p in range(Q)], lattice[Q, i, kz] > 0.5)
                for p in range(Q):
                    lattice[p, i, kz] = after[p]
            for p in range(Q):
                pair = passed([lattice[p, i, kz] for kz in range(NB)], p)
                for kz in range(NB):
                    ready[p, i, kz] = pair[kz]
        for d in range(owners):
            for t in range(NB):
                usual = final(d, t, 0)
                at_usual = seat(usual)
                at_below = seat(jnp.where(first, final(d, t, 1), usual))
                at_above = seat(jnp.where(last, final(d, t, 2), usual))
                for p in range(Q):
                    cx = VELOCITIES[p][0]
                    for i in range(planes):
                        kz, y = at_usual
                        if cx == 1 and i == planes - 1:
                            kz, y = at_above
                        if cx == -1 and i == 0:
                            kz, y = at_below
                        part, row = spot(p)
                        outs[d][part][pl.ds(row + i * PLANE + t, PLANE_ROWS, stride=NB), :] = ready[
                            p, i, kz, pl.ds(y, PLANE_ROWS), :
                        ]

    def crossing_kernel(*refs):
        whole, sloped, rest = cut(refs, (half, half))
        got = pieces(whole, (None,) * half, sloped, sizes_out)
        near, far, up, down = rest
        me, odd = position()
        for d in range(owners):
            place = dynamic_place(me ^ d, odd, owners)

            @pl.when(place == owners - 1)
            def _():
                for n, p in enumerate(UPWARD):
                    up[pl.ds(n * PLANE, PLANE), :] = got[d][1][
                        pl.ds(spot(p)[1] + share - PLANE, PLANE), :
                    ]

            @pl.when(place == 0)
            def _():
                for n, p in enumerate(DOWNWARD):
                    down[pl.ds(n * PLANE, PLANE), :] = got[d][1][
                        pl.ds(spot(p)[1], PLANE), :
                    ]

        for out in (up, down):
            out[pl.ds(faces, 4), :] = jnp.zeros((4, LANES), f32)
        send_sides(odd, up, down, near, far)

    def unpack_kernel(*refs):
        *groups, (main,) = cut(refs, (half,) * 3)
        got = pieces(*groups, sizes_out)
        me, odd = position()
        for d in range(owners):
            place = dynamic_place(me ^ d, odd, owners)
            here = pl.multiple_of(place * share, min(share, 8))
            for p in range(Q):
                cx = VELOCITIES[p][0]
                part, row = spot(p)
                main[p, pl.ds(8 + here + cx * PLANE, share), :] = got[d][part][
                    pl.ds(row, share), :
                ]

    def finish_kernel(main, near, far, out):
        below, above = sides(position()[1], near, far)
        for p in range(Q):
            out[pl.ds(p * WHOLE, WHOLE), :] = main[p, pl.ds(8, WHOLE), :]
        for n, p in enumerate(UPWARD):
            out[pl.ds(p * WHOLE, PLANE), :] = below[n * PLANE : (n + 1) * PLANE]
        for n, p in enumerate(DOWNWARD):
            out[pl.ds(p * WHOLE + WHOLE - PLANE, PLANE), :] = above[n * PLANE : (n + 1) * PLANE]

    def shape(*dims):
        return jax.ShapeDtypeStruct(dims, f32)

    def call(kernel, name, out_shape, inputs, cost, scratch=(), spec=VMEM_SPEC, limit=40):
        outs = jax.tree.map(lambda _: VMEM_SPEC, out_shape)
        return pl.pallas_call(
            kernel,
            out_shape=out_shape,
            in_specs=[spec] * len(inputs),
            out_specs=outs,
            scratch_shapes=list(scratch),
            compiler_params=pltpu.CompilerParams(vmem_limit_bytes=limit * 1024 * 1024),
            cost_estimate=pl.CostEstimate(flops=cost, bytes_accessed=cost, transcendentals=0),
            name=name,
        )(*inputs)

    def exchange(parts):
        done = []
        for n, (part, d) in enumerate(parts):
            if n >= FLIGHT:
                done[n - FLIGHT], part = lax.optimization_barrier((done[n - FLIGHT], part))
            done.append(lax.ppermute(part, "gx", [(g, g ^ d) for g in range(owners)]))
        return done

    def several(size, count=half):
        return (shape(size, LANES),) * count

    def hop(near, far):
        ahead = [(s + 1) % slabs if s % 2 == 0 else (s - 1) % slabs for s in range(slabs)]
        behind = [(s - 1) % slabs if s % 2 == 0 else (s + 1) % slabs for s in range(slabs)]
        return (
            lax.ppermute(near, "gy", list(enumerate(ahead))),
            lax.ppermute(far, "gy", list(enumerate(behind))),
        )

    def padded(count):
        return shape(count, 8 + WHOLE + 8, LANES)

    work = pltpu.VMEM((Q + 1, planes, NB, rows, LANES), f32)
    small, large = 100_000, 4_000_000

    def shards(populations, solid_mask, slot_blocks, swap_slots):
        tiles = B * B * B // LANES
        pops = populations[0].transpose(1, 0, 2).reshape(Q, NB, tiles, LANES)
        pops = pops.transpose(0, 2, 1, 3).reshape(Q, WHOLE, LANES)
        mask = solid_mask[0].reshape(NB, tiles, LANES).transpose(1, 0, 2).reshape(WHOLE, LANES)
        swaps = swap_slots[0, 0].T
        in_place = pl.BlockSpec(memory_space=pltpu.HBM)
        near, far, own = call(
            edge_kernel,
            "edge_planes",
            (shape(rows_hop, LANES), shape(rows_hop, LANES), shape(8, LANES)),
            (pops, mask, slot_blocks, swaps),
            small,
            (
                pltpu.VMEM((rows_hop, LANES), f32),
                pltpu.VMEM((rows_hop, LANES), f32),
                pltpu.VMEM((2, Q, 8, LANES), f32),
                pltpu.VMEM((2, 8, LANES), jnp.int32),
                pltpu.VMEM(slot_blocks.shape, jnp.int32),
                pltpu.VMEM(swaps.shape, jnp.int32),
                pltpu.SemaphoreType.DMA((6,)),
            ),
            in_place,
            62,
        )
        near, far = hop(near, far)
        post = call(
            collide_kernel,
            "first_collision",
            padded(Q + 1),
            (pops, mask),
            large,
        )
        parts = call(
            pack_kernel,
            "pack_planes",
            several(sum(sizes_in), owners),
            (post, own, near, far),
            large,
        )
        lines = [*range(1, 3), half, half + 1, *range(3, half), *range(half + 2, owners)]
        got = exchange([(parts[d], d) for d in lines])
        got = [parts[0]] + [got[lines.index(d)] for d in range(1, owners)]
        parts = call(
            middle_kernel,
            "second_step",
            several(sum(sizes_out)) + several(sizes_out[0]) + several(sizes_out[1]),
            got,
            large,
            (
                work,
                work,
                pltpu.SMEM((owners, 8, LANES), f32),
                pltpu.SemaphoreType.DMA((owners,)),
            ),
        )
        whole, level, sloped, _ = cut(parts, (half,) * 3)
        lines = [(whole[d], d) for d in range(1, half)]
        lines += [(part, d) for d, part in enumerate(sloped, half)]
        lines += [(part, d) for d, part in enumerate(level, half)]
        home = exchange(lines)
        own, sloped, level = whole[0], home[half - 1 :], home[half - 1 + half :]
        whole, sloped = [own] + home[: half - 1], sloped[:half]
        near, far = call(
            crossing_kernel,
            "crossing_planes",
            several(rows_hop, 2),
            (*whole, *sloped),
            small,
            (pltpu.VMEM((rows_hop, LANES), f32),) * 2,
        )
        near, far = hop(near, far)
        main = call(
            unpack_kernel, "unpack_planes", padded(Q), (*whole, *level, *sloped), large
        )
        out = call(
            finish_kernel, "finish", shape(Q * WHOLE, LANES), (main, near, far), small
        )
        out = out.reshape(Q, tiles, NB, LANES).transpose(0, 2, 1, 3)
        return out.reshape(Q, NB, B * B * B).transpose(1, 0, 2)[None]

    return shards


def solution(mesh):
    return jax.shard_map(
        build(mesh),
        mesh=mesh,
        in_specs=(
            P("gy", "gx", None, None),
            P("gy", "gx", None),
            P("gy", "gx"),
            P("gy", "gx", None, None),
        ),
        out_specs=P("gy", "gx", None, None),
        check_vma=False,
    )
```

```python
import jax
import jax.numpy as jnp
from jax import lax
from jax.experimental import pallas as pl
from jax.experimental.pallas import tpu as pltpu
from jax.sharding import PartitionSpec as P

B = 16
NB = 2
LANES = 128
PLANE_ROWS = B * B // LANES
PLANE = PLANE_ROWS * NB
WHOLE = B * PLANE

VELOCITIES = (
    (0, 0, 0),
    (1, 0, 0),
    (-1, 0, 0),
    (0, 1, 0),
    (0, -1, 0),
    (0, 0, 1),
    (0, 0, -1),
    (1, 1, 0),
    (-1, -1, 0),
    (1, -1, 0),
    (-1, 1, 0),
    (1, 0, 1),
    (-1, 0, -1),
    (1, 0, -1),
    (-1, 0, 1),
    (0, 1, 1),
    (0, -1, -1),
    (0, 1, -1),
    (0, -1, 1),
)
OPPOSITE = (0, 2, 1, 4, 3, 6, 5, 8, 7, 10, 9, 12, 11, 14, 13, 16, 15, 18, 17)
Q = len(VELOCITIES)
UPWARD = tuple(p for p in range(Q) if VELOCITIES[p][0] == 1)
DOWNWARD = tuple(p for p in range(Q) if VELOCITIES[p][0] == -1)

VMEM_SPEC = pl.BlockSpec(memory_space=pltpu.VMEM)


def dynamic_place(owner, odd_slab, owners):
    pair, core = owner // 2, owner % 2
    forward = 2 * pair + jnp.where(pair % 2 == 0, core, 1 - core)
    return jnp.where(odd_slab == 1, owners - 1 - forward, forward)


def collide(f, fluid):
    def pair(p):
        return f[p] + f[p + 1], f[p] - f[p + 1]

    sx, dx = pair(1)
    sy, dy = pair(3)
    sz, dz = pair(5)
    sxy_a, dxy_a = pair(7)
    sxy_b, dxy_b = pair(9)
    sxz_a, dxz_a = pair(11)
    sxz_b, dxz_b = pair(13)
    syz_a, dyz_a = pair(15)
    syz_b, dyz_b = pair(17)
    axy, bxy = sxy_a + sxy_b, sxy_a - sxy_b
    axz, bxz = sxz_a + sxz_b, sxz_a - sxz_b
    ayz, byz = syz_a + syz_b, syz_a - syz_b
    rho = f[0] + sx + sy + sz + axy + axz + ayz
    ox = dxy_a + dxy_b + dxz_a + dxz_b
    oy = dxy_a - dxy_b + dyz_a + dyz_b
    oz = dxz_a - dxz_b + dyz_a - dyz_b
    jx, jy, jz = dx + ox, dy + oy, dz + oz
    jxx, jyy, jzz = jx * jx, jy * jy, jz * jz
    base = rho * (1.3 / 9.0)
    wide = 1.3 / 3.0
    thin = 1.3 / 6.0
    axy1 = base - 0.3 * axy + wide * (jxx + jyy) - thin * jzz
    axz1 = base - 0.3 * axz + wide * (jxx + jzz) - thin * jyy
    ayz1 = base - 0.3 * ayz + wide * (jyy + jzz) - thin * jxx
    bxy1 = 1.25 * (jx * jy) - 0.25 * bxy
    bxz1 = 1.25 * (jx * jz) - 0.25 * bxz
    byz1 = 1.25 * (jy * jz) - 0.25 * byz
    third = rho * (1.25 / 3.0)
    sx1 = third + 1.25 * jxx - 0.25 * (sx + axy + axz) - axy1 - axz1
    sy1 = third + 1.25 * jyy - 0.25 * (sy + axy + ayz) - axy1 - ayz1
    sz1 = third + 1.25 * jzz - 0.25 * (sz + axz + ayz) - axz1 - ayz1
    rest = rho - sx1 - sy1 - sz1 - axy1 - axz1 - ayz1

    def split(even, odd):
        return 0.5 * (even + odd), 0.5 * (even - odd)

    def diagonal(a1, b1, d_a, d_b, j_first, j_second):
        plus = 0.25 * (j_first + j_second) - 0.5 * d_a
        minus = 0.25 * (j_first - j_second) - 0.5 * d_b
        return split(0.5 * (a1 + b1), plus) + split(0.5 * (a1 - b1), minus)

    relaxed = (
        (rest,)
        + split(sx1, 0.5 * ox)
        + split(sy1, 0.5 * oy)
        + split(sz1, 0.5 * oz)
        + diagonal(axy1, bxy1, dxy_a, dxy_b, jx, jy)
        + diagonal(axz1, bxz1, dxz_a, dxz_b, jx, jz)
        + diagonal(ayz1, byz1, dyz_a, dyz_b, jy, jz)
    )
    return [jnp.where(fluid, relaxed[p], f[OPPOSITE[p]]) for p in range(Q)]


def shift_y(value, step, lane):
    rows = value.shape[0]
    if step == 1:
        turned = pltpu.roll(value, B, 1)
        return jnp.where(lane < B, pltpu.roll(turned, 1, 0), turned)
    turned = pltpu.roll(value, LANES - B, 1)
    return jnp.where(lane >= LANES - B, pltpu.roll(turned, rows - 1, 0), turned)


def shift_z(value, other, step, lane):
    if step == 1:
        return jnp.where(
            lane % B == 0, pltpu.roll(other, LANES - (B - 1), 1), pltpu.roll(value, 1, 1)
        )
    return jnp.where(
        lane % B == B - 1, pltpu.roll(other, B - 1, 1), pltpu.roll(value, LANES - 1, 1)
    )


def build(mesh):
    owners, slabs = mesh.shape["gx"], mesh.shape["gy"]
    planes = B // owners
    share = planes * PLANE
    rows = owners * PLANE_ROWS
    head = (Q + 1) * share
    rows_in = head + 8
    rows_out = Q * share
    faces = len(UPWARD) * PLANE
    rows_hop = faces + 4
    f32 = jnp.float32

    half = owners // 2
    order = [0, 1, half, 2, *range(half + 1, owners), *range(3, half)]
    slot_of = [order.index(d) for d in range(owners)]

    def position():
        me = lax.axis_index("gx")
        return me, lax.axis_index("gy") % 2

    def sides(odd, near, far):
        return (
            jnp.where(odd == 1, near[...], far[...]),
            jnp.where(odd == 1, far[...], near[...]),
        )

    def send_sides(odd, up, down, near, far):
        near[...] = jnp.where(odd == 1, down[...], up[...])
        far[...] = jnp.where(odd == 1, up[...], down[...])

    def edge_kernel(pops, mask, slots, swaps, near, far, own, up, down, cells, solid, held, given, sem):
        ends = (WHOLE - 8, 0)
        copies = []
        for n, start in enumerate(ends):
            copies.append((pops.at[:, pl.ds(start, 8), :], cells.at[n]))
            copies.append((mask.at[pl.ds(start, 8), :], solid.at[n]))
        copies += [(slots, held), (swaps, given)]
        copies = [
            pltpu.make_async_copy(source, target, sem.at[n])
            for n, (source, target) in enumerate(copies)
        ]
        for copy in copies:
            copy.start()
        for copy in copies:
            copy.wait()
        own[...] = jnp.zeros((8, LANES), f32)
        own[0:1, 0:NB] = held[...].astype(f32)
        own[1:2, 0:3] = given[0:1].astype(f32)
        for n, (out, chosen, inside) in enumerate(((up, UPWARD, 8 - PLANE), (down, DOWNWARD, 0))):
            after = collide([cells[n, p] for p in range(Q)], solid[n] > 0)
            for m, p in enumerate(chosen):
                out[pl.ds(m * PLANE, PLANE), :] = after[p][inside : inside + PLANE]
            out[pl.ds(faces, 4), :] = own[0:4]
        send_sides(position()[1], up, down, near, far)

    def collide_kernel(cells, solid, post):
        for start in range(0, WHOLE, 8):
            here = pl.ds(start, 8)
            after = collide([cells[p, here, :] for p in range(Q)], solid[here, :] > 0)
            for p in range(Q):
                post[p, pl.ds(8 + start, 8), :] = after[p]
            post[Q, pl.ds(8 + start, 8), :] = solid[here, :].astype(f32)

    def pack_kernel(post, own, near, far, *outs):
        me, odd = position()
        below, above = sides(odd, near, far)
        for d in range(owners):
            out = outs[slot_of[d]]
            place = dynamic_place(me ^ d, odd, owners)
            here = pl.multiple_of(place * share, min(share, 8))
            for p in range(Q + 1):
                cx = VELOCITIES[p][0] if p < Q else 0
                out[pl.ds(p * share, share), :] = post[p, pl.ds(8 + here - cx * PLANE, share), :]
            out[pl.ds(head, 2), :] = own[0:2]
            out[pl.ds(head + 2, 2), :] = below[faces : faces + 2]
            out[pl.ds(head + 4, 2), :] = above[faces : faces + 2]
            out[pl.ds(head + 6, 2), :] = own[2:4]

            @pl.when(place == 0)
            def _():
                for n, p in enumerate(UPWARD):
                    out[pl.ds(p * share, PLANE), :] = below[n * PLANE : (n + 1) * PLANE]

            @pl.when(place == owners - 1)
            def _():
                for n, p in enumerate(DOWNWARD):
                    out[pl.ds(p * share + share - PLANE, PLANE), :] = above[
                        n * PLANE : (n + 1) * PLANE
                    ]

    def middle_kernel(*refs):
        got = [refs[slot_of[d]] for d in range(owners)]
        outs = [refs[owners + slot_of[d]] for d in range(owners)]
        lattice, ready, table, sem = refs[2 * owners :]
        me, odd = position()
        place = dynamic_place(me, odd, owners)
        first, last = place == 0, place == owners - 1
        copies = [
            pltpu.make_async_copy(got[d].at[pl.ds(head, 8), :], table.at[d], sem.at[d])
            for d in range(owners)
        ]
        for copy in copies:
            copy.start()
        for copy in copies:
            copy.wait()

        def number(d, row, column):
            return table[d, row, column].astype(jnp.int32)

        def held(d, t, which):
            return number(d, 2 * which, t)

        def final(d, t, which):
            def lead(e, r):
                return number(d ^ e, 2 * which + 1, r)

            flip = lead(0, 2) + lead(4, 2) + lead(4, 1) + lead(6, 1) + lead(6, 0) + lead(7, 0)
            one, two = held(d ^ 7, t, which), held(d ^ 7, 1 - t, which)
            return jnp.where(flip % 2 == 1, two, one)

        def seat(b):
            return b % NB, pl.multiple_of((b // NB) * PLANE_ROWS, PLANE_ROWS)

        for d in range(owners):
            for t in range(NB):
                usual = held(d, t, 0)
                at_usual = seat(usual)
                at_below = seat(jnp.where(first, held(d, t, 1), usual))
                at_above = seat(jnp.where(last, held(d, t, 2), usual))
                for p in range(Q + 1):
                    cx = VELOCITIES[p][0] if p < Q else 0
                    for i in range(planes):
                        kz, y = at_usual
                        if cx == 1 and i == 0:
                            kz, y = at_below
                        if cx == -1 and i == planes - 1:
                            kz, y = at_above
                        lattice[p, i, kz, pl.ds(y, PLANE_ROWS), :] = got[d][
                            pl.ds(p * share + i * PLANE + t, PLANE_ROWS, stride=NB), :
                        ]
        lane = lax.broadcasted_iota(jnp.int32, (rows, LANES), 1)

        def passed(pair, p):
            cx, cy, cz = VELOCITIES[p]
            if cy:
                pair = [shift_y(value, cy, lane) for value in pair]
            if cz:
                pair = [shift_z(pair[kz], pair[1 - kz], cz, lane) for kz in range(NB)]
            return pair

        for i in range(planes):
            for p in range(Q):
                pair = passed([lattice[p, i, kz] for kz in range(NB)], p)
                for kz in range(NB):
                    ready[p, i, kz] = pair[kz]
            for kz in range(NB):
                after = collide([ready[p, i, kz] for p in range(Q)], lattice[Q, i, kz] > 0.5)
                for p in range(Q):
                    lattice[p, i, kz] = after[p]
            for p in range(Q):
                pair = passed([lattice[p, i, kz] for kz in range(NB)], p)
                for kz in range(NB):
                    ready[p, i, kz] = pair[kz]
        for d in range(owners):
            for t in range(NB):
                usual = final(d, t, 0)
                at_usual = seat(usual)
                at_below = seat(jnp.where(first, final(d, t, 1), usual))
                at_above = seat(jnp.where(last, final(d, t, 2), usual))
                for p in range(Q):
                    cx = VELOCITIES[p][0]
                    for i in range(planes):
                        kz, y = at_usual
                        if cx == 1 and i == planes - 1:
                            kz, y = at_above
                        if cx == -1 and i == 0:
                            kz, y = at_below
                        outs[d][pl.ds(p * share + i * PLANE + t, PLANE_ROWS, stride=NB), :] = ready[
                            p, i, kz, pl.ds(y, PLANE_ROWS), :
                        ]

    def crossing_kernel(*refs):
        got = [refs[slot_of[d]] for d in range(owners)]
        near, far, up, down = refs[owners:]
        me, odd = position()
        for d in range(owners):
            place = dynamic_place(me ^ d, odd, owners)

            @pl.when(place == owners - 1)
            def _():
                for n, p in enumerate(UPWARD):
                    up[pl.ds(n * PLANE, PLANE), :] = got[d][
                        pl.ds(p * share + share - PLANE, PLANE), :
                    ]

            @pl.when(place == 0)
            def _():
                for n, p in enumerate(DOWNWARD):
                    down[pl.ds(n * PLANE, PLANE), :] = got[d][pl.ds(p * share, PLANE), :]

        for out in (up, down):
            out[pl.ds(faces, 4), :] = jnp.zeros((4, LANES), f32)
        send_sides(odd, up, down, near, far)

    def unpack_kernel(*refs):
        got, main = [refs[slot_of[d]] for d in range(owners)], refs[owners]
        me, odd = position()
        for d in range(owners):
            place = dynamic_place(me ^ d, odd, owners)
            here = pl.multiple_of(place * share, min(share, 8))
            for p in range(Q):
                cx = VELOCITIES[p][0]
                main[p, pl.ds(8 + here + cx * PLANE, share), :] = got[d][
                    pl.ds(p * share, share), :
                ]

    def finish_kernel(main, near, far, out):
        below, above = sides(position()[1], near, far)
        for p in range(Q):
            out[pl.ds(p * WHOLE, WHOLE), :] = main[p, pl.ds(8, WHOLE), :]
        for n, p in enumerate(UPWARD):
            out[pl.ds(p * WHOLE, PLANE), :] = below[n * PLANE : (n + 1) * PLANE]
        for n, p in enumerate(DOWNWARD):
            out[pl.ds(p * WHOLE + WHOLE - PLANE, PLANE), :] = above[n * PLANE : (n + 1) * PLANE]

    def shape(*dims):
        return jax.ShapeDtypeStruct(dims, f32)

    def call(kernel, name, out_shape, inputs, cost, scratch=(), spec=VMEM_SPEC, limit=40):
        outs = jax.tree.map(lambda _: VMEM_SPEC, out_shape)
        return pl.pallas_call(
            kernel,
            out_shape=out_shape,
            in_specs=[spec] * len(inputs),
            out_specs=outs,
            scratch_shapes=list(scratch),
            compiler_params=pltpu.CompilerParams(vmem_limit_bytes=limit * 1024 * 1024),
            cost_estimate=pl.CostEstimate(flops=cost, bytes_accessed=cost, transcendentals=0),
            name=name,
        )(*inputs)

    def exchange(parts):
        return [parts[0]] + [
            lax.ppermute(parts[n], "gx", [(g, g ^ order[n]) for g in range(owners)])
            for n in range(1, owners)
        ]

    def hop(near, far):
        ahead = [(s + 1) % slabs if s % 2 == 0 else (s - 1) % slabs for s in range(slabs)]
        behind = [(s - 1) % slabs if s % 2 == 0 else (s + 1) % slabs for s in range(slabs)]
        return (
            lax.ppermute(near, "gy", list(enumerate(ahead))),
            lax.ppermute(far, "gy", list(enumerate(behind))),
        )

    def padded(count):
        return shape(count, 8 + WHOLE + 8, LANES)

    work = pltpu.VMEM((Q + 1, planes, NB, rows, LANES), f32)
    small, large = 100_000, 4_000_000

    def shards(populations, solid_mask, slot_blocks, swap_slots):
        tiles = B * B * B // LANES
        pops = populations[0].transpose(1, 0, 2).reshape(Q, NB, tiles, LANES)
        pops = pops.transpose(0, 2, 1, 3).reshape(Q, WHOLE, LANES)
        mask = solid_mask[0].reshape(NB, tiles, LANES).transpose(1, 0, 2).reshape(WHOLE, LANES)
        swaps = swap_slots[0, 0].T
        in_place = pl.BlockSpec(memory_space=pltpu.HBM)
        near, far, own = call(
            edge_kernel,
            "edge_planes",
            (shape(rows_hop, LANES), shape(rows_hop, LANES), shape(8, LANES)),
            (pops, mask, slot_blocks, swaps),
            small,
            (
                pltpu.VMEM((rows_hop, LANES), f32),
                pltpu.VMEM((rows_hop, LANES), f32),
                pltpu.VMEM((2, Q, 8, LANES), f32),
                pltpu.VMEM((2, 8, LANES), jnp.int32),
                pltpu.VMEM(slot_blocks.shape, jnp.int32),
                pltpu.VMEM(swaps.shape, jnp.int32),
                pltpu.SemaphoreType.DMA((6,)),
            ),
            in_place,
            62,
        )
        near, far = hop(near, far)
        post = call(
            collide_kernel,
            "first_collision",
            padded(Q + 1),
            (pops, mask),
            large,
        )
        parts = call(
            pack_kernel,
            "pack_planes",
            (shape(rows_in, LANES),) * owners,
            (post, own, near, far),
            large,
        )
        got = exchange(parts)
        parts = call(
            middle_kernel,
            "second_step",
            (shape(rows_out, LANES),) * owners,
            got,
            large,
            (
                work,
                work,
                pltpu.SMEM((owners, 8, LANES), f32),
                pltpu.SemaphoreType.DMA((owners,)),
            ),
        )
        home = exchange(parts)
        near, far = call(
            crossing_kernel,
            "crossing_planes",
            (shape(rows_hop, LANES),) * 2,
            home,
            small,
            (pltpu.VMEM((rows_hop, LANES), f32),) * 2,
        )
        near, far = hop(near, far)
        main = call(unpack_kernel, "unpack_planes", padded(Q), home, large)
        out = call(
            finish_kernel, "finish", shape(Q * WHOLE, LANES), (main, near, far), small
        )
        out = out.reshape(Q, tiles, NB, LANES).transpose(0, 2, 1, 3)
        return out.reshape(Q, NB, B * B * B).transpose(1, 0, 2)[None]

    return shards


def solution(mesh):
    return jax.shard_map(
        build(mesh),
        mesh=mesh,
        in_specs=(
            P("gy", "gx", None, None),
            P("gy", "gx", None),
            P("gy", "gx"),
            P("gy", "gx", None, None),
        ),
        out_specs=P("gy", "gx", None, None),
        check_vma=False,
    )
```

```python
import jax
import jax.numpy as jnp
from jax import lax
from jax.experimental import pallas as pl
from jax.experimental.pallas import tpu as pltpu
from jax.sharding import PartitionSpec as P

B = 16
NB = 2
LANES = 128
PLANE_ROWS = B * B // LANES
PLANE = PLANE_ROWS * NB
WHOLE = B * PLANE

VELOCITIES = (
    (0, 0, 0),
    (1, 0, 0),
    (-1, 0, 0),
    (0, 1, 0),
    (0, -1, 0),
    (0, 0, 1),
    (0, 0, -1),
    (1, 1, 0),
    (-1, -1, 0),
    (1, -1, 0),
    (-1, 1, 0),
    (1, 0, 1),
    (-1, 0, -1),
    (1, 0, -1),
    (-1, 0, 1),
    (0, 1, 1),
    (0, -1, -1),
    (0, 1, -1),
    (0, -1, 1),
)
OPPOSITE = (0, 2, 1, 4, 3, 6, 5, 8, 7, 10, 9, 12, 11, 14, 13, 16, 15, 18, 17)
Q = len(VELOCITIES)
UPWARD = tuple(p for p in range(Q) if VELOCITIES[p][0] == 1)
DOWNWARD = tuple(p for p in range(Q) if VELOCITIES[p][0] == -1)

VMEM_SPEC = pl.BlockSpec(memory_space=pltpu.VMEM)


def dynamic_place(owner, odd_slab, owners):
    pair, core = owner // 2, owner % 2
    forward = 2 * pair + jnp.where(pair % 2 == 0, core, 1 - core)
    return jnp.where(odd_slab == 1, owners - 1 - forward, forward)


def collide(f, fluid):
    def pair(p):
        return f[p] + f[p + 1], f[p] - f[p + 1]

    sx, dx = pair(1)
    sy, dy = pair(3)
    sz, dz = pair(5)
    sxy_a, dxy_a = pair(7)
    sxy_b, dxy_b = pair(9)
    sxz_a, dxz_a = pair(11)
    sxz_b, dxz_b = pair(13)
    syz_a, dyz_a = pair(15)
    syz_b, dyz_b = pair(17)
    axy, bxy = sxy_a + sxy_b, sxy_a - sxy_b
    axz, bxz = sxz_a + sxz_b, sxz_a - sxz_b
    ayz, byz = syz_a + syz_b, syz_a - syz_b
    rho = f[0] + sx + sy + sz + axy + axz + ayz
    ox = dxy_a + dxy_b + dxz_a + dxz_b
    oy = dxy_a - dxy_b + dyz_a + dyz_b
    oz = dxz_a - dxz_b + dyz_a - dyz_b
    jx, jy, jz = dx + ox, dy + oy, dz + oz
    jxx, jyy, jzz = jx * jx, jy * jy, jz * jz
    base = rho * (1.3 / 9.0)
    wide = 1.3 / 3.0
    thin = 1.3 / 6.0
    axy1 = base - 0.3 * axy + wide * (jxx + jyy) - thin * jzz
    axz1 = base - 0.3 * axz + wide * (jxx + jzz) - thin * jyy
    ayz1 = base - 0.3 * ayz + wide * (jyy + jzz) - thin * jxx
    bxy1 = 1.25 * (jx * jy) - 0.25 * bxy
    bxz1 = 1.25 * (jx * jz) - 0.25 * bxz
    byz1 = 1.25 * (jy * jz) - 0.25 * byz
    third = rho * (1.25 / 3.0)
    sx1 = third + 1.25 * jxx - 0.25 * (sx + axy + axz) - axy1 - axz1
    sy1 = third + 1.25 * jyy - 0.25 * (sy + axy + ayz) - axy1 - ayz1
    sz1 = third + 1.25 * jzz - 0.25 * (sz + axz + ayz) - axz1 - ayz1
    rest = rho - sx1 - sy1 - sz1 - axy1 - axz1 - ayz1

    def split(even, odd):
        return 0.5 * (even + odd), 0.5 * (even - odd)

    def diagonal(a1, b1, d_a, d_b, j_first, j_second):
        plus = 0.25 * (j_first + j_second) - 0.5 * d_a
        minus = 0.25 * (j_first - j_second) - 0.5 * d_b
        return split(0.5 * (a1 + b1), plus) + split(0.5 * (a1 - b1), minus)

    relaxed = (
        (rest,)
        + split(sx1, 0.5 * ox)
        + split(sy1, 0.5 * oy)
        + split(sz1, 0.5 * oz)
        + diagonal(axy1, bxy1, dxy_a, dxy_b, jx, jy)
        + diagonal(axz1, bxz1, dxz_a, dxz_b, jx, jz)
        + diagonal(ayz1, byz1, dyz_a, dyz_b, jy, jz)
    )
    return [jnp.where(fluid, relaxed[p], f[OPPOSITE[p]]) for p in range(Q)]


def shift_y(value, step, lane, row, block):
    rows = value.shape[0]
    turned = pltpu.roll(value, B if step == 1 else LANES - B, 1)
    if step == 1:
        edge, start = lane < B, row % PLANE_ROWS == 0
        near, far = pltpu.roll(turned, 1, 0), pltpu.roll(turned, block - 1, 0)
    else:
        edge, start = lane >= LANES - B, row % PLANE_ROWS == PLANE_ROWS - 1
        near, far = pltpu.roll(turned, rows - 1, 0), pltpu.roll(turned, rows - block + 1, 0)
    return jnp.where(edge, jnp.where(start, far, near), turned)


def shift_z(value, other, step, lane):
    if step == 1:
        return jnp.where(
            lane % B == 0, pltpu.roll(other, LANES - (B - 1), 1), pltpu.roll(value, 1, 1)
        )
    return jnp.where(
        lane % B == B - 1, pltpu.roll(other, B - 1, 1), pltpu.roll(value, LANES - 1, 1)
    )


def build(mesh):
    owners, slabs = mesh.shape["gx"], mesh.shape["gy"]
    planes = B // owners
    share = planes * PLANE
    block = planes * PLANE_ROWS
    rows = owners * block
    head = (Q + 1) * share
    rows_in = head + 8
    rows_out = Q * share
    faces = len(UPWARD) * PLANE
    rows_hop = faces + 4
    f32 = jnp.float32

    half = owners // 2
    order = [0, half, 1, half + 1, 2, *range(half + 2, owners), *range(3, half)]
    slot_of = [order.index(d) for d in range(owners)]

    def position():
        me = lax.axis_index("gx")
        return me, lax.axis_index("gy") % 2

    def sides(odd, near, far):
        return (
            jnp.where(odd == 1, near[...], far[...]),
            jnp.where(odd == 1, far[...], near[...]),
        )

    def send_sides(odd, up, down, near, far):
        near[...] = jnp.where(odd == 1, down[...], up[...])
        far[...] = jnp.where(odd == 1, up[...], down[...])

    def edge_kernel(pops, mask, slots, swaps, near, far, own, up, down, cells, solid, held, given, sem):
        ends = (WHOLE - 8, 0)
        copies = []
        for n, start in enumerate(ends):
            copies.append((pops.at[:, pl.ds(start, 8), :], cells.at[n]))
            copies.append((mask.at[pl.ds(start, 8), :], solid.at[n]))
        copies += [(slots, held), (swaps, given)]
        copies = [
            pltpu.make_async_copy(source, target, sem.at[n])
            for n, (source, target) in enumerate(copies)
        ]
        for copy in copies:
            copy.start()
        for copy in copies:
            copy.wait()
        own[...] = jnp.zeros((8, LANES), f32)
        own[0:1, 0:NB] = held[...].astype(f32)
        own[1:2, 0:3] = given[0:1].astype(f32)
        for n, (out, chosen, inside) in enumerate(((up, UPWARD, 8 - PLANE), (down, DOWNWARD, 0))):
            after = collide([cells[n, p] for p in range(Q)], solid[n] > 0)
            for m, p in enumerate(chosen):
                out[pl.ds(m * PLANE, PLANE), :] = after[p][inside : inside + PLANE]
            out[pl.ds(faces, 4), :] = own[0:4]
        send_sides(position()[1], up, down, near, far)

    def collide_kernel(cells, solid, post):
        for start in range(0, WHOLE, 8):
            here = pl.ds(start, 8)
            after = collide([cells[p, here, :] for p in range(Q)], solid[here, :] > 0)
            for p in range(Q):
                post[p, pl.ds(8 + start, 8), :] = after[p]
            post[Q, pl.ds(8 + start, 8), :] = solid[here, :].astype(f32)

    def pack_kernel(post, own, near, far, *outs):
        me, odd = position()
        below, above = sides(odd, near, far)
        for d in range(owners):
            out = outs[slot_of[d]]
            place = dynamic_place(me ^ d, odd, owners)
            here = pl.multiple_of(place * share, min(share, 8))
            for p in range(Q + 1):
                cx = VELOCITIES[p][0] if p < Q else 0
                out[pl.ds(p * share, share), :] = post[p, pl.ds(8 + here - cx * PLANE, share), :]
            out[pl.ds(head, 2), :] = own[0:2]
            out[pl.ds(head + 2, 2), :] = below[faces : faces + 2]
            out[pl.ds(head + 4, 2), :] = above[faces : faces + 2]
            out[pl.ds(head + 6, 2), :] = own[2:4]

            @pl.when(place == 0)
            def _():
                for n, p in enumerate(UPWARD):
                    out[pl.ds(p * share, PLANE), :] = below[n * PLANE : (n + 1) * PLANE]

            @pl.when(place == owners - 1)
            def _():
                for n, p in enumerate(DOWNWARD):
                    out[pl.ds(p * share + share - PLANE, PLANE), :] = above[
                        n * PLANE : (n + 1) * PLANE
                    ]

    def middle_kernel(*refs):
        got = [refs[slot_of[d]] for d in range(owners)]
        outs = [refs[owners + slot_of[d]] for d in range(owners)]
        lattice, ready, table, sem = refs[2 * owners :]
        me, odd = position()
        place = dynamic_place(me, odd, owners)
        first, last = place == 0, place == owners - 1
        copies = [
            pltpu.make_async_copy(got[d].at[pl.ds(head, 8), :], table.at[d], sem.at[d])
            for d in range(owners)
        ]
        for copy in copies:
            copy.start()
        for copy in copies:
            copy.wait()

        def number(d, row, column):
            return table[d, row, column].astype(jnp.int32)

        other = jnp.where(first, 1, jnp.where(last, 2, 0))

        def seats(blocks):
            return [(b % NB, pl.multiple_of((b // NB) * block, block)) for b in blocks]

        def held(d, which):
            return [number(d, 2 * which, t) for t in range(NB)]

        def final(d, which):
            def lead(e, r):
                return number(d ^ e, 2 * which + 1, r)

            flip = lead(0, 2) + lead(4, 2) + lead(4, 1) + lead(6, 1) + lead(6, 0) + lead(7, 0)
            one, two = held(d ^ 7, which)
            crossed = flip % 2 == 1
            return [jnp.where(crossed, two, one), jnp.where(crossed, one, two)]

        for d in range(owners):
            for t, (kz, y) in enumerate(seats(held(d, 0))):
                for p in range(Q + 1):
                    lattice[p, kz, pl.ds(y, block), :] = got[d][
                        pl.ds(p * share + t, block, stride=NB), :
                    ]

        def bring(chosen, i):
            for d in range(owners):
                for t, (kz, y) in enumerate(seats(held(d, other))):
                    for p in chosen:
                        lattice[p, kz, pl.ds(y + i * PLANE_ROWS, PLANE_ROWS), :] = got[d][
                            pl.ds(p * share + i * PLANE + t, PLANE_ROWS, stride=NB), :
                        ]

        @pl.when(first)
        def _():
            bring(UPWARD, 0)

        @pl.when(last)
        def _():
            bring(DOWNWARD, planes - 1)

        lane = lax.broadcasted_iota(jnp.int32, (rows, LANES), 1)
        row = lax.broadcasted_iota(jnp.int32, (rows, LANES), 0)

        def passed(pair, p):
            cx, cy, cz = VELOCITIES[p]
            if cy:
                pair = [shift_y(value, cy, lane, row, block) for value in pair]
            if cz:
                pair = [shift_z(pair[kz], pair[1 - kz], cz, lane) for kz in range(NB)]
            return pair

        for p in range(Q):
            pair = passed([lattice[p, kz] for kz in range(NB)], p)
            for kz in range(NB):
                ready[p, kz] = pair[kz]
        for kz in range(NB):
            for start in range(0, rows, 16):
                here = pl.ds(start, 16)
                after = collide(
                    [ready[p, kz, here, :] for p in range(Q)], lattice[Q, kz, here, :] > 0.5
                )
                for p in range(Q):
                    lattice[p, kz, here, :] = after[p]
        for p in range(Q):
            pair = passed([lattice[p, kz] for kz in range(NB)], p)
            for kz in range(NB):
                ready[p, kz] = pair[kz]
        for d in range(owners):
            for t, (kz, y) in enumerate(seats(final(d, 0))):
                for p in range(Q):
                    outs[d][pl.ds(p * share + t, block, stride=NB), :] = ready[
                        p, kz, pl.ds(y, block), :
                    ]

        def bring_back(chosen, i):
            for d in range(owners):
                for t, (kz, y) in enumerate(seats(final(d, other))):
                    for p in chosen:
                        outs[d][
                            pl.ds(p * share + i * PLANE + t, PLANE_ROWS, stride=NB), :
                        ] = ready[p, kz, pl.ds(y + i * PLANE_ROWS, PLANE_ROWS), :]

        @pl.when(last)
        def _():
            bring_back(UPWARD, planes - 1)

        @pl.when(first)
        def _():
            bring_back(DOWNWARD, 0)

    def crossing_kernel(*refs):
        got = [refs[slot_of[d]] for d in range(owners)]
        near, far, up, down = refs[owners:]
        me, odd = position()
        for d in range(owners):
            place = dynamic_place(me ^ d, odd, owners)

            @pl.when(place == owners - 1)
            def _():
                for n, p in enumerate(UPWARD):
                    up[pl.ds(n * PLANE, PLANE), :] = got[d][
                        pl.ds(p * share + share - PLANE, PLANE), :
                    ]

            @pl.when(place == 0)
            def _():
                for n, p in enumerate(DOWNWARD):
                    down[pl.ds(n * PLANE, PLANE), :] = got[d][pl.ds(p * share, PLANE), :]

        for out in (up, down):
            out[pl.ds(faces, 4), :] = jnp.zeros((4, LANES), f32)
        send_sides(odd, up, down, near, far)

    def unpack_kernel(*refs):
        got, main = [refs[slot_of[d]] for d in range(owners)], refs[owners]
        me, odd = position()
        for d in range(owners):
            place = dynamic_place(me ^ d, odd, owners)
            here = pl.multiple_of(place * share, min(share, 8))
            for p in range(Q):
                cx = VELOCITIES[p][0]
                main[p, pl.ds(8 + here + cx * PLANE, share), :] = got[d][
                    pl.ds(p * share, share), :
                ]

    def finish_kernel(main, near, far, out):
        below, above = sides(position()[1], near, far)
        for p in range(Q):
            out[pl.ds(p * WHOLE, WHOLE), :] = main[p, pl.ds(8, WHOLE), :]
        for n, p in enumerate(UPWARD):
            out[pl.ds(p * WHOLE, PLANE), :] = below[n * PLANE : (n + 1) * PLANE]
        for n, p in enumerate(DOWNWARD):
            out[pl.ds(p * WHOLE + WHOLE - PLANE, PLANE), :] = above[n * PLANE : (n + 1) * PLANE]

    def shape(*dims):
        return jax.ShapeDtypeStruct(dims, f32)

    def call(kernel, name, out_shape, inputs, cost, scratch=(), spec=VMEM_SPEC, limit=40):
        outs = jax.tree.map(lambda _: VMEM_SPEC, out_shape)
        return pl.pallas_call(
            kernel,
            out_shape=out_shape,
            in_specs=[spec] * len(inputs),
            out_specs=outs,
            scratch_shapes=list(scratch),
            compiler_params=pltpu.CompilerParams(vmem_limit_bytes=limit * 1024 * 1024),
            cost_estimate=pl.CostEstimate(flops=cost, bytes_accessed=cost, transcendentals=0),
            name=name,
        )(*inputs)

    def exchange(parts):
        return [parts[0]] + [
            lax.ppermute(parts[n], "gx", [(g, g ^ order[n]) for g in range(owners)])
            for n in range(1, owners)
        ]

    def hop(near, far):
        ahead = [(s + 1) % slabs if s % 2 == 0 else (s - 1) % slabs for s in range(slabs)]
        behind = [(s - 1) % slabs if s % 2 == 0 else (s + 1) % slabs for s in range(slabs)]
        return (
            lax.ppermute(near, "gy", list(enumerate(ahead))),
            lax.ppermute(far, "gy", list(enumerate(behind))),
        )

    def padded(count):
        return shape(count, 8 + WHOLE + 8, LANES)

    work = pltpu.VMEM((Q + 1, NB, rows, LANES), f32)
    small, large = 100_000, 4_000_000

    def shards(populations, solid_mask, slot_blocks, swap_slots):
        tiles = B * B * B // LANES
        pops = populations[0].transpose(1, 0, 2).reshape(Q, NB, tiles, LANES)
        pops = pops.transpose(0, 2, 1, 3).reshape(Q, WHOLE, LANES)
        mask = solid_mask[0].reshape(NB, tiles, LANES).transpose(1, 0, 2).reshape(WHOLE, LANES)
        swaps = swap_slots[0, 0].T
        in_place = pl.BlockSpec(memory_space=pltpu.HBM)
        near, far, own = call(
            edge_kernel,
            "edge_planes",
            (shape(rows_hop, LANES), shape(rows_hop, LANES), shape(8, LANES)),
            (pops, mask, slot_blocks, swaps),
            small,
            (
                pltpu.VMEM((rows_hop, LANES), f32),
                pltpu.VMEM((rows_hop, LANES), f32),
                pltpu.VMEM((2, Q, 8, LANES), f32),
                pltpu.VMEM((2, 8, LANES), jnp.int32),
                pltpu.VMEM(slot_blocks.shape, jnp.int32),
                pltpu.VMEM(swaps.shape, jnp.int32),
                pltpu.SemaphoreType.DMA((6,)),
            ),
            in_place,
            62,
        )
        near, far = hop(near, far)
        post = call(
            collide_kernel,
            "first_collision",
            padded(Q + 1),
            (pops, mask),
            large,
        )
        parts = call(
            pack_kernel,
            "pack_planes",
            (shape(rows_in, LANES),) * owners,
            (post, own, near, far),
            large,
        )
        got = exchange(parts)
        parts = call(
            middle_kernel,
            "second_step",
            (shape(rows_out, LANES),) * owners,
            got,
            large,
            (
                work,
                work,
                pltpu.SMEM((owners, 8, LANES), f32),
                pltpu.SemaphoreType.DMA((owners,)),
            ),
        )
        home = exchange(parts)
        near, far = call(
            crossing_kernel,
            "crossing_planes",
            (shape(rows_hop, LANES),) * 2,
            home,
            small,
            (pltpu.VMEM((rows_hop, LANES), f32),) * 2,
        )
        near, far = hop(near, far)
        main = call(unpack_kernel, "unpack_planes", padded(Q), home, large)
        out = call(
            finish_kernel, "finish", shape(Q * WHOLE, LANES), (main, near, far), small
        )
        out = out.reshape(Q, tiles, NB, LANES).transpose(0, 2, 1, 3)
        return out.reshape(Q, NB, B * B * B).transpose(1, 0, 2)[None]

    return shards


def solution(mesh):
    return jax.shard_map(
        build(mesh),
        mesh=mesh,
        in_specs=(
            P("gy", "gx", None, None),
            P("gy", "gx", None),
            P("gy", "gx"),
            P("gy", "gx", None, None),
        ),
        out_specs=P("gy", "gx", None, None),
        check_vma=False,
    )
```

```python
import jax
import jax.numpy as jnp
from jax import lax
from jax.experimental import pallas as pl
from jax.experimental.pallas import tpu as pltpu
from jax.sharding import PartitionSpec as P

B = 16
NB = 2
LANES = 128
PLANE_ROWS = B * B // LANES
PLANE = PLANE_ROWS * NB
WHOLE = B * PLANE

VELOCITIES = (
    (0, 0, 0),
    (1, 0, 0),
    (-1, 0, 0),
    (0, 1, 0),
    (0, -1, 0),
    (0, 0, 1),
    (0, 0, -1),
    (1, 1, 0),
    (-1, -1, 0),
    (1, -1, 0),
    (-1, 1, 0),
    (1, 0, 1),
    (-1, 0, -1),
    (1, 0, -1),
    (-1, 0, 1),
    (0, 1, 1),
    (0, -1, -1),
    (0, 1, -1),
    (0, -1, 1),
)
OPPOSITE = (0, 2, 1, 4, 3, 6, 5, 8, 7, 10, 9, 12, 11, 14, 13, 16, 15, 18, 17)
Q = len(VELOCITIES)
UPWARD = tuple(p for p in range(Q) if VELOCITIES[p][0] == 1)
DOWNWARD = tuple(p for p in range(Q) if VELOCITIES[p][0] == -1)

VMEM_SPEC = pl.BlockSpec(memory_space=pltpu.VMEM)


def dynamic_place(owner, odd_slab, owners):
    pair, core = owner // 2, owner % 2
    forward = 2 * pair + jnp.where(pair % 2 == 0, core, 1 - core)
    return jnp.where(odd_slab == 1, owners - 1 - forward, forward)


def collide(f, fluid):
    def pair(p):
        return f[p] + f[p + 1], f[p] - f[p + 1]

    sx, dx = pair(1)
    sy, dy = pair(3)
    sz, dz = pair(5)
    sxy_a, dxy_a = pair(7)
    sxy_b, dxy_b = pair(9)
    sxz_a, dxz_a = pair(11)
    sxz_b, dxz_b = pair(13)
    syz_a, dyz_a = pair(15)
    syz_b, dyz_b = pair(17)
    axy, bxy = sxy_a + sxy_b, sxy_a - sxy_b
    axz, bxz = sxz_a + sxz_b, sxz_a - sxz_b
    ayz, byz = syz_a + syz_b, syz_a - syz_b
    rho = f[0] + sx + sy + sz + axy + axz + ayz
    ox = dxy_a + dxy_b + dxz_a + dxz_b
    oy = dxy_a - dxy_b + dyz_a + dyz_b
    oz = dxz_a - dxz_b + dyz_a - dyz_b
    jx, jy, jz = dx + ox, dy + oy, dz + oz
    jxx, jyy, jzz = jx * jx, jy * jy, jz * jz
    base = rho * (1.3 / 9.0)
    wide = 1.3 / 3.0
    thin = 1.3 / 6.0
    axy1 = base - 0.3 * axy + wide * (jxx + jyy) - thin * jzz
    axz1 = base - 0.3 * axz + wide * (jxx + jzz) - thin * jyy
    ayz1 = base - 0.3 * ayz + wide * (jyy + jzz) - thin * jxx
    bxy1 = 1.25 * (jx * jy) - 0.25 * bxy
    bxz1 = 1.25 * (jx * jz) - 0.25 * bxz
    byz1 = 1.25 * (jy * jz) - 0.25 * byz
    third = rho * (1.25 / 3.0)
    sx1 = third + 1.25 * jxx - 0.25 * (sx + axy + axz) - axy1 - axz1
    sy1 = third + 1.25 * jyy - 0.25 * (sy + axy + ayz) - axy1 - ayz1
    sz1 = third + 1.25 * jzz - 0.25 * (sz + axz + ayz) - axz1 - ayz1
    rest = rho - sx1 - sy1 - sz1 - axy1 - axz1 - ayz1

    def split(even, odd):
        return 0.5 * (even + odd), 0.5 * (even - odd)

    def diagonal(a1, b1, d_a, d_b, j_first, j_second):
        plus = 0.25 * (j_first + j_second) - 0.5 * d_a
        minus = 0.25 * (j_first - j_second) - 0.5 * d_b
        return split(0.5 * (a1 + b1), plus) + split(0.5 * (a1 - b1), minus)

    relaxed = (
        (rest,)
        + split(sx1, 0.5 * ox)
        + split(sy1, 0.5 * oy)
        + split(sz1, 0.5 * oz)
        + diagonal(axy1, bxy1, dxy_a, dxy_b, jx, jy)
        + diagonal(axz1, bxz1, dxz_a, dxz_b, jx, jz)
        + diagonal(ayz1, byz1, dyz_a, dyz_b, jy, jz)
    )
    return [jnp.where(fluid, relaxed[p], f[OPPOSITE[p]]) for p in range(Q)]


def shift_y(value, step, lane, row, block):
    rows = value.shape[0]
    turned = pltpu.roll(value, B if step == 1 else LANES - B, 1)
    if step == 1:
        edge, start = lane < B, row % PLANE_ROWS == 0
        near, far = pltpu.roll(turned, 1, 0), pltpu.roll(turned, block - 1, 0)
    else:
        edge, start = lane >= LANES - B, row % PLANE_ROWS == PLANE_ROWS - 1
        near, far = pltpu.roll(turned, rows - 1, 0), pltpu.roll(turned, rows - block + 1, 0)
    return jnp.where(edge, jnp.where(start, far, near), turned)


def shift_z(value, other, step, lane):
    if step == 1:
        return jnp.where(
            lane % B == 0, pltpu.roll(other, LANES - (B - 1), 1), pltpu.roll(value, 1, 1)
        )
    return jnp.where(
        lane % B == B - 1, pltpu.roll(other, B - 1, 1), pltpu.roll(value, LANES - 1, 1)
    )


def build(mesh):
    owners, slabs = mesh.shape["gx"], mesh.shape["gy"]
    planes = B // owners
    share = planes * PLANE
    block = planes * PLANE_ROWS
    rows = owners * block
    head = (Q + 1) * share
    rows_in = head + 8
    rows_out = Q * share
    faces = len(UPWARD) * PLANE
    rows_hop = faces + 4
    f32 = jnp.float32

    half = owners // 2
    spare = [*range(half + 2, owners), *range(4, half), 1]
    order_in = [0, 2, half, 3, half + 1, *spare]
    order_out = [0, half, 2, half + 1, 3, *spare]

    def by_owner(refs, order):
        return [refs[order.index(d)] for d in range(owners)]

    def position():
        me = lax.axis_index("gx")
        return me, lax.axis_index("gy") % 2

    def sides(odd, near, far):
        return (
            jnp.where(odd == 1, near[...], far[...]),
            jnp.where(odd == 1, far[...], near[...]),
        )

    def send_sides(odd, up, down, near, far):
        near[...] = jnp.where(odd == 1, down[...], up[...])
        far[...] = jnp.where(odd == 1, up[...], down[...])

    def edge_kernel(pops, mask, slots, swaps, near, far, own, up, down, cells, solid, held, given, sem):
        ends = (WHOLE - 8, 0)
        copies = []
        for n, start in enumerate(ends):
            copies.append((pops.at[:, pl.ds(start, 8), :], cells.at[n]))
            copies.append((mask.at[pl.ds(start, 8), :], solid.at[n]))
        copies += [(slots, held), (swaps, given)]
        copies = [
            pltpu.make_async_copy(source, target, sem.at[n])
            for n, (source, target) in enumerate(copies)
        ]
        for copy in copies:
            copy.start()
        for copy in copies:
            copy.wait()
        own[...] = jnp.zeros((8, LANES), f32)
        own[0:1, 0:NB] = held[...].astype(f32)
        own[1:2, 0:3] = given[0:1].astype(f32)
        for n, (out, chosen, inside) in enumerate(((up, UPWARD, 8 - PLANE), (down, DOWNWARD, 0))):
            after = collide([cells[n, p] for p in range(Q)], solid[n] > 0)
            for m, p in enumerate(chosen):
                out[pl.ds(m * PLANE, PLANE), :] = after[p][inside : inside + PLANE]
            out[pl.ds(faces, 4), :] = own[0:4]
        send_sides(position()[1], up, down, near, far)

    def collide_kernel(cells, solid, post):
        for start in range(0, WHOLE, 8):
            here = pl.ds(start, 8)
            after = collide([cells[p, here, :] for p in range(Q)], solid[here, :] > 0)
            for p in range(Q):
                post[p, pl.ds(8 + start, 8), :] = after[p]
            post[Q, pl.ds(8 + start, 8), :] = solid[here, :].astype(f32)

    def pack_kernel(post, own, near, far, *outs):
        me, odd = position()
        below, above = sides(odd, near, far)
        outs = by_owner(outs, order_in)
        for d in range(owners):
            out = outs[d]
            place = dynamic_place(me ^ d, odd, owners)
            here = pl.multiple_of(place * share, min(share, 8))
            for p in range(Q + 1):
                cx = VELOCITIES[p][0] if p < Q else 0
                out[pl.ds(p * share, share), :] = post[p, pl.ds(8 + here - cx * PLANE, share), :]
            out[pl.ds(head, 2), :] = own[0:2]
            out[pl.ds(head + 2, 2), :] = below[faces : faces + 2]
            out[pl.ds(head + 4, 2), :] = above[faces : faces + 2]
            out[pl.ds(head + 6, 2), :] = own[2:4]

            @pl.when(place == 0)
            def _():
                for n, p in enumerate(UPWARD):
                    out[pl.ds(p * share, PLANE), :] = below[n * PLANE : (n + 1) * PLANE]

            @pl.when(place == owners - 1)
            def _():
                for n, p in enumerate(DOWNWARD):
                    out[pl.ds(p * share + share - PLANE, PLANE), :] = above[
                        n * PLANE : (n + 1) * PLANE
                    ]

    def middle_kernel(*refs):
        got = by_owner(refs[:owners], order_in)
        outs = by_owner(refs[owners : 2 * owners], order_out)
        lattice, ready, table, sem = refs[2 * owners :]
        me, odd = position()
        place = dynamic_place(me, odd, owners)
        first, last = place == 0, place == owners - 1
        copies = [
            pltpu.make_async_copy(got[d].at[pl.ds(head, 8), :], table.at[d], sem.at[d])
            for d in range(owners)
        ]
        for copy in copies:
            copy.start()
        for copy in copies:
            copy.wait()

        def number(d, row, column):
            return table[d, row, column].astype(jnp.int32)

        other = jnp.where(first, 1, jnp.where(last, 2, 0))

        def seats(blocks):
            return [(b % NB, pl.multiple_of((b // NB) * block, block)) for b in blocks]

        def held(d, which):
            return [number(d, 2 * which, t) for t in range(NB)]

        def final(d, which):
            def lead(e, r):
                return number(d ^ e, 2 * which + 1, r)

            flip = lead(0, 2) + lead(4, 2) + lead(4, 1) + lead(6, 1) + lead(6, 0) + lead(7, 0)
            one, two = held(d ^ 7, which)
            crossed = flip % 2 == 1
            return [jnp.where(crossed, two, one), jnp.where(crossed, one, two)]

        for d in range(owners):
            for t, (kz, y) in enumerate(seats(held(d, 0))):
                for p in range(Q + 1):
                    lattice[p, kz, pl.ds(y, block), :] = got[d][
                        pl.ds(p * share + t, block, stride=NB), :
                    ]

        def bring(chosen, i):
            for d in range(owners):
                for t, (kz, y) in enumerate(seats(held(d, other))):
                    for p in chosen:
                        lattice[p, kz, pl.ds(y + i * PLANE_ROWS, PLANE_ROWS), :] = got[d][
                            pl.ds(p * share + i * PLANE + t, PLANE_ROWS, stride=NB), :
                        ]

        @pl.when(first)
        def _():
            bring(UPWARD, 0)

        @pl.when(last)
        def _():
            bring(DOWNWARD, planes - 1)

        lane = lax.broadcasted_iota(jnp.int32, (rows, LANES), 1)
        row = lax.broadcasted_iota(jnp.int32, (rows, LANES), 0)

        def passed(pair, p):
            cx, cy, cz = VELOCITIES[p]
            if cy:
                pair = [shift_y(value, cy, lane, row, block) for value in pair]
            if cz:
                pair = [shift_z(pair[kz], pair[1 - kz], cz, lane) for kz in range(NB)]
            return pair

        for p in range(Q):
            pair = passed([lattice[p, kz] for kz in range(NB)], p)
            for kz in range(NB):
                ready[p, kz] = pair[kz]
        for kz in range(NB):
            for start in range(0, rows, 16):
                here = pl.ds(start, 16)
                after = collide(
                    [ready[p, kz, here, :] for p in range(Q)], lattice[Q, kz, here, :] > 0.5
                )
                for p in range(Q):
                    lattice[p, kz, here, :] = after[p]
        for p in range(Q):
            pair = passed([lattice[p, kz] for kz in range(NB)], p)
            for kz in range(NB):
                ready[p, kz] = pair[kz]
        for d in range(owners):
            for t, (kz, y) in enumerate(seats(final(d, 0))):
                for p in range(Q):
                    outs[d][pl.ds(p * share + t, block, stride=NB), :] = ready[
                        p, kz, pl.ds(y, block), :
                    ]

        def bring_back(chosen, i):
            for d in range(owners):
                for t, (kz, y) in enumerate(seats(final(d, other))):
                    for p in chosen:
                        outs[d][
                            pl.ds(p * share + i * PLANE + t, PLANE_ROWS, stride=NB), :
                        ] = ready[p, kz, pl.ds(y + i * PLANE_ROWS, PLANE_ROWS), :]

        @pl.when(last)
        def _():
            bring_back(UPWARD, planes - 1)

        @pl.when(first)
        def _():
            bring_back(DOWNWARD, 0)

    def crossing_kernel(*refs):
        got = by_owner(refs[:owners], order_out)
        near, far, up, down = refs[owners:]
        me, odd = position()
        for d in range(owners):
            place = dynamic_place(me ^ d, odd, owners)

            @pl.when(place == owners - 1)
            def _():
                for n, p in enumerate(UPWARD):
                    up[pl.ds(n * PLANE, PLANE), :] = got[d][
                        pl.ds(p * share + share - PLANE, PLANE), :
                    ]

            @pl.when(place == 0)
            def _():
                for n, p in enumerate(DOWNWARD):
                    down[pl.ds(n * PLANE, PLANE), :] = got[d][pl.ds(p * share, PLANE), :]

        for out in (up, down):
            out[pl.ds(faces, 4), :] = jnp.zeros((4, LANES), f32)
        send_sides(odd, up, down, near, far)

    def unpack_kernel(*refs):
        got, main = by_owner(refs[:owners], order_out), refs[owners]
        me, odd = position()
        for d in range(owners):
            place = dynamic_place(me ^ d, odd, owners)
            here = pl.multiple_of(place * share, min(share, 8))
            for p in range(Q):
                cx = VELOCITIES[p][0]
                main[p, pl.ds(8 + here + cx * PLANE, share), :] = got[d][
                    pl.ds(p * share, share), :
                ]

    def finish_kernel(main, near, far, out):
        below, above = sides(position()[1], near, far)
        for p in range(Q):
            out[pl.ds(p * WHOLE, WHOLE), :] = main[p, pl.ds(8, WHOLE), :]
        for n, p in enumerate(UPWARD):
            out[pl.ds(p * WHOLE, PLANE), :] = below[n * PLANE : (n + 1) * PLANE]
        for n, p in enumerate(DOWNWARD):
            out[pl.ds(p * WHOLE + WHOLE - PLANE, PLANE), :] = above[n * PLANE : (n + 1) * PLANE]

    def shape(*dims):
        return jax.ShapeDtypeStruct(dims, f32)

    def call(kernel, name, out_shape, inputs, cost, scratch=(), spec=VMEM_SPEC, limit=40):
        outs = jax.tree.map(lambda _: VMEM_SPEC, out_shape)
        return pl.pallas_call(
            kernel,
            out_shape=out_shape,
            in_specs=[spec] * len(inputs),
            out_specs=outs,
            scratch_shapes=list(scratch),
            compiler_params=pltpu.CompilerParams(vmem_limit_bytes=limit * 1024 * 1024),
            cost_estimate=pl.CostEstimate(flops=cost, bytes_accessed=cost, transcendentals=0),
            name=name,
        )(*inputs)

    def exchange(parts, order):
        return [parts[0]] + [
            lax.ppermute(parts[n], "gx", [(g, g ^ order[n]) for g in range(owners)])
            for n in range(1, owners)
        ]

    def hop(near, far):
        ahead = [(s + 1) % slabs if s % 2 == 0 else (s - 1) % slabs for s in range(slabs)]
        behind = [(s - 1) % slabs if s % 2 == 0 else (s + 1) % slabs for s in range(slabs)]
        return (
            lax.ppermute(near, "gy", list(enumerate(ahead))),
            lax.ppermute(far, "gy", list(enumerate(behind))),
        )

    def padded(count):
        return shape(count, 8 + WHOLE + 8, LANES)

    work = pltpu.VMEM((Q + 1, NB, rows, LANES), f32)
    small, large = 100_000, 4_000_000

    def shards(populations, solid_mask, slot_blocks, swap_slots):
        tiles = B * B * B // LANES
        pops = populations[0].transpose(1, 0, 2).reshape(Q, NB, tiles, LANES)
        pops = pops.transpose(0, 2, 1, 3).reshape(Q, WHOLE, LANES)
        mask = solid_mask[0].reshape(NB, tiles, LANES).transpose(1, 0, 2).reshape(WHOLE, LANES)
        swaps = swap_slots[0, 0].T
        in_place = pl.BlockSpec(memory_space=pltpu.HBM)
        near, far, own = call(
            edge_kernel,
            "edge_planes",
            (shape(rows_hop, LANES), shape(rows_hop, LANES), shape(8, LANES)),
            (pops, mask, slot_blocks, swaps),
            small,
            (
                pltpu.VMEM((rows_hop, LANES), f32),
                pltpu.VMEM((rows_hop, LANES), f32),
                pltpu.VMEM((2, Q, 8, LANES), f32),
                pltpu.VMEM((2, 8, LANES), jnp.int32),
                pltpu.VMEM(slot_blocks.shape, jnp.int32),
                pltpu.VMEM(swaps.shape, jnp.int32),
                pltpu.SemaphoreType.DMA((6,)),
            ),
            in_place,
            62,
        )
        near, far = hop(near, far)
        post = call(
            collide_kernel,
            "first_collision",
            padded(Q + 1),
            (pops, mask),
            large,
        )
        parts = call(
            pack_kernel,
            "pack_planes",
            (shape(rows_in, LANES),) * owners,
            (post, own, near, far),
            large,
        )
        got = exchange(parts, order_in)
        parts = call(
            middle_kernel,
            "second_step",
            (shape(rows_out, LANES),) * owners,
            got,
            large,
            (
                work,
                work,
                pltpu.SMEM((owners, 8, LANES), f32),
                pltpu.SemaphoreType.DMA((owners,)),
            ),
        )
        home = exchange(parts, order_out)
        near, far = call(
            crossing_kernel,
            "crossing_planes",
            (shape(rows_hop, LANES),) * 2,
            home,
            small,
            (pltpu.VMEM((rows_hop, LANES), f32),) * 2,
        )
        near, far = hop(near, far)
        main = call(unpack_kernel, "unpack_planes", padded(Q), home, large)
        out = call(
            finish_kernel, "finish", shape(Q * WHOLE, LANES), (main, near, far), small
        )
        out = out.reshape(Q, tiles, NB, LANES).transpose(0, 2, 1, 3)
        return out.reshape(Q, NB, B * B * B).transpose(1, 0, 2)[None]

    return shards


def solution(mesh):
    return jax.shard_map(
        build(mesh),
        mesh=mesh,
        in_specs=(
            P("gy", "gx", None, None),
            P("gy", "gx", None),
            P("gy", "gx"),
            P("gy", "gx", None, None),
        ),
        out_specs=P("gy", "gx", None, None),
        check_vma=False,
    )
```

```python
import jax
import jax.numpy as jnp
from jax import lax
from jax.experimental import pallas as pl
from jax.experimental.pallas import tpu as pltpu
from jax.sharding import PartitionSpec as P

B = 16
NB = 2
LANES = 128
PLANE_ROWS = B * B // LANES
PLANE = PLANE_ROWS * NB
WHOLE = B * PLANE

VELOCITIES = (
    (0, 0, 0),
    (1, 0, 0),
    (-1, 0, 0),
    (0, 1, 0),
    (0, -1, 0),
    (0, 0, 1),
    (0, 0, -1),
    (1, 1, 0),
    (-1, -1, 0),
    (1, -1, 0),
    (-1, 1, 0),
    (1, 0, 1),
    (-1, 0, -1),
    (1, 0, -1),
    (-1, 0, 1),
    (0, 1, 1),
    (0, -1, -1),
    (0, 1, -1),
    (0, -1, 1),
)
OPPOSITE = (0, 2, 1, 4, 3, 6, 5, 8, 7, 10, 9, 12, 11, 14, 13, 16, 15, 18, 17)
Q = len(VELOCITIES)
UPWARD = tuple(p for p in range(Q) if VELOCITIES[p][0] == 1)
DOWNWARD = tuple(p for p in range(Q) if VELOCITIES[p][0] == -1)

VMEM_SPEC = pl.BlockSpec(memory_space=pltpu.VMEM)


def dynamic_place(owner, odd_slab, owners):
    pair, core = owner // 2, owner % 2
    forward = 2 * pair + jnp.where(pair % 2 == 0, core, 1 - core)
    return jnp.where(odd_slab == 1, owners - 1 - forward, forward)


def collide(f, fluid):
    def pair(p):
        return f[p] + f[p + 1], f[p] - f[p + 1]

    sx, dx = pair(1)
    sy, dy = pair(3)
    sz, dz = pair(5)
    sxy_a, dxy_a = pair(7)
    sxy_b, dxy_b = pair(9)
    sxz_a, dxz_a = pair(11)
    sxz_b, dxz_b = pair(13)
    syz_a, dyz_a = pair(15)
    syz_b, dyz_b = pair(17)
    axy, bxy = sxy_a + sxy_b, sxy_a - sxy_b
    axz, bxz = sxz_a + sxz_b, sxz_a - sxz_b
    ayz, byz = syz_a + syz_b, syz_a - syz_b
    rho = f[0] + sx + sy + sz + axy + axz + ayz
    ox = dxy_a + dxy_b + dxz_a + dxz_b
    oy = dxy_a - dxy_b + dyz_a + dyz_b
    oz = dxz_a - dxz_b + dyz_a - dyz_b
    jx, jy, jz = dx + ox, dy + oy, dz + oz
    jxx, jyy, jzz = jx * jx, jy * jy, jz * jz
    base = rho * (1.3 / 9.0)
    wide = 1.3 / 3.0
    thin = 1.3 / 6.0
    axy1 = base - 0.3 * axy + wide * (jxx + jyy) - thin * jzz
    axz1 = base - 0.3 * axz + wide * (jxx + jzz) - thin * jyy
    ayz1 = base - 0.3 * ayz + wide * (jyy + jzz) - thin * jxx
    bxy1 = 1.25 * (jx * jy) - 0.25 * bxy
    bxz1 = 1.25 * (jx * jz) - 0.25 * bxz
    byz1 = 1.25 * (jy * jz) - 0.25 * byz
    third = rho * (1.25 / 3.0)
    sx1 = third + 1.25 * jxx - 0.25 * (sx + axy + axz) - axy1 - axz1
    sy1 = third + 1.25 * jyy - 0.25 * (sy + axy + ayz) - axy1 - ayz1
    sz1 = third + 1.25 * jzz - 0.25 * (sz + axz + ayz) - axz1 - ayz1
    rest = rho - sx1 - sy1 - sz1 - axy1 - axz1 - ayz1

    def split(even, odd):
        return 0.5 * (even + odd), 0.5 * (even - odd)

    def diagonal(a1, b1, d_a, d_b, j_first, j_second):
        plus = 0.25 * (j_first + j_second) - 0.5 * d_a
        minus = 0.25 * (j_first - j_second) - 0.5 * d_b
        return split(0.5 * (a1 + b1), plus) + split(0.5 * (a1 - b1), minus)

    relaxed = (
        (rest,)
        + split(sx1, 0.5 * ox)
        + split(sy1, 0.5 * oy)
        + split(sz1, 0.5 * oz)
        + diagonal(axy1, bxy1, dxy_a, dxy_b, jx, jy)
        + diagonal(axz1, bxz1, dxz_a, dxz_b, jx, jz)
        + diagonal(ayz1, byz1, dyz_a, dyz_b, jy, jz)
    )
    return [jnp.where(fluid, relaxed[p], f[OPPOSITE[p]]) for p in range(Q)]


def shift_y(value, step, lane, row, block):
    rows = value.shape[0]
    turned = pltpu.roll(value, B if step == 1 else LANES - B, 1)
    if step == 1:
        edge, start = lane < B, row % PLANE_ROWS == 0
        near, far = pltpu.roll(turned, 1, 0), pltpu.roll(turned, block - 1, 0)
    else:
        edge, start = lane >= LANES - B, row % PLANE_ROWS == PLANE_ROWS - 1
        near, far = pltpu.roll(turned, rows - 1, 0), pltpu.roll(turned, rows - block + 1, 0)
    return jnp.where(edge, jnp.where(start, far, near), turned)


def shift_z(value, other, step, lane):
    if step == 1:
        return jnp.where(
            lane % B == 0, pltpu.roll(other, LANES - (B - 1), 1), pltpu.roll(value, 1, 1)
        )
    return jnp.where(
        lane % B == B - 1, pltpu.roll(other, B - 1, 1), pltpu.roll(value, LANES - 1, 1)
    )


def build(mesh):
    owners, slabs = mesh.shape["gx"], mesh.shape["gy"]
    planes = B // owners
    share = planes * PLANE
    block = planes * PLANE_ROWS
    rows = owners * block
    head = (Q + 1) * share
    rows_in = head + 8
    rows_out = Q * share
    faces = len(UPWARD) * PLANE
    rows_hop = faces + 4
    f32 = jnp.float32

    half = owners // 2
    spare = [*range(half + 2, owners), *range(4, half), 1]
    order_in = [0, half, 2, half + 1, 3, *spare]
    order_out = [0, half, 2, half + 1, 3, *spare]

    def by_owner(refs, order):
        return [refs[order.index(d)] for d in range(owners)]

    def position():
        me = lax.axis_index("gx")
        return me, lax.axis_index("gy") % 2

    def sides(odd, near, far):
        return (
            jnp.where(odd == 1, near[...], far[...]),
            jnp.where(odd == 1, far[...], near[...]),
        )

    def send_sides(odd, up, down, near, far):
        near[...] = jnp.where(odd == 1, down[...], up[...])
        far[...] = jnp.where(odd == 1, up[...], down[...])

    def edge_kernel(pops, mask, slots, swaps, near, far, own, up, down, cells, solid, held, given, sem):
        ends = (WHOLE - 8, 0)
        copies = []
        for n, start in enumerate(ends):
            copies.append((pops.at[:, pl.ds(start, 8), :], cells.at[n]))
            copies.append((mask.at[pl.ds(start, 8), :], solid.at[n]))
        copies += [(slots, held), (swaps, given)]
        copies = [
            pltpu.make_async_copy(source, target, sem.at[n])
            for n, (source, target) in enumerate(copies)
        ]
        for copy in copies:
            copy.start()
        for copy in copies:
            copy.wait()
        own[...] = jnp.zeros((8, LANES), f32)
        own[0:1, 0:NB] = held[...].astype(f32)
        own[1:2, 0:3] = given[0:1].astype(f32)
        for n, (out, chosen, inside) in enumerate(((up, UPWARD, 8 - PLANE), (down, DOWNWARD, 0))):
            after = collide([cells[n, p] for p in range(Q)], solid[n] > 0)
            for m, p in enumerate(chosen):
                out[pl.ds(m * PLANE, PLANE), :] = after[p][inside : inside + PLANE]
            out[pl.ds(faces, 4), :] = own[0:4]
        send_sides(position()[1], up, down, near, far)

    def collide_kernel(cells, solid, post):
        for start in range(0, WHOLE, 8):
            here = pl.ds(start, 8)
            after = collide([cells[p, here, :] for p in range(Q)], solid[here, :] > 0)
            for p in range(Q):
                post[p, pl.ds(8 + start, 8), :] = after[p]
            post[Q, pl.ds(8 + start, 8), :] = solid[here, :].astype(f32)

    def pack_kernel(post, own, near, far, *outs):
        me, odd = position()
        below, above = sides(odd, near, far)
        outs = by_owner(outs, order_in)
        for d in range(owners):
            out = outs[d]
            place = dynamic_place(me ^ d, odd, owners)
            here = pl.multiple_of(place * share, min(share, 8))
            for p in range(Q + 1):
                cx = VELOCITIES[p][0] if p < Q else 0
                out[pl.ds(p * share, share), :] = post[p, pl.ds(8 + here - cx * PLANE, share), :]
            out[pl.ds(head, 2), :] = own[0:2]
            out[pl.ds(head + 2, 2), :] = below[faces : faces + 2]
            out[pl.ds(head + 4, 2), :] = above[faces : faces + 2]
            out[pl.ds(head + 6, 2), :] = own[2:4]

            @pl.when(place == 0)
            def _():
                for n, p in enumerate(UPWARD):
                    out[pl.ds(p * share, PLANE), :] = below[n * PLANE : (n + 1) * PLANE]

            @pl.when(place == owners - 1)
            def _():
                for n, p in enumerate(DOWNWARD):
                    out[pl.ds(p * share + share - PLANE, PLANE), :] = above[
                        n * PLANE : (n + 1) * PLANE
                    ]

    def middle_kernel(*refs):
        got = by_owner(refs[:owners], order_in)
        outs = by_owner(refs[owners : 2 * owners], order_out)
        lattice, ready, table, sem = refs[2 * owners :]
        me, odd = position()
        place = dynamic_place(me, odd, owners)
        first, last = place == 0, place == owners - 1
        copies = [
            pltpu.make_async_copy(got[d].at[pl.ds(head, 8), :], table.at[d], sem.at[d])
            for d in range(owners)
        ]
        for copy in copies:
            copy.start()
        for copy in copies:
            copy.wait()

        def number(d, row, column):
            return table[d, row, column].astype(jnp.int32)

        other = jnp.where(first, 1, jnp.where(last, 2, 0))

        def seats(blocks):
            return [(b % NB, pl.multiple_of((b // NB) * block, block)) for b in blocks]

        def held(d, which):
            return [number(d, 2 * which, t) for t in range(NB)]

        def final(d, which):
            def lead(e, r):
                return number(d ^ e, 2 * which + 1, r)

            flip = lead(0, 2) + lead(4, 2) + lead(4, 1) + lead(6, 1) + lead(6, 0) + lead(7, 0)
            one, two = held(d ^ 7, which)
            crossed = flip % 2 == 1
            return [jnp.where(crossed, two, one), jnp.where(crossed, one, two)]

        for d in range(owners):
            for t, (kz, y) in enumerate(seats(held(d, 0))):
                for p in range(Q + 1):
                    lattice[p, kz, pl.ds(y, block), :] = got[d][
                        pl.ds(p * share + t, block, stride=NB), :
                    ]

        def bring(chosen, i):
            for d in range(owners):
                for t, (kz, y) in enumerate(seats(held(d, other))):
                    for p in chosen:
                        lattice[p, kz, pl.ds(y + i * PLANE_ROWS, PLANE_ROWS), :] = got[d][
                            pl.ds(p * share + i * PLANE + t, PLANE_ROWS, stride=NB), :
                        ]

        @pl.when(first)
        def _():
            bring(UPWARD, 0)

        @pl.when(last)
        def _():
            bring(DOWNWARD, planes - 1)

        lane = lax.broadcasted_iota(jnp.int32, (rows, LANES), 1)
        row = lax.broadcasted_iota(jnp.int32, (rows, LANES), 0)

        def passed(pair, p):
            cx, cy, cz = VELOCITIES[p]
            if cy:
                pair = [shift_y(value, cy, lane, row, block) for value in pair]
            if cz:
                pair = [shift_z(pair[kz], pair[1 - kz], cz, lane) for kz in range(NB)]
            return pair

        for p in range(Q):
            pair = passed([lattice[p, kz] for kz in range(NB)], p)
            for kz in range(NB):
                ready[p, kz] = pair[kz]
        for kz in range(NB):
            for start in range(0, rows, 16):
                here = pl.ds(start, 16)
                after = collide(
                    [ready[p, kz, here, :] for p in range(Q)], lattice[Q, kz, here, :] > 0.5
                )
                for p in range(Q):
                    lattice[p, kz, here, :] = after[p]
        for p in range(Q):
            pair = passed([lattice[p, kz] for kz in range(NB)], p)
            for kz in range(NB):
                ready[p, kz] = pair[kz]
        for d in range(owners):
            for t, (kz, y) in enumerate(seats(final(d, 0))):
                for p in range(Q):
                    outs[d][pl.ds(p * share + t, block, stride=NB), :] = ready[
                        p, kz, pl.ds(y, block), :
                    ]

        def bring_back(chosen, i):
            for d in range(owners):
                for t, (kz, y) in enumerate(seats(final(d, other))):
                    for p in chosen:
                        outs[d][
                            pl.ds(p * share + i * PLANE + t, PLANE_ROWS, stride=NB), :
                        ] = ready[p, kz, pl.ds(y + i * PLANE_ROWS, PLANE_ROWS), :]

        @pl.when(last)
        def _():
            bring_back(UPWARD, planes - 1)

        @pl.when(first)
        def _():
            bring_back(DOWNWARD, 0)

    def crossing_kernel(*refs):
        got = by_owner(refs[:owners], order_out)
        near, far, up, down = refs[owners:]
        me, odd = position()
        for d in range(owners):
            place = dynamic_place(me ^ d, odd, owners)

            @pl.when(place == owners - 1)
            def _():
                for n, p in enumerate(UPWARD):
                    up[pl.ds(n * PLANE, PLANE), :] = got[d][
                        pl.ds(p * share + share - PLANE, PLANE), :
                    ]

            @pl.when(place == 0)
            def _():
                for n, p in enumerate(DOWNWARD):
                    down[pl.ds(n * PLANE, PLANE), :] = got[d][pl.ds(p * share, PLANE), :]

        for out in (up, down):
            out[pl.ds(faces, 4), :] = jnp.zeros((4, LANES), f32)
        send_sides(odd, up, down, near, far)

    def unpack_kernel(*refs):
        got, main = by_owner(refs[:owners], order_out), refs[owners]
        me, odd = position()
        for d in range(owners):
            place = dynamic_place(me ^ d, odd, owners)
            here = pl.multiple_of(place * share, min(share, 8))
            for p in range(Q):
                cx = VELOCITIES[p][0]
                main[p, pl.ds(8 + here + cx * PLANE, share), :] = got[d][
                    pl.ds(p * share, share), :
                ]

    def finish_kernel(main, near, far, out):
        below, above = sides(position()[1], near, far)
        for p in range(Q):
            out[pl.ds(p * WHOLE, WHOLE), :] = main[p, pl.ds(8, WHOLE), :]
        for n, p in enumerate(UPWARD):
            out[pl.ds(p * WHOLE, PLANE), :] = below[n * PLANE : (n + 1) * PLANE]
        for n, p in enumerate(DOWNWARD):
            out[pl.ds(p * WHOLE + WHOLE - PLANE, PLANE), :] = above[n * PLANE : (n + 1) * PLANE]

    def shape(*dims):
        return jax.ShapeDtypeStruct(dims, f32)

    def call(kernel, name, out_shape, inputs, cost, scratch=(), spec=VMEM_SPEC, limit=40):
        outs = jax.tree.map(lambda _: VMEM_SPEC, out_shape)
        return pl.pallas_call(
            kernel,
            out_shape=out_shape,
            in_specs=[spec] * len(inputs),
            out_specs=outs,
            scratch_shapes=list(scratch),
            compiler_params=pltpu.CompilerParams(vmem_limit_bytes=limit * 1024 * 1024),
            cost_estimate=pl.CostEstimate(flops=cost, bytes_accessed=cost, transcendentals=0),
            name=name,
        )(*inputs)

    def exchange(parts, order):
        return [parts[0]] + [
            lax.ppermute(parts[n], "gx", [(g, g ^ order[n]) for g in range(owners)])
            for n in range(1, owners)
        ]

    def hop(near, far):
        ahead = [(s + 1) % slabs if s % 2 == 0 else (s - 1) % slabs for s in range(slabs)]
        behind = [(s - 1) % slabs if s % 2 == 0 else (s + 1) % slabs for s in range(slabs)]
        return (
            lax.ppermute(near, "gy", list(enumerate(ahead))),
            lax.ppermute(far, "gy", list(enumerate(behind))),
        )

    def padded(count):
        return shape(count, 8 + WHOLE + 8, LANES)

    work = pltpu.VMEM((Q + 1, NB, rows, LANES), f32)
    small, large = 100_000, 4_000_000

    def shards(populations, solid_mask, slot_blocks, swap_slots):
        tiles = B * B * B // LANES
        pops = populations[0].transpose(1, 0, 2).reshape(Q, NB, tiles, LANES)
        pops = pops.transpose(0, 2, 1, 3).reshape(Q, WHOLE, LANES)
        mask = solid_mask[0].reshape(NB, tiles, LANES).transpose(1, 0, 2).reshape(WHOLE, LANES)
        swaps = swap_slots[0, 0].T
        in_place = pl.BlockSpec(memory_space=pltpu.HBM)
        near, far, own = call(
            edge_kernel,
            "edge_planes",
            (shape(rows_hop, LANES), shape(rows_hop, LANES), shape(8, LANES)),
            (pops, mask, slot_blocks, swaps),
            small,
            (
                pltpu.VMEM((rows_hop, LANES), f32),
                pltpu.VMEM((rows_hop, LANES), f32),
                pltpu.VMEM((2, Q, 8, LANES), f32),
                pltpu.VMEM((2, 8, LANES), jnp.int32),
                pltpu.VMEM(slot_blocks.shape, jnp.int32),
                pltpu.VMEM(swaps.shape, jnp.int32),
                pltpu.SemaphoreType.DMA((6,)),
            ),
            in_place,
            62,
        )
        near, far = hop(near, far)
        post = call(
            collide_kernel,
            "first_collision",
            padded(Q + 1),
            (pops, mask),
            large,
        )
        parts = call(
            pack_kernel,
            "pack_planes",
            (shape(rows_in, LANES),) * owners,
            (post, own, near, far),
            large,
        )
        got = exchange(parts, order_in)
        parts = call(
            middle_kernel,
            "second_step",
            (shape(rows_out, LANES),) * owners,
            got,
            large,
            (
                work,
                work,
                pltpu.SMEM((owners, 8, LANES), f32),
                pltpu.SemaphoreType.DMA((owners,)),
            ),
        )
        home = exchange(parts, order_out)
        near, far = call(
            crossing_kernel,
            "crossing_planes",
            (shape(rows_hop, LANES),) * 2,
            home,
            small,
            (pltpu.VMEM((rows_hop, LANES), f32),) * 2,
        )
        near, far = hop(near, far)
        main = call(unpack_kernel, "unpack_planes", padded(Q), home, large)
        out = call(
            finish_kernel, "finish", shape(Q * WHOLE, LANES), (main, near, far), small
        )
        out = out.reshape(Q, tiles, NB, LANES).transpose(0, 2, 1, 3)
        return out.reshape(Q, NB, B * B * B).transpose(1, 0, 2)[None]

    return shards


def solution(mesh):
    return jax.shard_map(
        build(mesh),
        mesh=mesh,
        in_specs=(
            P("gy", "gx", None, None),
            P("gy", "gx", None),
            P("gy", "gx"),
            P("gy", "gx", None, None),
        ),
        out_specs=P("gy", "gx", None, None),
        check_vma=False,
    )
```

```python
import jax
import jax.numpy as jnp
from jax import lax
from jax.experimental import pallas as pl
from jax.experimental.pallas import tpu as pltpu
from jax.sharding import PartitionSpec as P

B = 16
NB = 2
LANES = 128
PLANE_ROWS = B * B // LANES
PLANE = PLANE_ROWS * NB
WHOLE = B * PLANE

VELOCITIES = (
    (0, 0, 0),
    (1, 0, 0),
    (-1, 0, 0),
    (0, 1, 0),
    (0, -1, 0),
    (0, 0, 1),
    (0, 0, -1),
    (1, 1, 0),
    (-1, -1, 0),
    (1, -1, 0),
    (-1, 1, 0),
    (1, 0, 1),
    (-1, 0, -1),
    (1, 0, -1),
    (-1, 0, 1),
    (0, 1, 1),
    (0, -1, -1),
    (0, 1, -1),
    (0, -1, 1),
)
OPPOSITE = (0, 2, 1, 4, 3, 6, 5, 8, 7, 10, 9, 12, 11, 14, 13, 16, 15, 18, 17)
Q = len(VELOCITIES)
UPWARD = tuple(p for p in range(Q) if VELOCITIES[p][0] == 1)
DOWNWARD = tuple(p for p in range(Q) if VELOCITIES[p][0] == -1)

LEVEL = tuple(p for p in range(Q) if VELOCITIES[p][0] == 0)
SLOPED = UPWARD + DOWNWARD

VMEM_SPEC = pl.BlockSpec(memory_space=pltpu.VMEM)


def dynamic_place(owner, odd_slab, owners):
    pair, core = owner // 2, owner % 2
    forward = 2 * pair + jnp.where(pair % 2 == 0, core, 1 - core)
    return jnp.where(odd_slab == 1, owners - 1 - forward, forward)


def collide(f, fluid):
    def pair(p):
        return f[p] + f[p + 1], f[p] - f[p + 1]

    sx, dx = pair(1)
    sy, dy = pair(3)
    sz, dz = pair(5)
    sxy_a, dxy_a = pair(7)
    sxy_b, dxy_b = pair(9)
    sxz_a, dxz_a = pair(11)
    sxz_b, dxz_b = pair(13)
    syz_a, dyz_a = pair(15)
    syz_b, dyz_b = pair(17)
    axy, bxy = sxy_a + sxy_b, sxy_a - sxy_b
    axz, bxz = sxz_a + sxz_b, sxz_a - sxz_b
    ayz, byz = syz_a + syz_b, syz_a - syz_b
    rho = f[0] + sx + sy + sz + axy + axz + ayz
    ox = dxy_a + dxy_b + dxz_a + dxz_b
    oy = dxy_a - dxy_b + dyz_a + dyz_b
    oz = dxz_a - dxz_b + dyz_a - dyz_b
    jx, jy, jz = dx + ox, dy + oy, dz + oz
    jxx, jyy, jzz = jx * jx, jy * jy, jz * jz
    base = rho * (1.3 / 9.0)
    wide = 1.3 / 3.0
    thin = 1.3 / 6.0
    axy1 = base - 0.3 * axy + wide * (jxx + jyy) - thin * jzz
    axz1 = base - 0.3 * axz + wide * (jxx + jzz) - thin * jyy
    ayz1 = base - 0.3 * ayz + wide * (jyy + jzz) - thin * jxx
    bxy1 = 1.25 * (jx * jy) - 0.25 * bxy
    bxz1 = 1.25 * (jx * jz) - 0.25 * bxz
    byz1 = 1.25 * (jy * jz) - 0.25 * byz
    third = rho * (1.25 / 3.0)
    sx1 = third + 1.25 * jxx - 0.25 * (sx + axy + axz) - axy1 - axz1
    sy1 = third + 1.25 * jyy - 0.25 * (sy + axy + ayz) - axy1 - ayz1
    sz1 = third + 1.25 * jzz - 0.25 * (sz + axz + ayz) - axz1 - ayz1
    rest = rho - sx1 - sy1 - sz1 - axy1 - axz1 - ayz1

    def split(even, odd):
        return 0.5 * (even + odd), 0.5 * (even - odd)

    def diagonal(a1, b1, d_a, d_b, j_first, j_second):
        plus = 0.25 * (j_first + j_second) - 0.5 * d_a
        minus = 0.25 * (j_first - j_second) - 0.5 * d_b
        return split(0.5 * (a1 + b1), plus) + split(0.5 * (a1 - b1), minus)

    relaxed = (
        (rest,)
        + split(sx1, 0.5 * ox)
        + split(sy1, 0.5 * oy)
        + split(sz1, 0.5 * oz)
        + diagonal(axy1, bxy1, dxy_a, dxy_b, jx, jy)
        + diagonal(axz1, bxz1, dxz_a, dxz_b, jx, jz)
        + diagonal(ayz1, byz1, dyz_a, dyz_b, jy, jz)
    )
    return [jnp.where(fluid, relaxed[p], f[OPPOSITE[p]]) for p in range(Q)]


def shift_y(value, step, lane, row, block):
    rows = value.shape[0]
    turned = pltpu.roll(value, B if step == 1 else LANES - B, 1)
    if step == 1:
        edge, start = lane < B, row % PLANE_ROWS == 0
        near, far = pltpu.roll(turned, 1, 0), pltpu.roll(turned, block - 1, 0)
    else:
        edge, start = lane >= LANES - B, row % PLANE_ROWS == PLANE_ROWS - 1
        near, far = pltpu.roll(turned, rows - 1, 0), pltpu.roll(turned, rows - block + 1, 0)
    return jnp.where(edge, jnp.where(start, far, near), turned)


def shift_z(value, other, step, lane):
    if step == 1:
        return jnp.where(
            lane % B == 0, pltpu.roll(other, LANES - (B - 1), 1), pltpu.roll(value, 1, 1)
        )
    return jnp.where(
        lane % B == B - 1, pltpu.roll(other, B - 1, 1), pltpu.roll(value, LANES - 1, 1)
    )


def build(mesh):
    owners, slabs = mesh.shape["gx"], mesh.shape["gy"]
    planes = B // owners
    share = planes * PLANE
    block = planes * PLANE_ROWS
    rows = owners * block
    head = (Q + 1) * share
    head_sloped = len(SLOPED) * share
    rows_in = head + 8
    rows_out = Q * share
    faces = len(UPWARD) * PLANE
    rows_hop = faces + 4
    f32 = jnp.float32

    half = owners // 2
    split = (half, half + 1)
    middle = [(d, "whole") for d in range(half + 2, owners)]
    beside = [(d, "whole") for d in range(1, half)]
    level = [(d, "level") for d in split]
    sloped = [(d, "sloped") for d in split]
    own = [(0, "whole")]
    rest = [*middle, *beside[3:], beside[0]]
    lines_in = own + [(half, "whole"), beside[1], (half + 1, "whole"), beside[2], *rest]
    lines_out = own + [sloped[0], beside[1], sloped[1], beside[2], *rest] + level
    sizes_in = {"whole": rows_in}
    sizes_out = {"whole": rows_out, "level": len(LEVEL) * share, "sloped": head_sloped}

    def spot(refs, lines, d, p):
        if (d, "whole") in lines:
            return refs[lines.index((d, "whole"))], p * share
        if p in SLOPED:
            return refs[lines.index((d, "sloped"))], SLOPED.index(p) * share
        return refs[lines.index((d, "level"))], LEVEL.index(p) * share

    def position():
        me = lax.axis_index("gx")
        return me, lax.axis_index("gy") % 2

    def sides(odd, near, far):
        return (
            jnp.where(odd == 1, near[...], far[...]),
            jnp.where(odd == 1, far[...], near[...]),
        )

    def send_sides(odd, up, down, near, far):
        near[...] = jnp.where(odd == 1, down[...], up[...])
        far[...] = jnp.where(odd == 1, up[...], down[...])

    def edge_kernel(pops, mask, slots, swaps, near, far, own, up, down, cells, solid, held, given, sem):
        ends = (WHOLE - 8, 0)
        copies = []
        for n, start in enumerate(ends):
            copies.append((pops.at[:, pl.ds(start, 8), :], cells.at[n]))
            copies.append((mask.at[pl.ds(start, 8), :], solid.at[n]))
        copies += [(slots, held), (swaps, given)]
        copies = [
            pltpu.make_async_copy(source, target, sem.at[n])
            for n, (source, target) in enumerate(copies)
        ]
        for copy in copies:
            copy.start()
        for copy in copies:
            copy.wait()
        own[...] = jnp.zeros((8, LANES), f32)
        own[0:1, 0:NB] = held[...].astype(f32)
        own[1:2, 0:3] = given[0:1].astype(f32)
        for n, (out, chosen, inside) in enumerate(((up, UPWARD, 8 - PLANE), (down, DOWNWARD, 0))):
            after = collide([cells[n, p] for p in range(Q)], solid[n] > 0)
            for m, p in enumerate(chosen):
                out[pl.ds(m * PLANE, PLANE), :] = after[p][inside : inside + PLANE]
            out[pl.ds(faces, 4), :] = own[0:4]
        send_sides(position()[1], up, down, near, far)

    def collide_kernel(cells, solid, post):
        for start in range(0, WHOLE, 8):
            here = pl.ds(start, 8)
            after = collide([cells[p, here, :] for p in range(Q)], solid[here, :] > 0)
            for p in range(Q):
                post[p, pl.ds(8 + start, 8), :] = after[p]
            post[Q, pl.ds(8 + start, 8), :] = solid[here, :].astype(f32)

    def pack_kernel(post, own, near, far, *outs):
        me, odd = position()
        below, above = sides(odd, near, far)
        for d in range(owners):
            place = dynamic_place(me ^ d, odd, owners)
            here = pl.multiple_of(place * share, min(share, 8))
            for p in range(Q + 1):
                cx = VELOCITIES[p][0] if p < Q else 0
                out, row = spot(outs, lines_in, d, p)
                out[pl.ds(row, share), :] = post[p, pl.ds(8 + here - cx * PLANE, share), :]
            out[pl.ds(head, 2), :] = own[0:2]
            out[pl.ds(head + 2, 2), :] = below[faces : faces + 2]
            out[pl.ds(head + 4, 2), :] = above[faces : faces + 2]
            out[pl.ds(head + 6, 2), :] = own[2:4]

            @pl.when(place == 0)
            def _():
                for n, p in enumerate(UPWARD):
                    out, row = spot(outs, lines_in, d, p)
                    out[pl.ds(row, PLANE), :] = below[n * PLANE : (n + 1) * PLANE]

            @pl.when(place == owners - 1)
            def _():
                for n, p in enumerate(DOWNWARD):
                    out, row = spot(outs, lines_in, d, p)
                    out[pl.ds(row + share - PLANE, PLANE), :] = above[n * PLANE : (n + 1) * PLANE]

    def middle_kernel(*refs):
        *messages, lattice, ready, table, sem = refs
        got, outs = messages[:owners], messages[owners:]
        me, odd = position()
        place = dynamic_place(me, odd, owners)
        first, last = place == 0, place == owners - 1
        copies = [
            pltpu.make_async_copy(ref.at[pl.ds(head, 8), :], table.at[d], sem.at[n])
            for n, (ref, (d, _)) in enumerate(zip(got, lines_in))
        ]
        for copy in copies:
            copy.start()
        for copy in copies:
            copy.wait()

        def number(d, row, column):
            return table[d, row, column].astype(jnp.int32)

        other = jnp.where(first, 1, jnp.where(last, 2, 0))

        def seats(blocks):
            return [(b % NB, pl.multiple_of((b // NB) * block, block)) for b in blocks]

        def held(d, which):
            return [number(d, 2 * which, t) for t in range(NB)]

        def final(d, which):
            def lead(e, r):
                return number(d ^ e, 2 * which + 1, r)

            flip = lead(0, 2) + lead(4, 2) + lead(4, 1) + lead(6, 1) + lead(6, 0) + lead(7, 0)
            one, two = held(d ^ 7, which)
            crossed = flip % 2 == 1
            return [jnp.where(crossed, two, one), jnp.where(crossed, one, two)]

        for d in range(owners):
            for t, (kz, y) in enumerate(seats(held(d, 0))):
                for p in range(Q + 1):
                    ref, start = spot(got, lines_in, d, p)
                    lattice[p, kz, pl.ds(y, block), :] = ref[pl.ds(start + t, block, stride=NB), :]

        def bring(chosen, i):
            for d in range(owners):
                for t, (kz, y) in enumerate(seats(held(d, other))):
                    for p in chosen:
                        ref, start = spot(got, lines_in, d, p)
                        lattice[p, kz, pl.ds(y + i * PLANE_ROWS, PLANE_ROWS), :] = ref[
                            pl.ds(start + i * PLANE + t, PLANE_ROWS, stride=NB), :
                        ]

        @pl.when(first)
        def _():
            bring(UPWARD, 0)

        @pl.when(last)
        def _():
            bring(DOWNWARD, planes - 1)

        lane = lax.broadcasted_iota(jnp.int32, (rows, LANES), 1)
        row = lax.broadcasted_iota(jnp.int32, (rows, LANES), 0)

        def passed(pair, p):
            cx, cy, cz = VELOCITIES[p]
            if cy:
                pair = [shift_y(value, cy, lane, row, block) for value in pair]
            if cz:
                pair = [shift_z(pair[kz], pair[1 - kz], cz, lane) for kz in range(NB)]
            return pair

        for p in range(Q):
            pair = passed([lattice[p, kz] for kz in range(NB)], p)
            for kz in range(NB):
                ready[p, kz] = pair[kz]
        for kz in range(NB):
            for start in range(0, rows, 16):
                here = pl.ds(start, 16)
                after = collide(
                    [ready[p, kz, here, :] for p in range(Q)], lattice[Q, kz, here, :] > 0.5
                )
                for p in range(Q):
                    lattice[p, kz, here, :] = after[p]
        for p in range(Q):
            pair = passed([lattice[p, kz] for kz in range(NB)], p)
            for kz in range(NB):
                ready[p, kz] = pair[kz]
        for d in range(owners):
            for t, (kz, y) in enumerate(seats(final(d, 0))):
                for p in range(Q):
                    ref, start = spot(outs, lines_out, d, p)
                    ref[pl.ds(start + t, block, stride=NB), :] = ready[p, kz, pl.ds(y, block), :]

        def bring_back(chosen, i):
            for d in range(owners):
                for t, (kz, y) in enumerate(seats(final(d, other))):
                    for p in chosen:
                        ref, start = spot(outs, lines_out, d, p)
                        ref[pl.ds(start + i * PLANE + t, PLANE_ROWS, stride=NB), :] = ready[
                            p, kz, pl.ds(y + i * PLANE_ROWS, PLANE_ROWS), :
                        ]

        @pl.when(last)
        def _():
            bring_back(UPWARD, planes - 1)

        @pl.when(first)
        def _():
            bring_back(DOWNWARD, 0)

    def crossing_kernel(*refs):
        got, (near, far, up, down) = refs[:owners], refs[owners:]
        me, odd = position()
        for d in range(owners):
            place = dynamic_place(me ^ d, odd, owners)

            @pl.when(place == owners - 1)
            def _():
                for n, p in enumerate(UPWARD):
                    ref, start = spot(got, lines_out, d, p)
                    up[pl.ds(n * PLANE, PLANE), :] = ref[pl.ds(start + share - PLANE, PLANE), :]

            @pl.when(place == 0)
            def _():
                for n, p in enumerate(DOWNWARD):
                    ref, start = spot(got, lines_out, d, p)
                    down[pl.ds(n * PLANE, PLANE), :] = ref[pl.ds(start, PLANE), :]

        for out in (up, down):
            out[pl.ds(faces, 4), :] = jnp.zeros((4, LANES), f32)
        send_sides(odd, up, down, near, far)

    def unpack_kernel(*refs):
        *got, main = refs
        me, odd = position()
        for d in range(owners):
            place = dynamic_place(me ^ d, odd, owners)
            here = pl.multiple_of(place * share, min(share, 8))
            for p in range(Q):
                cx = VELOCITIES[p][0]
                ref, start = spot(got, lines_out, d, p)
                main[p, pl.ds(8 + here + cx * PLANE, share), :] = ref[pl.ds(start, share), :]

    def finish_kernel(main, near, far, out):
        below, above = sides(position()[1], near, far)
        for p in range(Q):
            out[pl.ds(p * WHOLE, WHOLE), :] = main[p, pl.ds(8, WHOLE), :]
        for n, p in enumerate(UPWARD):
            out[pl.ds(p * WHOLE, PLANE), :] = below[n * PLANE : (n + 1) * PLANE]
        for n, p in enumerate(DOWNWARD):
            out[pl.ds(p * WHOLE + WHOLE - PLANE, PLANE), :] = above[n * PLANE : (n + 1) * PLANE]

    def shape(*dims):
        return jax.ShapeDtypeStruct(dims, f32)

    def call(kernel, name, out_shape, inputs, cost, scratch=(), spec=VMEM_SPEC, limit=40):
        outs = jax.tree.map(lambda _: VMEM_SPEC, out_shape)
        return pl.pallas_call(
            kernel,
            out_shape=out_shape,
            in_specs=[spec] * len(inputs),
            out_specs=outs,
            scratch_shapes=list(scratch),
            compiler_params=pltpu.CompilerParams(vmem_limit_bytes=limit * 1024 * 1024),
            cost_estimate=pl.CostEstimate(flops=cost, bytes_accessed=cost, transcendentals=0),
            name=name,
        )(*inputs)

    def exchange(parts, lines):
        return [
            part if d == 0 else lax.ppermute(part, "gx", [(g, g ^ d) for g in range(owners)])
            for part, (d, kind) in zip(parts, lines)
        ]

    def shapes(lines, sizes):
        return tuple(shape(sizes[kind], LANES) for d, kind in lines)

    def hop(near, far):
        ahead = [(s + 1) % slabs if s % 2 == 0 else (s - 1) % slabs for s in range(slabs)]
        behind = [(s - 1) % slabs if s % 2 == 0 else (s + 1) % slabs for s in range(slabs)]
        return (
            lax.ppermute(near, "gy", list(enumerate(ahead))),
            lax.ppermute(far, "gy", list(enumerate(behind))),
        )

    def padded(count):
        return shape(count, 8 + WHOLE + 8, LANES)

    work = pltpu.VMEM((Q + 1, NB, rows, LANES), f32)
    small, large = 100_000, 4_000_000

    def shards(populations, solid_mask, slot_blocks, swap_slots):
        tiles = B * B * B // LANES
        pops = populations[0].transpose(1, 0, 2).reshape(Q, NB, tiles, LANES)
        pops = pops.transpose(0, 2, 1, 3).reshape(Q, WHOLE, LANES)
        mask = solid_mask[0].reshape(NB, tiles, LANES).transpose(1, 0, 2).reshape(WHOLE, LANES)
        swaps = swap_slots[0, 0].T
        in_place = pl.BlockSpec(memory_space=pltpu.HBM)
        near, far, own = call(
            edge_kernel,
            "edge_planes",
            (shape(rows_hop, LANES), shape(rows_hop, LANES), shape(8, LANES)),
            (pops, mask, slot_blocks, swaps),
            small,
            (
                pltpu.VMEM((rows_hop, LANES), f32),
                pltpu.VMEM((rows_hop, LANES), f32),
                pltpu.VMEM((2, Q, 8, LANES), f32),
                pltpu.VMEM((2, 8, LANES), jnp.int32),
                pltpu.VMEM(slot_blocks.shape, jnp.int32),
                pltpu.VMEM(swaps.shape, jnp.int32),
                pltpu.SemaphoreType.DMA((6,)),
            ),
            in_place,
            62,
        )
        near, far = hop(near, far)
        post = call(
            collide_kernel,
            "first_collision",
            padded(Q + 1),
            (pops, mask),
            large,
        )
        parts = call(
            pack_kernel, "pack_planes", shapes(lines_in, sizes_in), (post, own, near, far), large
        )
        parts = call(
            middle_kernel,
            "second_step",
            shapes(lines_out, sizes_out),
            exchange(parts, lines_in),
            large,
            (
                work,
                work,
                pltpu.SMEM((owners, 8, LANES), f32),
                pltpu.SemaphoreType.DMA((owners,)),
            ),
        )
        home = exchange(parts, lines_out)
        near, far = call(
            crossing_kernel,
            "crossing_planes",
            (shape(rows_hop, LANES),) * 2,
            home[:owners],
            small,
            (pltpu.VMEM((rows_hop, LANES), f32),) * 2,
        )
        near, far = hop(near, far)
        main = call(unpack_kernel, "unpack_planes", padded(Q), home, large)
        out = call(
            finish_kernel, "finish", shape(Q * WHOLE, LANES), (main, near, far), small
        )
        out = out.reshape(Q, tiles, NB, LANES).transpose(0, 2, 1, 3)
        return out.reshape(Q, NB, B * B * B).transpose(1, 0, 2)[None]

    return shards


def solution(mesh):
    return jax.shard_map(
        build(mesh),
        mesh=mesh,
        in_specs=(
            P("gy", "gx", None, None),
            P("gy", "gx", None),
            P("gy", "gx"),
            P("gy", "gx", None, None),
        ),
        out_specs=P("gy", "gx", None, None),
        check_vma=False,
    )
```

```python
import jax
import jax.numpy as jnp
from jax import lax
from jax.experimental import pallas as pl
from jax.experimental.pallas import tpu as pltpu
from jax.sharding import PartitionSpec as P

B = 16
NB = 2
LANES = 128
PLANE_ROWS = B * B // LANES
PLANE = PLANE_ROWS * NB
WHOLE = B * PLANE

VELOCITIES = (
    (0, 0, 0),
    (1, 0, 0),
    (-1, 0, 0),
    (0, 1, 0),
    (0, -1, 0),
    (0, 0, 1),
    (0, 0, -1),
    (1, 1, 0),
    (-1, -1, 0),
    (1, -1, 0),
    (-1, 1, 0),
    (1, 0, 1),
    (-1, 0, -1),
    (1, 0, -1),
    (-1, 0, 1),
    (0, 1, 1),
    (0, -1, -1),
    (0, 1, -1),
    (0, -1, 1),
)
OPPOSITE = (0, 2, 1, 4, 3, 6, 5, 8, 7, 10, 9, 12, 11, 14, 13, 16, 15, 18, 17)
Q = len(VELOCITIES)
UPWARD = tuple(p for p in range(Q) if VELOCITIES[p][0] == 1)
DOWNWARD = tuple(p for p in range(Q) if VELOCITIES[p][0] == -1)

VMEM_SPEC = pl.BlockSpec(memory_space=pltpu.VMEM)


def dynamic_place(owner, odd_slab, owners):
    pair, core = owner // 2, owner % 2
    forward = 2 * pair + jnp.where(pair % 2 == 0, core, 1 - core)
    return jnp.where(odd_slab == 1, owners - 1 - forward, forward)


def collide(f, fluid):
    def pair(p):
        return f[p] + f[p + 1], f[p] - f[p + 1]

    sx, dx = pair(1)
    sy, dy = pair(3)
    sz, dz = pair(5)
    sxy_a, dxy_a = pair(7)
    sxy_b, dxy_b = pair(9)
    sxz_a, dxz_a = pair(11)
    sxz_b, dxz_b = pair(13)
    syz_a, dyz_a = pair(15)
    syz_b, dyz_b = pair(17)
    axy, bxy = sxy_a + sxy_b, sxy_a - sxy_b
    axz, bxz = sxz_a + sxz_b, sxz_a - sxz_b
    ayz, byz = syz_a + syz_b, syz_a - syz_b
    rho = f[0] + sx + sy + sz + axy + axz + ayz
    ox = dxy_a + dxy_b + dxz_a + dxz_b
    oy = dxy_a - dxy_b + dyz_a + dyz_b
    oz = dxz_a - dxz_b + dyz_a - dyz_b
    jx, jy, jz = dx + ox, dy + oy, dz + oz
    jxx, jyy, jzz = jx * jx, jy * jy, jz * jz
    base = rho * (1.3 / 9.0)
    wide = 1.3 / 3.0
    thin = 1.3 / 6.0
    axy1 = base - 0.3 * axy + wide * (jxx + jyy) - thin * jzz
    axz1 = base - 0.3 * axz + wide * (jxx + jzz) - thin * jyy
    ayz1 = base - 0.3 * ayz + wide * (jyy + jzz) - thin * jxx
    bxy1 = 1.25 * (jx * jy) - 0.25 * bxy
    bxz1 = 1.25 * (jx * jz) - 0.25 * bxz
    byz1 = 1.25 * (jy * jz) - 0.25 * byz
    third = rho * (1.25 / 3.0)
    sx1 = third + 1.25 * jxx - 0.25 * (sx + axy + axz) - axy1 - axz1
    sy1 = third + 1.25 * jyy - 0.25 * (sy + axy + ayz) - axy1 - ayz1
    sz1 = third + 1.25 * jzz - 0.25 * (sz + axz + ayz) - axz1 - ayz1
    rest = rho - sx1 - sy1 - sz1 - axy1 - axz1 - ayz1

    def split(even, odd):
        return 0.5 * (even + odd), 0.5 * (even - odd)

    def diagonal(a1, b1, d_a, d_b, j_first, j_second):
        plus = 0.25 * (j_first + j_second) - 0.5 * d_a
        minus = 0.25 * (j_first - j_second) - 0.5 * d_b
        return split(0.5 * (a1 + b1), plus) + split(0.5 * (a1 - b1), minus)

    relaxed = (
        (rest,)
        + split(sx1, 0.5 * ox)
        + split(sy1, 0.5 * oy)
        + split(sz1, 0.5 * oz)
        + diagonal(axy1, bxy1, dxy_a, dxy_b, jx, jy)
        + diagonal(axz1, bxz1, dxz_a, dxz_b, jx, jz)
        + diagonal(ayz1, byz1, dyz_a, dyz_b, jy, jz)
    )
    return [jnp.where(fluid, relaxed[p], f[OPPOSITE[p]]) for p in range(Q)]


def shift_y(value, step, lane, row, block):
    rows = value.shape[0]
    turned = pltpu.roll(value, B if step == 1 else LANES - B, 1)
    if step == 1:
        edge, start = lane < B, row % PLANE_ROWS == 0
        near, far = pltpu.roll(turned, 1, 0), pltpu.roll(turned, block - 1, 0)
    else:
        edge, start = lane >= LANES - B, row % PLANE_ROWS == PLANE_ROWS - 1
        near, far = pltpu.roll(turned, rows - 1, 0), pltpu.roll(turned, rows - block + 1, 0)
    return jnp.where(edge, jnp.where(start, far, near), turned)


def shift_z(value, other, step, lane):
    if step == 1:
        return jnp.where(
            lane % B == 0, pltpu.roll(other, LANES - (B - 1), 1), pltpu.roll(value, 1, 1)
        )
    return jnp.where(
        lane % B == B - 1, pltpu.roll(other, B - 1, 1), pltpu.roll(value, LANES - 1, 1)
    )


def build(mesh):
    owners, slabs = mesh.shape["gx"], mesh.shape["gy"]
    planes = B // owners
    share = planes * PLANE
    block = planes * PLANE_ROWS
    rows = owners * block
    head = (Q + 1) * share
    rows_in = head + 8
    rows_out = Q * share
    faces = len(UPWARD) * PLANE
    rows_hop = faces + 4
    f32 = jnp.float32

    half = owners // 2
    spare = [*range(half + 2, owners), *range(4, half), 1]
    order_in = [0, half, 2, half + 1, 3, *spare]
    order_out = [0, half, 2, half + 1, 3, *spare]

    def by_owner(refs, order):
        return [refs[order.index(d)] for d in range(owners)]

    def position():
        me = lax.axis_index("gx")
        return me, lax.axis_index("gy") % 2

    def sides(odd, near, far):
        return (
            jnp.where(odd == 1, near[...], far[...]),
            jnp.where(odd == 1, far[...], near[...]),
        )

    def send_sides(odd, up, down, near, far):
        near[...] = jnp.where(odd == 1, down[...], up[...])
        far[...] = jnp.where(odd == 1, up[...], down[...])

    def edge_kernel(pops, mask, slots, swaps, near, far, own, up, down, cells, solid, held, given, sem):
        ends = (WHOLE - 8, 0)
        copies = []
        for n, start in enumerate(ends):
            copies.append((pops.at[:, pl.ds(start, 8), :], cells.at[n]))
            copies.append((mask.at[pl.ds(start, 8), :], solid.at[n]))
        copies += [(slots, held), (swaps, given)]
        copies = [
            pltpu.make_async_copy(source, target, sem.at[n])
            for n, (source, target) in enumerate(copies)
        ]
        for copy in copies:
            copy.start()
        for copy in copies:
            copy.wait()
        own[...] = jnp.zeros((8, LANES), f32)
        own[0:1, 0:NB] = held[...].astype(f32)
        own[1:2, 0:3] = given[0:1].astype(f32)
        for n, (out, chosen, inside) in enumerate(((up, UPWARD, 8 - PLANE), (down, DOWNWARD, 0))):
            after = collide([cells[n, p] for p in range(Q)], solid[n] > 0)
            for m, p in enumerate(chosen):
                out[pl.ds(m * PLANE, PLANE), :] = after[p][inside : inside + PLANE]
            out[pl.ds(faces, 4), :] = own[0:4]
        send_sides(position()[1], up, down, near, far)

    def collide_kernel(cells, solid, post):
        for start in range(0, WHOLE, 8):
            here = pl.ds(start, 8)
            after = collide([cells[p, here, :] for p in range(Q)], solid[here, :] > 0)
            for p in range(Q):
                post[p, pl.ds(8 + start, 8), :] = after[p]
            post[Q, pl.ds(8 + start, 8), :] = solid[here, :].astype(f32)

    def pack_kernel(post, own, near, far, *outs):
        me, odd = position()
        below, above = sides(odd, near, far)
        outs = by_owner(outs, order_in)
        for d in range(owners):
            out = outs[d]
            place = dynamic_place(me ^ d, odd, owners)
            here = pl.multiple_of(place * share, min(share, 8))
            for p in range(Q + 1):
                cx = VELOCITIES[p][0] if p < Q else 0
                out[pl.ds(p * share, share), :] = post[p, pl.ds(8 + here - cx * PLANE, share), :]
            out[pl.ds(head, 2), :] = own[0:2]
            out[pl.ds(head + 2, 2), :] = below[faces : faces + 2]
            out[pl.ds(head + 4, 2), :] = above[faces : faces + 2]
            out[pl.ds(head + 6, 2), :] = own[2:4]

            @pl.when(place == 0)
            def _():
                for n, p in enumerate(UPWARD):
                    out[pl.ds(p * share, PLANE), :] = below[n * PLANE : (n + 1) * PLANE]

            @pl.when(place == owners - 1)
            def _():
                for n, p in enumerate(DOWNWARD):
                    out[pl.ds(p * share + share - PLANE, PLANE), :] = above[
                        n * PLANE : (n + 1) * PLANE
                    ]

    def seats(blocks):
        return [(b % NB, pl.multiple_of((b // NB) * block, block)) for b in blocks]

    def place_in(d, blocks, message, lattice):
        for t, (kz, y) in enumerate(seats(blocks)):
            for p in range(Q + 1):
                lattice[p, kz, pl.ds(y, block), :] = message[
                    pl.ds(p * share + t, block, stride=NB), :
                ]

    early = [0, half, 2, 3]
    late = [d for d in order_in if d not in early]

    def early_kernel(*refs):
        *got, lattice, table, sem = refs
        copies = [
            pltpu.make_async_copy(ref.at[pl.ds(head, 8), :], table.at[n], sem.at[n])
            for n, ref in enumerate(got)
        ]
        for copy in copies:
            copy.start()
        for copy in copies:
            copy.wait()
        for n, d in enumerate(early):
            blocks = [table[n, 0, t].astype(jnp.int32) for t in range(NB)]
            place_in(d, blocks, got[n], lattice)

    def middle_kernel(*refs):
        got = by_owner(refs[:owners], order_in)
        lattice = refs[owners]
        outs = by_owner(refs[owners + 1 : 2 * owners + 1], order_out)
        _, ready, table, sem = refs[2 * owners + 1 :]
        me, odd = position()
        place = dynamic_place(me, odd, owners)
        first, last = place == 0, place == owners - 1
        copies = [
            pltpu.make_async_copy(got[d].at[pl.ds(head, 8), :], table.at[d], sem.at[d])
            for d in range(owners)
        ]
        for copy in copies:
            copy.start()
        for copy in copies:
            copy.wait()

        def number(d, row, column):
            return table[d, row, column].astype(jnp.int32)

        other = jnp.where(first, 1, jnp.where(last, 2, 0))

        def held(d, which):
            return [number(d, 2 * which, t) for t in range(NB)]

        def final(d, which):
            def lead(e, r):
                return number(d ^ e, 2 * which + 1, r)

            flip = lead(0, 2) + lead(4, 2) + lead(4, 1) + lead(6, 1) + lead(6, 0) + lead(7, 0)
            one, two = held(d ^ 7, which)
            crossed = flip % 2 == 1
            return [jnp.where(crossed, two, one), jnp.where(crossed, one, two)]

        for d in late:
            place_in(d, held(d, 0), got[d], lattice)

        def bring(chosen, i):
            for d in range(owners):
                for t, (kz, y) in enumerate(seats(held(d, other))):
                    for p in chosen:
                        lattice[p, kz, pl.ds(y + i * PLANE_ROWS, PLANE_ROWS), :] = got[d][
                            pl.ds(p * share + i * PLANE + t, PLANE_ROWS, stride=NB), :
                        ]

        @pl.when(first)
        def _():
            bring(UPWARD, 0)

        @pl.when(last)
        def _():
            bring(DOWNWARD, planes - 1)

        lane = lax.broadcasted_iota(jnp.int32, (rows, LANES), 1)
        row = lax.broadcasted_iota(jnp.int32, (rows, LANES), 0)

        def passed(pair, p):
            cx, cy, cz = VELOCITIES[p]
            if cy:
                pair = [shift_y(value, cy, lane, row, block) for value in pair]
            if cz:
                pair = [shift_z(pair[kz], pair[1 - kz], cz, lane) for kz in range(NB)]
            return pair

        for p in range(Q):
            pair = passed([lattice[p, kz] for kz in range(NB)], p)
            for kz in range(NB):
                ready[p, kz] = pair[kz]
        for kz in range(NB):
            for start in range(0, rows, 16):
                here = pl.ds(start, 16)
                after = collide(
                    [ready[p, kz, here, :] for p in range(Q)], lattice[Q, kz, here, :] > 0.5
                )
                for p in range(Q):
                    lattice[p, kz, here, :] = after[p]
        for p in range(Q):
            pair = passed([lattice[p, kz] for kz in range(NB)], p)
            for kz in range(NB):
                ready[p, kz] = pair[kz]
        for d in range(owners):
            for t, (kz, y) in enumerate(seats(final(d, 0))):
                for p in range(Q):
                    outs[d][pl.ds(p * share + t, block, stride=NB), :] = ready[
                        p, kz, pl.ds(y, block), :
                    ]

        def bring_back(chosen, i):
            for d in range(owners):
                for t, (kz, y) in enumerate(seats(final(d, other))):
                    for p in chosen:
                        outs[d][
                            pl.ds(p * share + i * PLANE + t, PLANE_ROWS, stride=NB), :
                        ] = ready[p, kz, pl.ds(y + i * PLANE_ROWS, PLANE_ROWS), :]

        @pl.when(last)
        def _():
            bring_back(UPWARD, planes - 1)

        @pl.when(first)
        def _():
            bring_back(DOWNWARD, 0)

    def crossing_kernel(*refs):
        got = by_owner(refs[:owners], order_out)
        near, far, up, down = refs[owners:]
        me, odd = position()
        for d in range(owners):
            place = dynamic_place(me ^ d, odd, owners)

            @pl.when(place == owners - 1)
            def _():
                for n, p in enumerate(UPWARD):
                    up[pl.ds(n * PLANE, PLANE), :] = got[d][
                        pl.ds(p * share + share - PLANE, PLANE), :
                    ]

            @pl.when(place == 0)
            def _():
                for n, p in enumerate(DOWNWARD):
                    down[pl.ds(n * PLANE, PLANE), :] = got[d][pl.ds(p * share, PLANE), :]

        for out in (up, down):
            out[pl.ds(faces, 4), :] = jnp.zeros((4, LANES), f32)
        send_sides(odd, up, down, near, far)

    ends = [(p, 0) for p in UPWARD] + [(p, WHOLE - 8) for p in DOWNWARD]

    def unpack_kernel(*refs):
        got, (out, edge, main, sem) = by_owner(refs[:owners], order_out), refs[owners:]
        me, odd = position()
        for d in range(owners):
            place = dynamic_place(me ^ d, odd, owners)
            here = pl.multiple_of(place * share, min(share, 8))
            for p in range(Q):
                cx = VELOCITIES[p][0]
                main[p, pl.ds(8 + here + cx * PLANE, share), :] = got[d][
                    pl.ds(p * share, share), :
                ]
        copy = pltpu.make_async_copy(main.at[:, pl.ds(8, WHOLE), :], out, sem.at[0])
        copy.start()
        for n, (p, start) in enumerate(ends):
            edge[n] = main[p, pl.ds(8 + start, 8), :]
        copy.wait()

    def finish_kernel(_, edge, near, far, out, patch, sem):
        below, above = sides(position()[1], near, far)
        for n in range(len(ends)):
            patch[n] = edge[n]
        for n in range(len(UPWARD)):
            patch[n, pl.ds(0, PLANE), :] = below[n * PLANE : (n + 1) * PLANE]
            patch[len(UPWARD) + n, pl.ds(8 - PLANE, PLANE), :] = above[n * PLANE : (n + 1) * PLANE]
        copies = [
            pltpu.make_async_copy(patch.at[n], out.at[p, pl.ds(start, 8), :], sem.at[n])
            for n, (p, start) in enumerate(ends)
        ]
        for copy in copies:
            copy.start()
        for copy in copies:
            copy.wait()

    def shape(*dims):
        return jax.ShapeDtypeStruct(dims, f32)

    def call(
        kernel,
        name,
        out_shape,
        inputs,
        cost,
        scratch=(),
        spec=VMEM_SPEC,
        limit=40,
        aliases=None,
        out_specs=None,
    ):
        outs = out_specs or jax.tree.map(lambda _: VMEM_SPEC, out_shape)
        specs = spec if isinstance(spec, tuple) else (spec,) * len(inputs)
        return pl.pallas_call(
            kernel,
            out_shape=out_shape,
            in_specs=specs,
            out_specs=outs,
            scratch_shapes=list(scratch),
            input_output_aliases=aliases or {},
            compiler_params=pltpu.CompilerParams(vmem_limit_bytes=limit * 1024 * 1024),
            cost_estimate=pl.CostEstimate(flops=cost, bytes_accessed=cost, transcendentals=0),
            name=name,
        )(*inputs)

    def exchange(parts, order):
        return [parts[0]] + [
            lax.ppermute(parts[n], "gx", [(g, g ^ order[n]) for g in range(owners)])
            for n in range(1, owners)
        ]

    def hop(near, far):
        ahead = [(s + 1) % slabs if s % 2 == 0 else (s - 1) % slabs for s in range(slabs)]
        behind = [(s - 1) % slabs if s % 2 == 0 else (s + 1) % slabs for s in range(slabs)]
        return (
            lax.ppermute(near, "gy", list(enumerate(ahead))),
            lax.ppermute(far, "gy", list(enumerate(behind))),
        )

    def padded(count):
        return shape(count, 8 + WHOLE + 8, LANES)

    whole_lattice = (Q + 1, NB, rows, LANES)
    small, large = 100_000, 4_000_000

    def shards(populations, solid_mask, slot_blocks, swap_slots):
        tiles = B * B * B // LANES
        pops = populations[0].transpose(1, 0, 2).reshape(Q, NB, tiles, LANES)
        pops = pops.transpose(0, 2, 1, 3).reshape(Q, WHOLE, LANES)
        mask = solid_mask[0].reshape(NB, tiles, LANES).transpose(1, 0, 2).reshape(WHOLE, LANES)
        swaps = swap_slots[0, 0].T
        in_place = pl.BlockSpec(memory_space=pltpu.HBM)
        near, far, own = call(
            edge_kernel,
            "edge_planes",
            (shape(rows_hop, LANES), shape(rows_hop, LANES), shape(8, LANES)),
            (pops, mask, slot_blocks, swaps),
            small,
            (
                pltpu.VMEM((rows_hop, LANES), f32),
                pltpu.VMEM((rows_hop, LANES), f32),
                pltpu.VMEM((2, Q, 8, LANES), f32),
                pltpu.VMEM((2, 8, LANES), jnp.int32),
                pltpu.VMEM(slot_blocks.shape, jnp.int32),
                pltpu.VMEM(swaps.shape, jnp.int32),
                pltpu.SemaphoreType.DMA((6,)),
            ),
            in_place,
            62,
        )
        near, far = hop(near, far)
        post = call(
            collide_kernel,
            "first_collision",
            padded(Q + 1),
            (pops, mask),
            large,
        )
        parts = call(
            pack_kernel,
            "pack_planes",
            (shape(rows_in, LANES),) * owners,
            (post, own, near, far),
            large,
        )
        got = exchange(parts, order_in)
        lattice = call(
            early_kernel,
            "place_early",
            shape(*whole_lattice),
            [got[order_in.index(d)] for d in early],
            large,
            (pltpu.SMEM((len(early), 8, LANES), f32), pltpu.SemaphoreType.DMA((len(early),))),
        )
        *parts, _ = call(
            middle_kernel,
            "second_step",
            (shape(rows_out, LANES),) * owners + (shape(*whole_lattice),),
            (*got, lattice),
            large,
            (
                pltpu.VMEM(whole_lattice, f32),
                pltpu.SMEM((owners, 8, LANES), f32),
                pltpu.SemaphoreType.DMA((owners,)),
            ),
            aliases={owners: owners},
        )
        home = exchange(parts, order_out)
        near, far = call(
            crossing_kernel,
            "crossing_planes",
            (shape(rows_hop, LANES),) * 2,
            home,
            small,
            (pltpu.VMEM((rows_hop, LANES), f32),) * 2,
        )
        near, far = hop(near, far)
        out, edge = call(
            unpack_kernel,
            "unpack_planes",
            (shape(Q, WHOLE, LANES), shape(len(ends), 8, LANES)),
            home,
            large,
            (pltpu.VMEM((Q, 8 + WHOLE + 8, LANES), f32), pltpu.SemaphoreType.DMA((1,))),
            out_specs=(in_place, VMEM_SPEC),
        )
        out = call(
            finish_kernel,
            "finish",
            shape(Q, WHOLE, LANES),
            (out, edge, near, far),
            small,
            (pltpu.VMEM((len(ends), 8, LANES), f32), pltpu.SemaphoreType.DMA((len(ends),))),
            spec=(in_place, VMEM_SPEC, VMEM_SPEC, VMEM_SPEC),
            aliases={0: 0},
            out_specs=in_place,
        )
        out = out.reshape(Q, tiles, NB, LANES).transpose(0, 2, 1, 3)
        return out.reshape(Q, NB, B * B * B).transpose(1, 0, 2)[None]

    return shards


def solution(mesh):
    return jax.shard_map(
        build(mesh),
        mesh=mesh,
        in_specs=(
            P("gy", "gx", None, None),
            P("gy", "gx", None),
            P("gy", "gx"),
            P("gy", "gx", None, None),
        ),
        out_specs=P("gy", "gx", None, None),
        check_vma=False,
    )
```

```python
import jax
import jax.numpy as jnp
from jax import lax
from jax.experimental import pallas as pl
from jax.experimental.pallas import tpu as pltpu
from jax.sharding import PartitionSpec as P

B = 16
NB = 2
LANES = 128
PLANE_ROWS = B * B // LANES
PLANE = PLANE_ROWS * NB
FIELDS = NB + 3
WHOLE = B * PLANE

VELOCITIES = (
    (0, 0, 0),
    (1, 0, 0),
    (-1, 0, 0),
    (0, 1, 0),
    (0, -1, 0),
    (0, 0, 1),
    (0, 0, -1),
    (1, 1, 0),
    (-1, -1, 0),
    (1, -1, 0),
    (-1, 1, 0),
    (1, 0, 1),
    (-1, 0, -1),
    (1, 0, -1),
    (-1, 0, 1),
    (0, 1, 1),
    (0, -1, -1),
    (0, 1, -1),
    (0, -1, 1),
)
OPPOSITE = (0, 2, 1, 4, 3, 6, 5, 8, 7, 10, 9, 12, 11, 14, 13, 16, 15, 18, 17)
Q = len(VELOCITIES)
UPWARD = tuple(p for p in range(Q) if VELOCITIES[p][0] == 1)
DOWNWARD = tuple(p for p in range(Q) if VELOCITIES[p][0] == -1)

VMEM_SPEC = pl.BlockSpec(memory_space=pltpu.VMEM)


def dynamic_place(owner, odd_slab, owners):
    pair, core = owner // 2, owner % 2
    forward = 2 * pair + jnp.where(pair % 2 == 0, core, 1 - core)
    return jnp.where(odd_slab == 1, owners - 1 - forward, forward)


def collide(f, fluid):
    def pair(p):
        return f[p] + f[p + 1], f[p] - f[p + 1]

    sx, dx = pair(1)
    sy, dy = pair(3)
    sz, dz = pair(5)
    sxy_a, dxy_a = pair(7)
    sxy_b, dxy_b = pair(9)
    sxz_a, dxz_a = pair(11)
    sxz_b, dxz_b = pair(13)
    syz_a, dyz_a = pair(15)
    syz_b, dyz_b = pair(17)
    axy, bxy = sxy_a + sxy_b, sxy_a - sxy_b
    axz, bxz = sxz_a + sxz_b, sxz_a - sxz_b
    ayz, byz = syz_a + syz_b, syz_a - syz_b
    rho = f[0] + sx + sy + sz + axy + axz + ayz
    ox = dxy_a + dxy_b + dxz_a + dxz_b
    oy = dxy_a - dxy_b + dyz_a + dyz_b
    oz = dxz_a - dxz_b + dyz_a - dyz_b
    jx, jy, jz = dx + ox, dy + oy, dz + oz
    jxx, jyy, jzz = jx * jx, jy * jy, jz * jz
    base = rho * (1.3 / 9.0)
    wide = 1.3 / 3.0
    thin = 1.3 / 6.0
    axy1 = base - 0.3 * axy + wide * (jxx + jyy) - thin * jzz
    axz1 = base - 0.3 * axz + wide * (jxx + jzz) - thin * jyy
    ayz1 = base - 0.3 * ayz + wide * (jyy + jzz) - thin * jxx
    bxy1 = 1.25 * (jx * jy) - 0.25 * bxy
    bxz1 = 1.25 * (jx * jz) - 0.25 * bxz
    byz1 = 1.25 * (jy * jz) - 0.25 * byz
    third = rho * (1.25 / 3.0)
    sx1 = third + 1.25 * jxx - 0.25 * (sx + axy + axz) - axy1 - axz1
    sy1 = third + 1.25 * jyy - 0.25 * (sy + axy + ayz) - axy1 - ayz1
    sz1 = third + 1.25 * jzz - 0.25 * (sz + axz + ayz) - axz1 - ayz1
    rest = rho - sx1 - sy1 - sz1 - axy1 - axz1 - ayz1

    def split(even, odd):
        return 0.5 * (even + odd), 0.5 * (even - odd)

    def diagonal(a1, b1, d_a, d_b, j_first, j_second):
        plus = 0.25 * (j_first + j_second) - 0.5 * d_a
        minus = 0.25 * (j_first - j_second) - 0.5 * d_b
        return split(0.5 * (a1 + b1), plus) + split(0.5 * (a1 - b1), minus)

    relaxed = (
        (rest,)
        + split(sx1, 0.5 * ox)
        + split(sy1, 0.5 * oy)
        + split(sz1, 0.5 * oz)
        + diagonal(axy1, bxy1, dxy_a, dxy_b, jx, jy)
        + diagonal(axz1, bxz1, dxz_a, dxz_b, jx, jz)
        + diagonal(ayz1, byz1, dyz_a, dyz_b, jy, jz)
    )
    return [jnp.where(fluid, relaxed[p], f[OPPOSITE[p]]) for p in range(Q)]


def shift_y(value, step, lane, row, block):
    rows = value.shape[0]
    turned = pltpu.roll(value, B if step == 1 else LANES - B, 1)
    if step == 1:
        edge, start = lane < B, row % PLANE_ROWS == 0
        near, far = pltpu.roll(turned, 1, 0), pltpu.roll(turned, block - 1, 0)
    else:
        edge, start = lane >= LANES - B, row % PLANE_ROWS == PLANE_ROWS - 1
        near, far = pltpu.roll(turned, rows - 1, 0), pltpu.roll(turned, rows - block + 1, 0)
    return jnp.where(edge, jnp.where(start, far, near), turned)


def shift_z(value, other, step, lane):
    if step == 1:
        return jnp.where(
            lane % B == 0, pltpu.roll(other, LANES - (B - 1), 1), pltpu.roll(value, 1, 1)
        )
    return jnp.where(
        lane % B == B - 1, pltpu.roll(other, B - 1, 1), pltpu.roll(value, LANES - 1, 1)
    )


def build(mesh):
    owners, slabs = mesh.shape["gx"], mesh.shape["gy"]
    planes = B // owners
    share = planes * PLANE
    block = planes * PLANE_ROWS
    rows = owners * block
    head = (Q + 1) * share
    rows_in = head + 8
    rows_out = Q * share
    faces = len(UPWARD) * PLANE
    rows_hop = faces + 4
    f32 = jnp.float32

    half = owners // 2
    spare = [*range(half + 2, owners), *range(4, half), 1]
    order_in = [0, half, 2, half + 1, 3, *spare]
    order_out = [0, half, 2, half + 1, 3, *spare]

    def by_owner(refs, order):
        return [refs[order.index(d)] for d in range(owners)]

    def position():
        me = lax.axis_index("gx")
        return me, lax.axis_index("gy") % 2

    def sides(odd, near, far):
        return (
            jnp.where(odd == 1, near[...], far[...]),
            jnp.where(odd == 1, far[...], near[...]),
        )

    def send_sides(odd, up, down, near, far):
        near[...] = jnp.where(odd == 1, down[...], up[...])
        far[...] = jnp.where(odd == 1, up[...], down[...])

    def edge_kernel(pops, mask, slots, swaps, near, far, own, up, down, cells, solid, held, given, sem):
        ends = (WHOLE - 8, 0)
        copies = []
        for n, start in enumerate(ends):
            copies.append((pops.at[:, pl.ds(start, 8), :], cells.at[n]))
            copies.append((mask.at[pl.ds(start, 8), :], solid.at[n]))
        copies += [(slots, held), (swaps, given)]
        copies = [
            pltpu.make_async_copy(source, target, sem.at[n])
            for n, (source, target) in enumerate(copies)
        ]
        for copy in copies:
            copy.start()
        for copy in copies:
            copy.wait()
        own[...] = jnp.zeros((8, LANES), f32)
        own[4:5, 0:NB] = held[...].astype(f32)
        own[5:6, 0:3] = given[0:1].astype(f32)
        lane = lax.broadcasted_iota(jnp.int32, (8, LANES), 1)
        swaps_beside = pltpu.roll(pltpu.roll(own[...], NB, 1), 7, 0)
        own[...] = jnp.where(lane < NB, own[...], swaps_beside)
        for n, (out, chosen, inside) in enumerate(((up, UPWARD, 8 - PLANE), (down, DOWNWARD, 0))):
            after = collide([cells[n, p] for p in range(Q)], solid[n] > 0)
            for m, p in enumerate(chosen):
                out[pl.ds(m * PLANE, PLANE), :] = after[p][inside : inside + PLANE]
            out[pl.ds(faces, 4), :] = own[4:8]
        send_sides(position()[1], up, down, near, far)

    def collide_kernel(cells, solid, post):
        for start in range(0, WHOLE, 8):
            here = pl.ds(start, 8)
            after = collide([cells[p, here, :] for p in range(Q)], solid[here, :] > 0)
            for p in range(Q):
                post[p, pl.ds(8 + start, 8), :] = after[p]
            post[Q, pl.ds(8 + start, 8), :] = solid[here, :].astype(f32)

    def pack_kernel(post, own, near, far, *outs):
        me, odd = position()
        below, above = sides(odd, near, far)
        outs = by_owner(outs, order_in)
        lane = lax.broadcasted_iota(jnp.int32, (8, LANES), 1)
        tail_below = pltpu.roll(below[faces - 4 : faces + 4], FIELDS, 1)
        tail_above = pltpu.roll(above[faces - 4 : faces + 4], 2 * FIELDS, 1)
        header = jnp.where(lane < 2 * FIELDS, tail_below, tail_above)
        header = jnp.where(lane < FIELDS, own[...], header)
        for d in range(owners):
            out = outs[d]
            place = dynamic_place(me ^ d, odd, owners)
            here = pl.multiple_of(place * share, min(share, 8))
            for p in range(Q + 1):
                cx = VELOCITIES[p][0] if p < Q else 0
                out[pl.ds(p * share, share), :] = post[p, pl.ds(8 + here - cx * PLANE, share), :]
            out[pl.ds(head, 8), :] = header

            @pl.when(place == 0)
            def _():
                for n, p in enumerate(UPWARD):
                    out[pl.ds(p * share, PLANE), :] = below[n * PLANE : (n + 1) * PLANE]

            @pl.when(place == owners - 1)
            def _():
                for n, p in enumerate(DOWNWARD):
                    out[pl.ds(p * share + share - PLANE, PLANE), :] = above[
                        n * PLANE : (n + 1) * PLANE
                    ]

    def seats(blocks):
        return [(b % NB, pl.multiple_of((b // NB) * block, block)) for b in blocks]

    def place_in(d, blocks, message, lattice):
        for t, (kz, y) in enumerate(seats(blocks)):
            for p in range(Q + 1):
                lattice[p, kz, pl.ds(y, block), :] = message[
                    pl.ds(p * share + t, block, stride=NB), :
                ]

    early = [0, half, 2, 3]
    late = [d for d in order_in if d not in early]

    def early_kernel(*refs):
        *got, lattice, table, sem = refs
        copies = [
            pltpu.make_async_copy(ref.at[pl.ds(head + 4, 1), :], table.at[pl.ds(n, 1), :], sem.at[n])
            for n, ref in enumerate(got)
        ]
        for copy in copies:
            copy.start()
        for copy in copies:
            copy.wait()
        for n, d in enumerate(early):
            blocks = [table[n, t].astype(jnp.int32) for t in range(NB)]
            place_in(d, blocks, got[n], lattice)

    def middle_kernel(*refs):
        got = by_owner(refs[:owners], order_in)
        lattice = refs[owners]
        outs = by_owner(refs[owners + 1 : 2 * owners + 1], order_out)
        _, ready, table, sem = refs[2 * owners + 1 :]
        me, odd = position()
        place = dynamic_place(me, odd, owners)
        first, last = place == 0, place == owners - 1
        copies = [
            pltpu.make_async_copy(
                got[d].at[pl.ds(head + 4, 1), :], table.at[pl.ds(d, 1), :], sem.at[d]
            )
            for d in range(owners)
        ]
        for copy in copies:
            copy.start()
        for copy in copies:
            copy.wait()

        def number(d, which, field):
            return table[d, which * FIELDS + field].astype(jnp.int32)

        other = jnp.where(first, 1, jnp.where(last, 2, 0))

        def held(d, which):
            return [number(d, which, t) for t in range(NB)]

        def final(d, which):
            def lead(e, r):
                return number(d ^ e, which, NB + r)

            flip = lead(0, 2) + lead(4, 2) + lead(4, 1) + lead(6, 1) + lead(6, 0) + lead(7, 0)
            one, two = held(d ^ 7, which)
            crossed = flip % 2 == 1
            return [jnp.where(crossed, two, one), jnp.where(crossed, one, two)]

        for d in late:
            place_in(d, held(d, 0), got[d], lattice)

        def bring(chosen, i):
            for d in range(owners):
                for t, (kz, y) in enumerate(seats(held(d, other))):
                    for p in chosen:
                        lattice[p, kz, pl.ds(y + i * PLANE_ROWS, PLANE_ROWS), :] = got[d][
                            pl.ds(p * share + i * PLANE + t, PLANE_ROWS, stride=NB), :
                        ]

        @pl.when(first)
        def _():
            bring(UPWARD, 0)

        @pl.when(last)
        def _():
            bring(DOWNWARD, planes - 1)

        lane = lax.broadcasted_iota(jnp.int32, (rows, LANES), 1)
        row = lax.broadcasted_iota(jnp.int32, (rows, LANES), 0)

        def passed(pair, p):
            cx, cy, cz = VELOCITIES[p]
            if cy:
                pair = [shift_y(value, cy, lane, row, block) for value in pair]
            if cz:
                pair = [shift_z(pair[kz], pair[1 - kz], cz, lane) for kz in range(NB)]
            return pair

        for p in range(Q):
            pair = passed([lattice[p, kz] for kz in range(NB)], p)
            for kz in range(NB):
                ready[p, kz] = pair[kz]
        for kz in range(NB):
            for start in range(0, rows, 16):
                here = pl.ds(start, 16)
                after = collide(
                    [ready[p, kz, here, :] for p in range(Q)], lattice[Q, kz, here, :] > 0.5
                )
                for p in range(Q):
                    lattice[p, kz, here, :] = after[p]
        for p in range(Q):
            pair = passed([lattice[p, kz] for kz in range(NB)], p)
            for kz in range(NB):
                ready[p, kz] = pair[kz]
        for d in range(owners):
            for t, (kz, y) in enumerate(seats(final(d, 0))):
                for p in range(Q):
                    outs[d][pl.ds(p * share + t, block, stride=NB), :] = ready[
                        p, kz, pl.ds(y, block), :
                    ]

        def bring_back(chosen, i):
            for d in range(owners):
                for t, (kz, y) in enumerate(seats(final(d, other))):
                    for p in chosen:
                        outs[d][
                            pl.ds(p * share + i * PLANE + t, PLANE_ROWS, stride=NB), :
                        ] = ready[p, kz, pl.ds(y + i * PLANE_ROWS, PLANE_ROWS), :]

        @pl.when(last)
        def _():
            bring_back(UPWARD, planes - 1)

        @pl.when(first)
        def _():
            bring_back(DOWNWARD, 0)

    def crossing_kernel(*refs):
        got = by_owner(refs[:owners], order_out)
        near, far, up, down = refs[owners:]
        me, odd = position()
        for d in range(owners):
            place = dynamic_place(me ^ d, odd, owners)

            @pl.when(place == owners - 1)
            def _():
                for n, p in enumerate(UPWARD):
                    up[pl.ds(n * PLANE, PLANE), :] = got[d][
                        pl.ds(p * share + share - PLANE, PLANE), :
                    ]

            @pl.when(place == 0)
            def _():
                for n, p in enumerate(DOWNWARD):
                    down[pl.ds(n * PLANE, PLANE), :] = got[d][pl.ds(p * share, PLANE), :]

        for out in (up, down):
            out[pl.ds(faces, 4), :] = jnp.zeros((4, LANES), f32)
        send_sides(odd, up, down, near, far)

    ends = [(p, 0) for p in UPWARD] + [(p, WHOLE - 8) for p in DOWNWARD]

    def unpack_kernel(*refs):
        got, (out, edge, main, sem) = by_owner(refs[:owners], order_out), refs[owners:]
        me, odd = position()
        for d in range(owners):
            place = dynamic_place(me ^ d, odd, owners)
            here = pl.multiple_of(place * share, min(share, 8))
            for p in range(Q):
                cx = VELOCITIES[p][0]
                main[p, pl.ds(8 + here + cx * PLANE, share), :] = got[d][
                    pl.ds(p * share, share), :
                ]
        copy = pltpu.make_async_copy(main.at[:, pl.ds(8, WHOLE), :], out, sem.at[0])
        copy.start()
        for n, (p, start) in enumerate(ends):
            edge[n] = main[p, pl.ds(8 + start, 8), :]
        copy.wait()

    def finish_kernel(_, edge, near, far, out, patch, sem):
        below, above = sides(position()[1], near, far)
        for n in range(len(ends)):
            patch[n] = edge[n]
        for n in range(len(UPWARD)):
            patch[n, pl.ds(0, PLANE), :] = below[n * PLANE : (n + 1) * PLANE]
            patch[len(UPWARD) + n, pl.ds(8 - PLANE, PLANE), :] = above[n * PLANE : (n + 1) * PLANE]
        copies = [
            pltpu.make_async_copy(patch.at[n], out.at[p, pl.ds(start, 8), :], sem.at[n])
            for n, (p, start) in enumerate(ends)
        ]
        for copy in copies:
            copy.start()
        for copy in copies:
            copy.wait()

    def shape(*dims):
        return jax.ShapeDtypeStruct(dims, f32)

    def call(
        kernel,
        name,
        out_shape,
        inputs,
        cost,
        scratch=(),
        spec=VMEM_SPEC,
        limit=40,
        aliases=None,
        out_specs=None,
    ):
        outs = out_specs or jax.tree.map(lambda _: VMEM_SPEC, out_shape)
        specs = spec if isinstance(spec, tuple) else (spec,) * len(inputs)
        return pl.pallas_call(
            kernel,
            out_shape=out_shape,
            in_specs=specs,
            out_specs=outs,
            scratch_shapes=list(scratch),
            input_output_aliases=aliases or {},
            compiler_params=pltpu.CompilerParams(vmem_limit_bytes=limit * 1024 * 1024),
            cost_estimate=pl.CostEstimate(flops=cost, bytes_accessed=cost, transcendentals=0),
            name=name,
        )(*inputs)

    def exchange(parts, order):
        return [parts[0]] + [
            lax.ppermute(parts[n], "gx", [(g, g ^ order[n]) for g in range(owners)])
            for n in range(1, owners)
        ]

    def hop(near, far):
        ahead = [(s + 1) % slabs if s % 2 == 0 else (s - 1) % slabs for s in range(slabs)]
        behind = [(s - 1) % slabs if s % 2 == 0 else (s + 1) % slabs for s in range(slabs)]
        return (
            lax.ppermute(near, "gy", list(enumerate(ahead))),
            lax.ppermute(far, "gy", list(enumerate(behind))),
        )

    def padded(count):
        return shape(count, 8 + WHOLE + 8, LANES)

    whole_lattice = (Q + 1, NB, rows, LANES)
    small, large = 100_000, 4_000_000

    def shards(populations, solid_mask, slot_blocks, swap_slots):
        tiles = B * B * B // LANES
        pops = populations[0].transpose(1, 0, 2).reshape(Q, NB, tiles, LANES)
        pops = pops.transpose(0, 2, 1, 3).reshape(Q, WHOLE, LANES)
        mask = solid_mask[0].reshape(NB, tiles, LANES).transpose(1, 0, 2).reshape(WHOLE, LANES)
        swaps = swap_slots[0, 0].T
        in_place = pl.BlockSpec(memory_space=pltpu.HBM)
        near, far, own = call(
            edge_kernel,
            "edge_planes",
            (shape(rows_hop, LANES), shape(rows_hop, LANES), shape(8, LANES)),
            (pops, mask, slot_blocks, swaps),
            small,
            (
                pltpu.VMEM((rows_hop, LANES), f32),
                pltpu.VMEM((rows_hop, LANES), f32),
                pltpu.VMEM((2, Q, 8, LANES), f32),
                pltpu.VMEM((2, 8, LANES), jnp.int32),
                pltpu.VMEM(slot_blocks.shape, jnp.int32),
                pltpu.VMEM(swaps.shape, jnp.int32),
                pltpu.SemaphoreType.DMA((6,)),
            ),
            in_place,
            62,
        )
        near, far = hop(near, far)
        post = call(
            collide_kernel,
            "first_collision",
            padded(Q + 1),
            (pops, mask),
            large,
        )
        parts = call(
            pack_kernel,
            "pack_planes",
            (shape(rows_in, LANES),) * owners,
            (post, own, near, far),
            large,
        )
        got = exchange(parts, order_in)
        lattice = call(
            early_kernel,
            "place_early",
            shape(*whole_lattice),
            [got[order_in.index(d)] for d in early],
            large,
            (pltpu.SMEM((len(early), LANES), f32), pltpu.SemaphoreType.DMA((len(early),))),
        )
        *parts, _ = call(
            middle_kernel,
            "second_step",
            (shape(rows_out, LANES),) * owners + (shape(*whole_lattice),),
            (*got, lattice),
            large,
            (
                pltpu.VMEM(whole_lattice, f32),
                pltpu.SMEM((owners, LANES), f32),
                pltpu.SemaphoreType.DMA((owners,)),
            ),
            aliases={owners: owners},
        )
        home = exchange(parts, order_out)
        near, far = call(
            crossing_kernel,
            "crossing_planes",
            (shape(rows_hop, LANES),) * 2,
            home,
            small,
            (pltpu.VMEM((rows_hop, LANES), f32),) * 2,
        )
        near, far = hop(near, far)
        out, edge = call(
            unpack_kernel,
            "unpack_planes",
            (shape(Q, WHOLE, LANES), shape(len(ends), 8, LANES)),
            home,
            large,
            (pltpu.VMEM((Q, 8 + WHOLE + 8, LANES), f32), pltpu.SemaphoreType.DMA((1,))),
            out_specs=(in_place, VMEM_SPEC),
        )
        out = call(
            finish_kernel,
            "finish",
            shape(Q, WHOLE, LANES),
            (out, edge, near, far),
            small,
            (pltpu.VMEM((len(ends), 8, LANES), f32), pltpu.SemaphoreType.DMA((len(ends),))),
            spec=(in_place, VMEM_SPEC, VMEM_SPEC, VMEM_SPEC),
            aliases={0: 0},
            out_specs=in_place,
        )
        out = out.reshape(Q, tiles, NB, LANES).transpose(0, 2, 1, 3)
        return out.reshape(Q, NB, B * B * B).transpose(1, 0, 2)[None]

    return shards


def solution(mesh):
    return jax.shard_map(
        build(mesh),
        mesh=mesh,
        in_specs=(
            P("gy", "gx", None, None),
            P("gy", "gx", None),
            P("gy", "gx"),
            P("gy", "gx", None, None),
        ),
        out_specs=P("gy", "gx", None, None),
        check_vma=False,
    )
```

```python
import jax
import jax.numpy as jnp
from jax import lax
from jax.experimental import pallas as pl
from jax.experimental.pallas import tpu as pltpu
from jax.sharding import PartitionSpec as P

B = 16
NB = 2
LANES = 128
PLANE_ROWS = B * B // LANES
PLANE = PLANE_ROWS * NB
FIELDS = NB + 3
WHOLE = B * PLANE

VELOCITIES = (
    (0, 0, 0),
    (1, 0, 0),
    (-1, 0, 0),
    (0, 1, 0),
    (0, -1, 0),
    (0, 0, 1),
    (0, 0, -1),
    (1, 1, 0),
    (-1, -1, 0),
    (1, -1, 0),
    (-1, 1, 0),
    (1, 0, 1),
    (-1, 0, -1),
    (1, 0, -1),
    (-1, 0, 1),
    (0, 1, 1),
    (0, -1, -1),
    (0, 1, -1),
    (0, -1, 1),
)
OPPOSITE = (0, 2, 1, 4, 3, 6, 5, 8, 7, 10, 9, 12, 11, 14, 13, 16, 15, 18, 17)
Q = len(VELOCITIES)
UPWARD = tuple(p for p in range(Q) if VELOCITIES[p][0] == 1)
DOWNWARD = tuple(p for p in range(Q) if VELOCITIES[p][0] == -1)

VMEM_SPEC = pl.BlockSpec(memory_space=pltpu.VMEM)


def dynamic_place(owner, odd_slab, owners):
    pair, core = owner // 2, owner % 2
    forward = 2 * pair + jnp.where(pair % 2 == 0, core, 1 - core)
    return jnp.where(odd_slab == 1, owners - 1 - forward, forward)


def collide(f, fluid):
    def pair(p):
        return f[p] + f[p + 1], f[p] - f[p + 1]

    sx, dx = pair(1)
    sy, dy = pair(3)
    sz, dz = pair(5)
    sxy_a, dxy_a = pair(7)
    sxy_b, dxy_b = pair(9)
    sxz_a, dxz_a = pair(11)
    sxz_b, dxz_b = pair(13)
    syz_a, dyz_a = pair(15)
    syz_b, dyz_b = pair(17)
    axy, bxy = sxy_a + sxy_b, sxy_a - sxy_b
    axz, bxz = sxz_a + sxz_b, sxz_a - sxz_b
    ayz, byz = syz_a + syz_b, syz_a - syz_b
    rho = f[0] + sx + sy + sz + axy + axz + ayz
    ox = dxy_a + dxy_b + dxz_a + dxz_b
    oy = dxy_a - dxy_b + dyz_a + dyz_b
    oz = dxz_a - dxz_b + dyz_a - dyz_b
    jx, jy, jz = dx + ox, dy + oy, dz + oz
    jxx, jyy, jzz = jx * jx, jy * jy, jz * jz
    base = rho * (1.3 / 9.0)
    wide = 1.3 / 3.0
    thin = 1.3 / 6.0
    axy1 = base - 0.3 * axy + wide * (jxx + jyy) - thin * jzz
    axz1 = base - 0.3 * axz + wide * (jxx + jzz) - thin * jyy
    ayz1 = base - 0.3 * ayz + wide * (jyy + jzz) - thin * jxx
    bxy1 = 1.25 * (jx * jy) - 0.25 * bxy
    bxz1 = 1.25 * (jx * jz) - 0.25 * bxz
    byz1 = 1.25 * (jy * jz) - 0.25 * byz
    third = rho * (1.25 / 3.0)
    sx1 = third + 1.25 * jxx - 0.25 * (sx + axy + axz) - axy1 - axz1
    sy1 = third + 1.25 * jyy - 0.25 * (sy + axy + ayz) - axy1 - ayz1
    sz1 = third + 1.25 * jzz - 0.25 * (sz + axz + ayz) - axz1 - ayz1
    rest = rho - sx1 - sy1 - sz1 - axy1 - axz1 - ayz1

    def split(even, odd):
        return 0.5 * (even + odd), 0.5 * (even - odd)

    def diagonal(a1, b1, d_a, d_b, j_first, j_second):
        plus = 0.25 * (j_first + j_second) - 0.5 * d_a
        minus = 0.25 * (j_first - j_second) - 0.5 * d_b
        return split(0.5 * (a1 + b1), plus) + split(0.5 * (a1 - b1), minus)

    relaxed = (
        (rest,)
        + split(sx1, 0.5 * ox)
        + split(sy1, 0.5 * oy)
        + split(sz1, 0.5 * oz)
        + diagonal(axy1, bxy1, dxy_a, dxy_b, jx, jy)
        + diagonal(axz1, bxz1, dxz_a, dxz_b, jx, jz)
        + diagonal(ayz1, byz1, dyz_a, dyz_b, jy, jz)
    )
    return [jnp.where(fluid, relaxed[p], f[OPPOSITE[p]]) for p in range(Q)]


def shift_y(value, step, lane, row, block):
    rows = value.shape[0]
    turned = pltpu.roll(value, B if step == 1 else LANES - B, 1)
    if step == 1:
        edge, start = lane < B, row % PLANE_ROWS == 0
        near, far = pltpu.roll(turned, 1, 0), pltpu.roll(turned, block - 1, 0)
    else:
        edge, start = lane >= LANES - B, row % PLANE_ROWS == PLANE_ROWS - 1
        near, far = pltpu.roll(turned, rows - 1, 0), pltpu.roll(turned, rows - block + 1, 0)
    return jnp.where(edge, jnp.where(start, far, near), turned)


def shift_z(value, other, step, lane):
    if step == 1:
        return jnp.where(
            lane % B == 0, pltpu.roll(other, LANES - (B - 1), 1), pltpu.roll(value, 1, 1)
        )
    return jnp.where(
        lane % B == B - 1, pltpu.roll(other, B - 1, 1), pltpu.roll(value, LANES - 1, 1)
    )


def build(mesh):
    owners, slabs = mesh.shape["gx"], mesh.shape["gy"]
    planes = B // owners
    share = planes * PLANE
    block = planes * PLANE_ROWS
    rows = owners * block
    head = (Q + 1) * share
    rows_in = head + 8
    rows_out = Q * share
    faces = len(UPWARD) * PLANE
    rows_hop = faces + 4
    f32 = jnp.float32

    half = owners // 2
    spare = [*range(half + 2, owners), *range(4, half), 1]
    order_in = [0, half, 2, half + 1, 3, *spare]
    order_out = [0, half, 2, half + 1, 3, *spare]

    def by_owner(refs, order):
        return [refs[order.index(d)] for d in range(owners)]

    def position():
        me = lax.axis_index("gx")
        return me, lax.axis_index("gy") % 2

    def sides(odd, near, far):
        return (
            jnp.where(odd == 1, near[...], far[...]),
            jnp.where(odd == 1, far[...], near[...]),
        )

    def send_sides(odd, up, down, near, far):
        near[...] = jnp.where(odd == 1, down[...], up[...])
        far[...] = jnp.where(odd == 1, up[...], down[...])

    def edge_kernel(pops, mask, slots, swaps, near, far, own, up, down, cells, solid, held, given, sem):
        ends = (WHOLE - 8, 0)
        copies = []
        for n, start in enumerate(ends):
            copies.append((pops.at[:, pl.ds(start, 8), :], cells.at[n]))
            copies.append((mask.at[pl.ds(start, 8), :], solid.at[n]))
        copies += [(slots, held), (swaps, given)]
        copies = [
            pltpu.make_async_copy(source, target, sem.at[n])
            for n, (source, target) in enumerate(copies)
        ]
        for copy in copies:
            copy.start()
        for copy in copies:
            copy.wait()
        own[...] = jnp.zeros((8, LANES), f32)
        own[4:5, 0:NB] = held[...].astype(f32)
        own[5:6, 0:3] = given[0:1].astype(f32)
        lane = lax.broadcasted_iota(jnp.int32, (8, LANES), 1)
        swaps_beside = pltpu.roll(pltpu.roll(own[...], NB, 1), 7, 0)
        own[...] = jnp.where(lane < NB, own[...], swaps_beside)
        for n, (out, chosen, inside) in enumerate(((up, UPWARD, 8 - PLANE), (down, DOWNWARD, 0))):
            after = collide([cells[n, p] for p in range(Q)], solid[n] > 0)
            for m, p in enumerate(chosen):
                out[pl.ds(m * PLANE, PLANE), :] = after[p][inside : inside + PLANE]
            out[pl.ds(faces, 4), :] = own[4:8]
        send_sides(position()[1], up, down, near, far)

    def collide_kernel(cells, solid, post):
        for start in range(0, WHOLE, 8):
            here = pl.ds(start, 8)
            after = collide([cells[p, here, :] for p in range(Q)], solid[here, :] > 0)
            for p in range(Q):
                post[p, pl.ds(8 + start, 8), :] = after[p]
            post[Q, pl.ds(8 + start, 8), :] = solid[here, :].astype(f32)

    def pack_kernel(post, own, far, near, *outs):
        me, odd = position()
        below, above = sides(odd, near, far)
        outs = by_owner(outs, order_in)
        lane = lax.broadcasted_iota(jnp.int32, (8, LANES), 1)
        tail_below = pltpu.roll(below[faces - 4 : faces + 4], FIELDS, 1)
        tail_above = pltpu.roll(above[faces - 4 : faces + 4], 2 * FIELDS, 1)
        header = jnp.where(lane < 2 * FIELDS, tail_below, tail_above)
        header = jnp.where(lane < FIELDS, own[...], header)
        for d in range(owners):
            out = outs[d]
            place = dynamic_place(me ^ d, odd, owners)
            here = pl.multiple_of(place * share, min(share, 8))
            for p in range(Q + 1):
                cx = VELOCITIES[p][0] if p < Q else 0
                out[pl.ds(p * share, share), :] = post[p, pl.ds(8 + here - cx * PLANE, share), :]
            out[pl.ds(head, 8), :] = header

            @pl.when(place == 0)
            def _():
                for n, p in enumerate(UPWARD):
                    out[pl.ds(p * share, PLANE), :] = below[n * PLANE : (n + 1) * PLANE]

            @pl.when(place == owners - 1)
            def _():
                for n, p in enumerate(DOWNWARD):
                    out[pl.ds(p * share + share - PLANE, PLANE), :] = above[
                        n * PLANE : (n + 1) * PLANE
                    ]

    def seats(blocks):
        return [(b % NB, pl.multiple_of((b // NB) * block, block)) for b in blocks]

    def place_in(d, blocks, message, lattice):
        for t, (kz, y) in enumerate(seats(blocks)):
            for p in range(Q + 1):
                lattice[p, kz, pl.ds(y, block), :] = message[
                    pl.ds(p * share + t, block, stride=NB), :
                ]

    early = [0, half, 2, 3]
    late = [d for d in order_in if d not in early]

    def early_kernel(*refs):
        *got, lattice, table, sem = refs
        copies = [
            pltpu.make_async_copy(ref.at[pl.ds(head + 4, 1), :], table.at[pl.ds(n, 1), :], sem.at[n])
            for n, ref in enumerate(got)
        ]
        for copy in copies:
            copy.start()
        for copy in copies:
            copy.wait()
        for n, d in enumerate(early):
            blocks = [table[n, t].astype(jnp.int32) for t in range(NB)]
            place_in(d, blocks, got[n], lattice)

    def middle_kernel(*refs):
        got = by_owner(refs[:owners], order_in)
        lattice = refs[owners]
        outs = by_owner(refs[owners + 1 : 2 * owners + 1], order_out)
        _, ready, table, sem = refs[2 * owners + 1 :]
        me, odd = position()
        place = dynamic_place(me, odd, owners)
        first, last = place == 0, place == owners - 1
        copies = [
            pltpu.make_async_copy(
                got[d].at[pl.ds(head + 4, 1), :], table.at[pl.ds(d, 1), :], sem.at[d]
            )
            for d in range(owners)
        ]
        for copy in copies:
            copy.start()
        for copy in copies:
            copy.wait()

        def number(d, which, field):
            return table[d, which * FIELDS + field].astype(jnp.int32)

        other = jnp.where(first, 1, jnp.where(last, 2, 0))

        def held(d, which):
            return [number(d, which, t) for t in range(NB)]

        def final(d, which):
            def lead(e, r):
                return number(d ^ e, which, NB + r)

            flip = lead(0, 2) + lead(4, 2) + lead(4, 1) + lead(6, 1) + lead(6, 0) + lead(7, 0)
            one, two = held(d ^ 7, which)
            crossed = flip % 2 == 1
            return [jnp.where(crossed, two, one), jnp.where(crossed, one, two)]

        for d in late:
            place_in(d, held(d, 0), got[d], lattice)

        def bring(chosen, i):
            for d in range(owners):
                for t, (kz, y) in enumerate(seats(held(d, other))):
                    for p in chosen:
                        lattice[p, kz, pl.ds(y + i * PLANE_ROWS, PLANE_ROWS), :] = got[d][
                            pl.ds(p * share + i * PLANE + t, PLANE_ROWS, stride=NB), :
                        ]

        @pl.when(first)
        def _():
            bring(UPWARD, 0)

        @pl.when(last)
        def _():
            bring(DOWNWARD, planes - 1)

        lane = lax.broadcasted_iota(jnp.int32, (rows, LANES), 1)
        row = lax.broadcasted_iota(jnp.int32, (rows, LANES), 0)

        def passed(pair, p):
            cx, cy, cz = VELOCITIES[p]
            if cy:
                pair = [shift_y(value, cy, lane, row, block) for value in pair]
            if cz:
                pair = [shift_z(pair[kz], pair[1 - kz], cz, lane) for kz in range(NB)]
            return pair

        for p in range(Q):
            pair = passed([lattice[p, kz] for kz in range(NB)], p)
            for kz in range(NB):
                ready[p, kz] = pair[kz]
        for kz in range(NB):
            for start in range(0, rows, 16):
                here = pl.ds(start, 16)
                after = collide(
                    [ready[p, kz, here, :] for p in range(Q)], lattice[Q, kz, here, :] > 0.5
                )
                for p in range(Q):
                    lattice[p, kz, here, :] = after[p]
        for p in range(Q):
            pair = passed([lattice[p, kz] for kz in range(NB)], p)
            for kz in range(NB):
                ready[p, kz] = pair[kz]
        for d in range(owners):
            for t, (kz, y) in enumerate(seats(final(d, 0))):
                for p in range(Q):
                    outs[d][pl.ds(p * share + t, block, stride=NB), :] = ready[
                        p, kz, pl.ds(y, block), :
                    ]

        def bring_back(chosen, i):
            for d in range(owners):
                for t, (kz, y) in enumerate(seats(final(d, other))):
                    for p in chosen:
                        outs[d][
                            pl.ds(p * share + i * PLANE + t, PLANE_ROWS, stride=NB), :
                        ] = ready[p, kz, pl.ds(y + i * PLANE_ROWS, PLANE_ROWS), :]

        @pl.when(last)
        def _():
            bring_back(UPWARD, planes - 1)

        @pl.when(first)
        def _():
            bring_back(DOWNWARD, 0)

    def crossing_kernel(*refs):
        got = by_owner(refs[:owners], order_out)
        near, far, up, down = refs[owners:]
        me, odd = position()
        for d in range(owners):
            place = dynamic_place(me ^ d, odd, owners)

            @pl.when(place == owners - 1)
            def _():
                for n, p in enumerate(UPWARD):
                    up[pl.ds(n * PLANE, PLANE), :] = got[d][
                        pl.ds(p * share + share - PLANE, PLANE), :
                    ]

            @pl.when(place == 0)
            def _():
                for n, p in enumerate(DOWNWARD):
                    down[pl.ds(n * PLANE, PLANE), :] = got[d][pl.ds(p * share, PLANE), :]

        for out in (up, down):
            out[pl.ds(faces, 4), :] = jnp.zeros((4, LANES), f32)
        send_sides(odd, up, down, near, far)

    ends = [(p, 0) for p in UPWARD] + [(p, WHOLE - 8) for p in DOWNWARD]

    def unpack_kernel(*refs):
        got, (out, edge, main, sem) = by_owner(refs[:owners], order_out), refs[owners:]
        me, odd = position()
        for d in range(owners):
            place = dynamic_place(me ^ d, odd, owners)
            here = pl.multiple_of(place * share, min(share, 8))
            for p in range(Q):
                cx = VELOCITIES[p][0]
                main[p, pl.ds(8 + here + cx * PLANE, share), :] = got[d][
                    pl.ds(p * share, share), :
                ]
        copy = pltpu.make_async_copy(main.at[:, pl.ds(8, WHOLE), :], out, sem.at[0])
        copy.start()
        for n, (p, start) in enumerate(ends):
            edge[n] = main[p, pl.ds(8 + start, 8), :]
        copy.wait()

    def finish_kernel(_, edge, far, near, out, patch, sem):
        below, above = sides(position()[1], near, far)
        for n in range(len(ends)):
            patch[n] = edge[n]
        for n in range(len(UPWARD)):
            patch[n, pl.ds(0, PLANE), :] = below[n * PLANE : (n + 1) * PLANE]
            patch[len(UPWARD) + n, pl.ds(8 - PLANE, PLANE), :] = above[n * PLANE : (n + 1) * PLANE]
        copies = [
            pltpu.make_async_copy(patch.at[n], out.at[p, pl.ds(start, 8), :], sem.at[n])
            for n, (p, start) in enumerate(ends)
        ]
        for copy in copies:
            copy.start()
        for copy in copies:
            copy.wait()

    def shape(*dims):
        return jax.ShapeDtypeStruct(dims, f32)

    def call(
        kernel,
        name,
        out_shape,
        inputs,
        cost,
        scratch=(),
        spec=VMEM_SPEC,
        limit=40,
        aliases=None,
        out_specs=None,
    ):
        outs = out_specs or jax.tree.map(lambda _: VMEM_SPEC, out_shape)
        specs = spec if isinstance(spec, tuple) else (spec,) * len(inputs)
        return pl.pallas_call(
            kernel,
            out_shape=out_shape,
            in_specs=specs,
            out_specs=outs,
            scratch_shapes=list(scratch),
            input_output_aliases=aliases or {},
            compiler_params=pltpu.CompilerParams(vmem_limit_bytes=limit * 1024 * 1024),
            cost_estimate=pl.CostEstimate(flops=cost, bytes_accessed=cost, transcendentals=0),
            name=name,
        )(*inputs)

    def exchange(parts, order):
        return [parts[0]] + [
            lax.ppermute(parts[n], "gx", [(g, g ^ order[n]) for g in range(owners)])
            for n in range(1, owners)
        ]

    def hop(near, far):
        ahead = [(s + 1) % slabs if s % 2 == 0 else (s - 1) % slabs for s in range(slabs)]
        behind = [(s - 1) % slabs if s % 2 == 0 else (s + 1) % slabs for s in range(slabs)]
        far = lax.ppermute(far, "gy", list(enumerate(behind)))
        return lax.ppermute(near, "gy", list(enumerate(ahead))), far

    def padded(count):
        return shape(count, 8 + WHOLE + 8, LANES)

    whole_lattice = (Q + 1, NB, rows, LANES)
    small, large = 100_000, 4_000_000

    def shards(populations, solid_mask, slot_blocks, swap_slots):
        tiles = B * B * B // LANES
        pops = populations[0].transpose(1, 0, 2).reshape(Q, NB, tiles, LANES)
        pops = pops.transpose(0, 2, 1, 3).reshape(Q, WHOLE, LANES)
        mask = solid_mask[0].reshape(NB, tiles, LANES).transpose(1, 0, 2).reshape(WHOLE, LANES)
        swaps = swap_slots[0, 0].T
        in_place = pl.BlockSpec(memory_space=pltpu.HBM)
        near, far, own = call(
            edge_kernel,
            "edge_planes",
            (shape(rows_hop, LANES), shape(rows_hop, LANES), shape(8, LANES)),
            (pops, mask, slot_blocks, swaps),
            small,
            (
                pltpu.VMEM((rows_hop, LANES), f32),
                pltpu.VMEM((rows_hop, LANES), f32),
                pltpu.VMEM((2, Q, 8, LANES), f32),
                pltpu.VMEM((2, 8, LANES), jnp.int32),
                pltpu.VMEM(slot_blocks.shape, jnp.int32),
                pltpu.VMEM(swaps.shape, jnp.int32),
                pltpu.SemaphoreType.DMA((6,)),
            ),
            in_place,
            62,
        )
        near, far = hop(near, far)
        post = call(
            collide_kernel,
            "first_collision",
            padded(Q + 1),
            (pops, mask),
            large,
        )
        parts = call(
            pack_kernel,
            "pack_planes",
            (shape(rows_in, LANES),) * owners,
            (post, own, far, near),
            large,
        )
        got = exchange(parts, order_in)
        lattice = call(
            early_kernel,
            "place_early",
            shape(*whole_lattice),
            [got[order_in.index(d)] for d in early],
            large,
            (pltpu.SMEM((len(early), LANES), f32), pltpu.SemaphoreType.DMA((len(early),))),
        )
        *parts, _ = call(
            middle_kernel,
            "second_step",
            (shape(rows_out, LANES),) * owners + (shape(*whole_lattice),),
            (*got, lattice),
            large,
            (
                pltpu.VMEM(whole_lattice, f32),
                pltpu.SMEM((owners, LANES), f32),
                pltpu.SemaphoreType.DMA((owners,)),
            ),
            aliases={owners: owners},
        )
        home = exchange(parts, order_out)
        near, far = call(
            crossing_kernel,
            "crossing_planes",
            (shape(rows_hop, LANES),) * 2,
            home,
            small,
            (pltpu.VMEM((rows_hop, LANES), f32),) * 2,
        )
        near, far = hop(near, far)
        out, edge = call(
            unpack_kernel,
            "unpack_planes",
            (shape(Q, WHOLE, LANES), shape(len(ends), 8, LANES)),
            home,
            large,
            (pltpu.VMEM((Q, 8 + WHOLE + 8, LANES), f32), pltpu.SemaphoreType.DMA((1,))),
            out_specs=(in_place, VMEM_SPEC),
        )
        out = call(
            finish_kernel,
            "finish",
            shape(Q, WHOLE, LANES),
            (out, edge, far, near),
            small,
            (pltpu.VMEM((len(ends), 8, LANES), f32), pltpu.SemaphoreType.DMA((len(ends),))),
            spec=(in_place, VMEM_SPEC, VMEM_SPEC, VMEM_SPEC),
            aliases={0: 0},
            out_specs=in_place,
        )
        out = out.reshape(Q, tiles, NB, LANES).transpose(0, 2, 1, 3)
        return out.reshape(Q, NB, B * B * B).transpose(1, 0, 2)[None]

    return shards


def solution(mesh):
    return jax.shard_map(
        build(mesh),
        mesh=mesh,
        in_specs=(
            P("gy", "gx", None, None),
            P("gy", "gx", None),
            P("gy", "gx"),
            P("gy", "gx", None, None),
        ),
        out_specs=P("gy", "gx", None, None),
        check_vma=False,
    )
```

```python
import jax
import jax.numpy as jnp
from jax import lax
from jax.experimental import pallas as pl
from jax.experimental.pallas import tpu as pltpu
from jax.sharding import PartitionSpec as P

B = 16
NB = 2
LANES = 128
PLANE_ROWS = B * B // LANES
PLANE = PLANE_ROWS * NB
FIELDS = NB + 3
WHOLE = B * PLANE

VELOCITIES = (
    (0, 0, 0),
    (1, 0, 0),
    (-1, 0, 0),
    (0, 1, 0),
    (0, -1, 0),
    (0, 0, 1),
    (0, 0, -1),
    (1, 1, 0),
    (-1, -1, 0),
    (1, -1, 0),
    (-1, 1, 0),
    (1, 0, 1),
    (-1, 0, -1),
    (1, 0, -1),
    (-1, 0, 1),
    (0, 1, 1),
    (0, -1, -1),
    (0, 1, -1),
    (0, -1, 1),
)
OPPOSITE = (0, 2, 1, 4, 3, 6, 5, 8, 7, 10, 9, 12, 11, 14, 13, 16, 15, 18, 17)
Q = len(VELOCITIES)
UPWARD = tuple(p for p in range(Q) if VELOCITIES[p][0] == 1)
DOWNWARD = tuple(p for p in range(Q) if VELOCITIES[p][0] == -1)

VMEM_SPEC = pl.BlockSpec(memory_space=pltpu.VMEM)


def dynamic_place(owner, odd_slab, owners):
    pair, core = owner // 2, owner % 2
    forward = 2 * pair + jnp.where(pair % 2 == 0, core, 1 - core)
    return jnp.where(odd_slab == 1, owners - 1 - forward, forward)


def collide(f, fluid):
    def pair(p):
        return f[p] + f[p + 1], f[p] - f[p + 1]

    sx, dx = pair(1)
    sy, dy = pair(3)
    sz, dz = pair(5)
    sxy_a, dxy_a = pair(7)
    sxy_b, dxy_b = pair(9)
    sxz_a, dxz_a = pair(11)
    sxz_b, dxz_b = pair(13)
    syz_a, dyz_a = pair(15)
    syz_b, dyz_b = pair(17)
    axy, bxy = sxy_a + sxy_b, sxy_a - sxy_b
    axz, bxz = sxz_a + sxz_b, sxz_a - sxz_b
    ayz, byz = syz_a + syz_b, syz_a - syz_b
    rho = f[0] + sx + sy + sz + axy + axz + ayz
    ox = dxy_a + dxy_b + dxz_a + dxz_b
    oy = dxy_a - dxy_b + dyz_a + dyz_b
    oz = dxz_a - dxz_b + dyz_a - dyz_b
    jx, jy, jz = dx + ox, dy + oy, dz + oz
    jxx, jyy, jzz = jx * jx, jy * jy, jz * jz
    base = rho * (1.3 / 9.0)
    wide = 1.3 / 3.0
    thin = 1.3 / 6.0
    axy1 = base - 0.3 * axy + wide * (jxx + jyy) - thin * jzz
    axz1 = base - 0.3 * axz + wide * (jxx + jzz) - thin * jyy
    ayz1 = base - 0.3 * ayz + wide * (jyy + jzz) - thin * jxx
    bxy1 = 1.25 * (jx * jy) - 0.25 * bxy
    bxz1 = 1.25 * (jx * jz) - 0.25 * bxz
    byz1 = 1.25 * (jy * jz) - 0.25 * byz
    third = rho * (1.25 / 3.0)
    sx1 = third + 1.25 * jxx - 0.25 * (sx + axy + axz) - axy1 - axz1
    sy1 = third + 1.25 * jyy - 0.25 * (sy + axy + ayz) - axy1 - ayz1
    sz1 = third + 1.25 * jzz - 0.25 * (sz + axz + ayz) - axz1 - ayz1
    rest = rho - sx1 - sy1 - sz1 - axy1 - axz1 - ayz1

    def split(even, odd):
        return 0.5 * (even + odd), 0.5 * (even - odd)

    def diagonal(a1, b1, d_a, d_b, j_first, j_second):
        plus = 0.25 * (j_first + j_second) - 0.5 * d_a
        minus = 0.25 * (j_first - j_second) - 0.5 * d_b
        return split(0.5 * (a1 + b1), plus) + split(0.5 * (a1 - b1), minus)

    relaxed = (
        (rest,)
        + split(sx1, 0.5 * ox)
        + split(sy1, 0.5 * oy)
        + split(sz1, 0.5 * oz)
        + diagonal(axy1, bxy1, dxy_a, dxy_b, jx, jy)
        + diagonal(axz1, bxz1, dxz_a, dxz_b, jx, jz)
        + diagonal(ayz1, byz1, dyz_a, dyz_b, jy, jz)
    )
    return [jnp.where(fluid, relaxed[p], f[OPPOSITE[p]]) for p in range(Q)]


def shift_y(value, step, lane, row, block):
    rows = value.shape[0]
    turned = pltpu.roll(value, B if step == 1 else LANES - B, 1)
    if step == 1:
        edge, start = lane < B, row % PLANE_ROWS == 0
        near, far = pltpu.roll(turned, 1, 0), pltpu.roll(turned, block - 1, 0)
    else:
        edge, start = lane >= LANES - B, row % PLANE_ROWS == PLANE_ROWS - 1
        near, far = pltpu.roll(turned, rows - 1, 0), pltpu.roll(turned, rows - block + 1, 0)
    return jnp.where(edge, jnp.where(start, far, near), turned)


def shift_z(value, other, step, lane):
    if step == 1:
        return jnp.where(
            lane % B == 0, pltpu.roll(other, LANES - (B - 1), 1), pltpu.roll(value, 1, 1)
        )
    return jnp.where(
        lane % B == B - 1, pltpu.roll(other, B - 1, 1), pltpu.roll(value, LANES - 1, 1)
    )


def build(mesh):
    owners, slabs = mesh.shape["gx"], mesh.shape["gy"]
    planes = B // owners
    share = planes * PLANE
    block = planes * PLANE_ROWS
    rows = owners * block
    head = (Q + 1) * share
    rows_in = head + 8
    rows_out = Q * share
    faces = len(UPWARD) * PLANE
    rows_hop = faces + 4
    f32 = jnp.float32

    half = owners // 2
    spare = [*range(half + 2, owners), *range(4, half), 1]
    order_in = [0, half, 2, half + 1, 3, *spare]
    order_out = [0, half, 2, half + 1, 3, *spare]

    def by_owner(refs, order):
        return [refs[order.index(d)] for d in range(owners)]

    def position():
        me = lax.axis_index("gx")
        return me, lax.axis_index("gy") % 2

    def sides(odd, near, far):
        return (
            jnp.where(odd == 1, near[...], far[...]),
            jnp.where(odd == 1, far[...], near[...]),
        )

    def send_sides(odd, up, down, near, far):
        near[...] = jnp.where(odd == 1, down[...], up[...])
        far[...] = jnp.where(odd == 1, up[...], down[...])

    def edge_kernel(pops, mask, slots, swaps, near, far, own, up, down, cells, solid, held, given, sem):
        ends = (WHOLE - 8, 0)
        copies = [(slots, held), (swaps, given)]
        for n, start in enumerate(ends):
            copies.append((pops.at[:, pl.ds(start, 8), :], cells.at[n]))
            copies.append((mask.at[pl.ds(start, 8), :], solid.at[n]))
        copies = [
            pltpu.make_async_copy(source, target, sem.at[n])
            for n, (source, target) in enumerate(copies)
        ]
        for copy in copies:
            copy.start()
        for copy in copies:
            copy.wait()
        own[...] = jnp.zeros((8, LANES), f32)
        own[4:5, 0:NB] = held[...].astype(f32)
        own[5:6, 0:3] = given[0:1].astype(f32)
        lane = lax.broadcasted_iota(jnp.int32, (8, LANES), 1)
        swaps_beside = pltpu.roll(pltpu.roll(own[...], NB, 1), 7, 0)
        own[...] = jnp.where(lane < NB, own[...], swaps_beside)
        for n, (out, chosen, inside) in enumerate(((up, UPWARD, 8 - PLANE), (down, DOWNWARD, 0))):
            after = collide([cells[n, p] for p in range(Q)], solid[n] > 0)
            for m, p in enumerate(chosen):
                out[pl.ds(m * PLANE, PLANE), :] = after[p][inside : inside + PLANE]
            out[pl.ds(faces, 4), :] = own[4:8]
        send_sides(position()[1], up, down, near, far)

    def collide_kernel(cells, solid, post):
        for start in range(0, WHOLE, 8):
            here = pl.ds(start, 8)
            after = collide([cells[p, here, :] for p in range(Q)], solid[here, :] > 0)
            for p in range(Q):
                post[p, pl.ds(8 + start, 8), :] = after[p]
            post[Q, pl.ds(8 + start, 8), :] = solid[here, :].astype(f32)

    def pack_kernel(post, own, far, near, *outs):
        me, odd = position()
        below, above = sides(odd, near, far)
        outs = by_owner(outs, order_in)
        lane = lax.broadcasted_iota(jnp.int32, (8, LANES), 1)
        tail_below = pltpu.roll(below[faces - 4 : faces + 4], FIELDS, 1)
        tail_above = pltpu.roll(above[faces - 4 : faces + 4], 2 * FIELDS, 1)
        header = jnp.where(lane < 2 * FIELDS, tail_below, tail_above)
        header = jnp.where(lane < FIELDS, own[...], header)
        for d in range(owners):
            out = outs[d]
            place = dynamic_place(me ^ d, odd, owners)
            here = pl.multiple_of(place * share, min(share, 8))
            for p in range(Q + 1):
                cx = VELOCITIES[p][0] if p < Q else 0
                out[pl.ds(p * share, share), :] = post[p, pl.ds(8 + here - cx * PLANE, share), :]
            out[pl.ds(head, 8), :] = header

            @pl.when(place == 0)
            def _():
                for n, p in enumerate(UPWARD):
                    out[pl.ds(p * share, PLANE), :] = below[n * PLANE : (n + 1) * PLANE]

            @pl.when(place == owners - 1)
            def _():
                for n, p in enumerate(DOWNWARD):
                    out[pl.ds(p * share + share - PLANE, PLANE), :] = above[
                        n * PLANE : (n + 1) * PLANE
                    ]

    def seats(blocks):
        return [(b % NB, pl.multiple_of((b // NB) * block, block)) for b in blocks]

    def place_in(d, blocks, message, lattice):
        for t, (kz, y) in enumerate(seats(blocks)):
            for p in range(Q + 1):
                lattice[p, kz, pl.ds(y, block), :] = message[
                    pl.ds(p * share + t, block, stride=NB), :
                ]

    early = [0, half, 2]
    late = [d for d in order_in if d not in early]

    def early_kernel(*refs):
        *got, lattice, table, sem = refs
        copies = [
            pltpu.make_async_copy(ref.at[pl.ds(head + 4, 1), :], table.at[pl.ds(n, 1), :], sem.at[n])
            for n, ref in enumerate(got)
        ]
        for copy in copies:
            copy.start()
        for copy in copies:
            copy.wait()
        for n, d in enumerate(early):
            blocks = [table[n, t].astype(jnp.int32) for t in range(NB)]
            place_in(d, blocks, got[n], lattice)

    def middle_kernel(*refs):
        got = by_owner(refs[:owners], order_in)
        lattice = refs[owners]
        outs = by_owner(refs[owners + 1 : 2 * owners + 1], order_out)
        _, ready, table, sem = refs[2 * owners + 1 :]
        me, odd = position()
        place = dynamic_place(me, odd, owners)
        first, last = place == 0, place == owners - 1
        copies = [
            pltpu.make_async_copy(
                got[d].at[pl.ds(head + 4, 1), :], table.at[pl.ds(d, 1), :], sem.at[d]
            )
            for d in range(owners)
        ]
        for copy in copies:
            copy.start()
        for copy in copies:
            copy.wait()

        def number(d, which, field):
            return table[d, which * FIELDS + field].astype(jnp.int32)

        other = jnp.where(first, 1, jnp.where(last, 2, 0))

        def held(d, which):
            return [number(d, which, t) for t in range(NB)]

        def final(d, which):
            def lead(e, r):
                return number(d ^ e, which, NB + r)

            flip = lead(0, 2) + lead(4, 2) + lead(4, 1) + lead(6, 1) + lead(6, 0) + lead(7, 0)
            one, two = held(d ^ 7, which)
            crossed = flip % 2 == 1
            return [jnp.where(crossed, two, one), jnp.where(crossed, one, two)]

        for d in late:
            place_in(d, held(d, 0), got[d], lattice)

        def bring(chosen, i):
            for d in range(owners):
                for t, (kz, y) in enumerate(seats(held(d, other))):
                    for p in chosen:
                        lattice[p, kz, pl.ds(y + i * PLANE_ROWS, PLANE_ROWS), :] = got[d][
                            pl.ds(p * share + i * PLANE + t, PLANE_ROWS, stride=NB), :
                        ]

        @pl.when(first)
        def _():
            bring(UPWARD, 0)

        @pl.when(last)
        def _():
            bring(DOWNWARD, planes - 1)

        lane = lax.broadcasted_iota(jnp.int32, (rows, LANES), 1)
        row = lax.broadcasted_iota(jnp.int32, (rows, LANES), 0)

        def passed(pair, p):
            cx, cy, cz = VELOCITIES[p]
            if cy:
                pair = [shift_y(value, cy, lane, row, block) for value in pair]
            if cz:
                pair = [shift_z(pair[kz], pair[1 - kz], cz, lane) for kz in range(NB)]
            return pair

        for p in range(Q):
            pair = passed([lattice[p, kz] for kz in range(NB)], p)
            for kz in range(NB):
                ready[p, kz] = pair[kz]
        for kz in range(NB):
            for start in range(0, rows, 16):
                here = pl.ds(start, 16)
                after = collide(
                    [ready[p, kz, here, :] for p in range(Q)], lattice[Q, kz, here, :] > 0.5
                )
                for p in range(Q):
                    lattice[p, kz, here, :] = after[p]
        for p in range(Q):
            pair = passed([lattice[p, kz] for kz in range(NB)], p)
            for kz in range(NB):
                ready[p, kz] = pair[kz]
        for d in range(owners):
            for t, (kz, y) in enumerate(seats(final(d, 0))):
                for p in range(Q):
                    outs[d][pl.ds(p * share + t, block, stride=NB), :] = ready[
                        p, kz, pl.ds(y, block), :
                    ]

        def bring_back(chosen, i):
            for d in range(owners):
                for t, (kz, y) in enumerate(seats(final(d, other))):
                    for p in chosen:
                        outs[d][
                            pl.ds(p * share + i * PLANE + t, PLANE_ROWS, stride=NB), :
                        ] = ready[p, kz, pl.ds(y + i * PLANE_ROWS, PLANE_ROWS), :]

        @pl.when(last)
        def _():
            bring_back(UPWARD, planes - 1)

        @pl.when(first)
        def _():
            bring_back(DOWNWARD, 0)

    def crossing_kernel(*refs):
        got = by_owner(refs[:owners], order_out)
        near, far, up, down = refs[owners:]
        me, odd = position()
        for d in range(owners):
            place = dynamic_place(me ^ d, odd, owners)

            @pl.when(place == owners - 1)
            def _():
                for n, p in enumerate(UPWARD):
                    up[pl.ds(n * PLANE, PLANE), :] = got[d][
                        pl.ds(p * share + share - PLANE, PLANE), :
                    ]

            @pl.when(place == 0)
            def _():
                for n, p in enumerate(DOWNWARD):
                    down[pl.ds(n * PLANE, PLANE), :] = got[d][pl.ds(p * share, PLANE), :]

        for out in (up, down):
            out[pl.ds(faces, 4), :] = jnp.zeros((4, LANES), f32)
        send_sides(odd, up, down, near, far)

    ends = [(p, 0) for p in UPWARD] + [(p, WHOLE - 8) for p in DOWNWARD]

    def unpack_kernel(*refs):
        got, (out, edge, main, sem) = by_owner(refs[:owners], order_out), refs[owners:]
        me, odd = position()
        for d in range(owners):
            place = dynamic_place(me ^ d, odd, owners)
            here = pl.multiple_of(place * share, min(share, 8))
            for p in range(Q):
                cx = VELOCITIES[p][0]
                main[p, pl.ds(8 + here + cx * PLANE, share), :] = got[d][
                    pl.ds(p * share, share), :
                ]
        copy = pltpu.make_async_copy(main.at[:, pl.ds(8, WHOLE), :], out, sem.at[0])
        copy.start()
        for n, (p, start) in enumerate(ends):
            edge[n] = main[p, pl.ds(8 + start, 8), :]
        copy.wait()

    def finish_kernel(_, edge, far, near, out, patch, sem):
        below, above = sides(position()[1], near, far)
        for n in range(len(ends)):
            patch[n] = edge[n]
        for n in range(len(UPWARD)):
            patch[n, pl.ds(0, PLANE), :] = below[n * PLANE : (n + 1) * PLANE]
            patch[len(UPWARD) + n, pl.ds(8 - PLANE, PLANE), :] = above[n * PLANE : (n + 1) * PLANE]
        copies = [
            pltpu.make_async_copy(patch.at[n], out.at[p, pl.ds(start, 8), :], sem.at[n])
            for n, (p, start) in enumerate(ends)
        ]
        for copy in copies:
            copy.start()
        for copy in copies:
            copy.wait()

    def shape(*dims):
        return jax.ShapeDtypeStruct(dims, f32)

    def call(
        kernel,
        name,
        out_shape,
        inputs,
        cost,
        scratch=(),
        spec=VMEM_SPEC,
        limit=40,
        aliases=None,
        out_specs=None,
    ):
        outs = out_specs or jax.tree.map(lambda _: VMEM_SPEC, out_shape)
        specs = spec if isinstance(spec, tuple) else (spec,) * len(inputs)
        return pl.pallas_call(
            kernel,
            out_shape=out_shape,
            in_specs=specs,
            out_specs=outs,
            scratch_shapes=list(scratch),
            input_output_aliases=aliases or {},
            compiler_params=pltpu.CompilerParams(vmem_limit_bytes=limit * 1024 * 1024),
            cost_estimate=pl.CostEstimate(flops=cost, bytes_accessed=cost, transcendentals=0),
            name=name,
        )(*inputs)

    def exchange(parts, order):
        return [parts[0]] + [
            lax.ppermute(parts[n], "gx", [(g, g ^ order[n]) for g in range(owners)])
            for n in range(1, owners)
        ]

    def hop(near, far):
        ahead = [(s + 1) % slabs if s % 2 == 0 else (s - 1) % slabs for s in range(slabs)]
        behind = [(s - 1) % slabs if s % 2 == 0 else (s + 1) % slabs for s in range(slabs)]
        far = lax.ppermute(far, "gy", list(enumerate(behind)))
        return lax.ppermute(near, "gy", list(enumerate(ahead))), far

    def padded(count):
        return shape(count, 8 + WHOLE + 8, LANES)

    whole_lattice = (Q + 1, NB, rows, LANES)
    small, large = 100_000, 4_000_000

    def shards(populations, solid_mask, slot_blocks, swap_slots):
        tiles = B * B * B // LANES
        pops = populations[0].transpose(1, 0, 2).reshape(Q, NB, tiles, LANES)
        pops = pops.transpose(0, 2, 1, 3).reshape(Q, WHOLE, LANES)
        mask = solid_mask[0].reshape(NB, tiles, LANES).transpose(1, 0, 2).reshape(WHOLE, LANES)
        swaps = swap_slots[0, 0].T
        in_place = pl.BlockSpec(memory_space=pltpu.HBM)
        near, far, own = call(
            edge_kernel,
            "edge_planes",
            (shape(rows_hop, LANES), shape(rows_hop, LANES), shape(8, LANES)),
            (pops, mask, slot_blocks, swaps),
            small,
            (
                pltpu.VMEM((rows_hop, LANES), f32),
                pltpu.VMEM((rows_hop, LANES), f32),
                pltpu.VMEM((2, Q, 8, LANES), f32),
                pltpu.VMEM((2, 8, LANES), jnp.int32),
                pltpu.VMEM(slot_blocks.shape, jnp.int32),
                pltpu.VMEM(swaps.shape, jnp.int32),
                pltpu.SemaphoreType.DMA((6,)),
            ),
            in_place,
            62,
        )
        near, far = hop(near, far)
        post = call(
            collide_kernel,
            "first_collision",
            padded(Q + 1),
            (pops, mask),
            large,
        )
        parts = call(
            pack_kernel,
            "pack_planes",
            (shape(rows_in, LANES),) * owners,
            (post, own, far, near),
            large,
        )
        got = exchange(parts, order_in)
        lattice = call(
            early_kernel,
            "place_early",
            shape(*whole_lattice),
            [got[order_in.index(d)] for d in early],
            large,
            (pltpu.SMEM((len(early), LANES), f32), pltpu.SemaphoreType.DMA((len(early),))),
        )
        *parts, _ = call(
            middle_kernel,
            "second_step",
            (shape(rows_out, LANES),) * owners + (shape(*whole_lattice),),
            (*got, lattice),
            large,
            (
                pltpu.VMEM(whole_lattice, f32),
                pltpu.SMEM((owners, LANES), f32),
                pltpu.SemaphoreType.DMA((owners,)),
            ),
            aliases={owners: owners},
        )
        home = exchange(parts, order_out)
        near, far = call(
            crossing_kernel,
            "crossing_planes",
            (shape(rows_hop, LANES),) * 2,
            home,
            small,
            (pltpu.VMEM((rows_hop, LANES), f32),) * 2,
        )
        near, far = hop(near, far)
        out, edge = call(
            unpack_kernel,
            "unpack_planes",
            (shape(Q, WHOLE, LANES), shape(len(ends), 8, LANES)),
            home,
            large,
            (pltpu.VMEM((Q, 8 + WHOLE + 8, LANES), f32), pltpu.SemaphoreType.DMA((1,))),
            out_specs=(in_place, VMEM_SPEC),
        )
        out = call(
            finish_kernel,
            "finish",
            shape(Q, WHOLE, LANES),
            (out, edge, far, near),
            small,
            (pltpu.VMEM((len(ends), 8, LANES), f32), pltpu.SemaphoreType.DMA((len(ends),))),
            spec=(in_place, VMEM_SPEC, VMEM_SPEC, VMEM_SPEC),
            aliases={0: 0},
            out_specs=in_place,
        )
        out = out.reshape(Q, tiles, NB, LANES).transpose(0, 2, 1, 3)
        return out.reshape(Q, NB, B * B * B).transpose(1, 0, 2)[None]

    return shards


def solution(mesh):
    return jax.shard_map(
        build(mesh),
        mesh=mesh,
        in_specs=(
            P("gy", "gx", None, None),
            P("gy", "gx", None),
            P("gy", "gx"),
            P("gy", "gx", None, None),
        ),
        out_specs=P("gy", "gx", None, None),
        check_vma=False,
    )
```

```python
import jax
import jax.numpy as jnp
from jax import lax
from jax.experimental import pallas as pl
from jax.experimental.pallas import tpu as pltpu
from jax.sharding import PartitionSpec as P

B = 16
NB = 2
LANES = 128
PLANE_ROWS = B * B // LANES
PLANE = PLANE_ROWS * NB
FIELDS = NB + 3
WHOLE = B * PLANE

VELOCITIES = (
    (0, 0, 0),
    (1, 0, 0),
    (-1, 0, 0),
    (0, 1, 0),
    (0, -1, 0),
    (0, 0, 1),
    (0, 0, -1),
    (1, 1, 0),
    (-1, -1, 0),
    (1, -1, 0),
    (-1, 1, 0),
    (1, 0, 1),
    (-1, 0, -1),
    (1, 0, -1),
    (-1, 0, 1),
    (0, 1, 1),
    (0, -1, -1),
    (0, 1, -1),
    (0, -1, 1),
)
OPPOSITE = (0, 2, 1, 4, 3, 6, 5, 8, 7, 10, 9, 12, 11, 14, 13, 16, 15, 18, 17)
Q = len(VELOCITIES)
UPWARD = tuple(p for p in range(Q) if VELOCITIES[p][0] == 1)
DOWNWARD = tuple(p for p in range(Q) if VELOCITIES[p][0] == -1)

VMEM_SPEC = pl.BlockSpec(memory_space=pltpu.VMEM)


def dynamic_place(owner, odd_slab, owners):
    pair, core = owner // 2, owner % 2
    forward = 2 * pair + jnp.where(pair % 2 == 0, core, 1 - core)
    return jnp.where(odd_slab == 1, owners - 1 - forward, forward)


def collide(f, fluid):
    def pair(p):
        return f[p] + f[p + 1], f[p] - f[p + 1]

    sx, dx = pair(1)
    sy, dy = pair(3)
    sz, dz = pair(5)
    sxy_a, dxy_a = pair(7)
    sxy_b, dxy_b = pair(9)
    sxz_a, dxz_a = pair(11)
    sxz_b, dxz_b = pair(13)
    syz_a, dyz_a = pair(15)
    syz_b, dyz_b = pair(17)
    axy, bxy = sxy_a + sxy_b, sxy_a - sxy_b
    axz, bxz = sxz_a + sxz_b, sxz_a - sxz_b
    ayz, byz = syz_a + syz_b, syz_a - syz_b
    rho = f[0] + sx + sy + sz + axy + axz + ayz
    ox = dxy_a + dxy_b + dxz_a + dxz_b
    oy = dxy_a - dxy_b + dyz_a + dyz_b
    oz = dxz_a - dxz_b + dyz_a - dyz_b
    jx, jy, jz = dx + ox, dy + oy, dz + oz
    jxx, jyy, jzz = jx * jx, jy * jy, jz * jz
    base = rho * (1.3 / 9.0)
    wide = 1.3 / 3.0
    thin = 1.3 / 6.0
    axy1 = base - 0.3 * axy + wide * (jxx + jyy) - thin * jzz
    axz1 = base - 0.3 * axz + wide * (jxx + jzz) - thin * jyy
    ayz1 = base - 0.3 * ayz + wide * (jyy + jzz) - thin * jxx
    bxy1 = 1.25 * (jx * jy) - 0.25 * bxy
    bxz1 = 1.25 * (jx * jz) - 0.25 * bxz
    byz1 = 1.25 * (jy * jz) - 0.25 * byz
    third = rho * (1.25 / 3.0)
    sx1 = third + 1.25 * jxx - 0.25 * (sx + axy + axz) - axy1 - axz1
    sy1 = third + 1.25 * jyy - 0.25 * (sy + axy + ayz) - axy1 - ayz1
    sz1 = third + 1.25 * jzz - 0.25 * (sz + axz + ayz) - axz1 - ayz1
    rest = rho - sx1 - sy1 - sz1 - axy1 - axz1 - ayz1

    def split(even, odd):
        return 0.5 * (even + odd), 0.5 * (even - odd)

    def diagonal(a1, b1, d_a, d_b, j_first, j_second):
        plus = 0.25 * (j_first + j_second) - 0.5 * d_a
        minus = 0.25 * (j_first - j_second) - 0.5 * d_b
        return split(0.5 * (a1 + b1), plus) + split(0.5 * (a1 - b1), minus)

    relaxed = (
        (rest,)
        + split(sx1, 0.5 * ox)
        + split(sy1, 0.5 * oy)
        + split(sz1, 0.5 * oz)
        + diagonal(axy1, bxy1, dxy_a, dxy_b, jx, jy)
        + diagonal(axz1, bxz1, dxz_a, dxz_b, jx, jz)
        + diagonal(ayz1, byz1, dyz_a, dyz_b, jy, jz)
    )
    return [jnp.where(fluid, relaxed[p], f[OPPOSITE[p]]) for p in range(Q)]


def shift_y(value, step, lane, row, block):
    rows = value.shape[0]
    turned = pltpu.roll(value, B if step == 1 else LANES - B, 1)
    if step == 1:
        edge, start = lane < B, row % PLANE_ROWS == 0
        near, far = pltpu.roll(turned, 1, 0), pltpu.roll(turned, block - 1, 0)
    else:
        edge, start = lane >= LANES - B, row % PLANE_ROWS == PLANE_ROWS - 1
        near, far = pltpu.roll(turned, rows - 1, 0), pltpu.roll(turned, rows - block + 1, 0)
    return jnp.where(edge, jnp.where(start, far, near), turned)


def shift_z(value, other, step, lane):
    if step == 1:
        return jnp.where(
            lane % B == 0, pltpu.roll(other, LANES - (B - 1), 1), pltpu.roll(value, 1, 1)
        )
    return jnp.where(
        lane % B == B - 1, pltpu.roll(other, B - 1, 1), pltpu.roll(value, LANES - 1, 1)
    )


def build(mesh):
    owners, slabs = mesh.shape["gx"], mesh.shape["gy"]
    planes = B // owners
    share = planes * PLANE
    block = planes * PLANE_ROWS
    rows = owners * block
    head = (Q + 1) * share
    rows_in = head + 8
    rows_out = Q * share
    faces = len(UPWARD) * PLANE
    rows_hop = faces + 4
    f32 = jnp.float32

    half = owners // 2
    spare = [*range(half + 2, owners), *range(4, half), 1]
    order_in = [0, half, 2, half + 1, 3, *spare]
    order_out = [0, half, 2, half + 1, half + 2, 3, *spare[1:]]

    def by_owner(refs, order):
        return [refs[order.index(d)] for d in range(owners)]

    def position():
        me = lax.axis_index("gx")
        return me, lax.axis_index("gy") % 2

    def sides(odd, near, far):
        return (
            jnp.where(odd == 1, near[...], far[...]),
            jnp.where(odd == 1, far[...], near[...]),
        )

    def send_sides(odd, up, down, near, far):
        near[...] = jnp.where(odd == 1, down[...], up[...])
        far[...] = jnp.where(odd == 1, up[...], down[...])

    def edge_kernel(pops, mask, slots, swaps, near, far, own, up, down, cells, solid, held, given, sem):
        ends = (WHOLE - 8, 0)
        copies = []
        for n, start in enumerate(ends):
            copies.append((pops.at[:, pl.ds(start, 8), :], cells.at[n]))
            copies.append((mask.at[pl.ds(start, 8), :], solid.at[n]))
        copies += [(slots, held), (swaps, given)]
        copies = [
            pltpu.make_async_copy(source, target, sem.at[n])
            for n, (source, target) in enumerate(copies)
        ]
        for copy in copies:
            copy.start()
        for copy in copies:
            copy.wait()
        own[...] = jnp.zeros((8, LANES), f32)
        own[4:5, 0:NB] = held[...].astype(f32)
        own[5:6, 0:3] = given[0:1].astype(f32)
        lane = lax.broadcasted_iota(jnp.int32, (8, LANES), 1)
        swaps_beside = pltpu.roll(pltpu.roll(own[...], NB, 1), 7, 0)
        own[...] = jnp.where(lane < NB, own[...], swaps_beside)
        for n, (out, chosen, inside) in enumerate(((up, UPWARD, 8 - PLANE), (down, DOWNWARD, 0))):
            after = collide([cells[n, p] for p in range(Q)], solid[n] > 0)
            for m, p in enumerate(chosen):
                out[pl.ds(m * PLANE, PLANE), :] = after[p][inside : inside + PLANE]
            out[pl.ds(faces, 4), :] = own[4:8]
        send_sides(position()[1], up, down, near, far)

    def collide_kernel(cells, solid, post):
        for start in range(0, WHOLE, 8):
            here = pl.ds(start, 8)
            after = collide([cells[p, here, :] for p in range(Q)], solid[here, :] > 0)
            for p in range(Q):
                post[p, pl.ds(8 + start, 8), :] = after[p]
            post[Q, pl.ds(8 + start, 8), :] = solid[here, :].astype(f32)

    def pack_kernel(post, own, far, near, *outs):
        me, odd = position()
        below, above = sides(odd, near, far)
        outs = by_owner(outs, order_in)
        lane = lax.broadcasted_iota(jnp.int32, (8, LANES), 1)
        tail_below = pltpu.roll(below[faces - 4 : faces + 4], FIELDS, 1)
        tail_above = pltpu.roll(above[faces - 4 : faces + 4], 2 * FIELDS, 1)
        header = jnp.where(lane < 2 * FIELDS, tail_below, tail_above)
        header = jnp.where(lane < FIELDS, own[...], header)
        for d in range(owners):
            out = outs[d]
            place = dynamic_place(me ^ d, odd, owners)
            here = pl.multiple_of(place * share, min(share, 8))
            for p in range(Q + 1):
                cx = VELOCITIES[p][0] if p < Q else 0
                out[pl.ds(p * share, share), :] = post[p, pl.ds(8 + here - cx * PLANE, share), :]
            out[pl.ds(head, 8), :] = header

            @pl.when(place == 0)
            def _():
                for n, p in enumerate(UPWARD):
                    out[pl.ds(p * share, PLANE), :] = below[n * PLANE : (n + 1) * PLANE]

            @pl.when(place == owners - 1)
            def _():
                for n, p in enumerate(DOWNWARD):
                    out[pl.ds(p * share + share - PLANE, PLANE), :] = above[
                        n * PLANE : (n + 1) * PLANE
                    ]

    def seats(blocks):
        return [(b % NB, pl.multiple_of((b // NB) * block, block)) for b in blocks]

    def place_in(d, blocks, message, lattice):
        for t, (kz, y) in enumerate(seats(blocks)):
            for p in range(Q + 1):
                lattice[p, kz, pl.ds(y, block), :] = message[
                    pl.ds(p * share + t, block, stride=NB), :
                ]

    early = [0, half, 2, 3]
    late = [d for d in order_in if d not in early]

    def early_kernel(*refs):
        *got, lattice, table, sem = refs
        copies = [
            pltpu.make_async_copy(ref.at[pl.ds(head + 4, 1), :], table.at[pl.ds(n, 1), :], sem.at[n])
            for n, ref in enumerate(got)
        ]
        for copy in copies:
            copy.start()
        for copy in copies:
            copy.wait()
        for n, d in enumerate(early):
            blocks = [table[n, t].astype(jnp.int32) for t in range(NB)]
            place_in(d, blocks, got[n], lattice)

    def middle_kernel(*refs):
        got = by_owner(refs[:owners], order_in)
        lattice = refs[owners]
        outs = by_owner(refs[owners + 1 : 2 * owners + 1], order_out)
        _, ready, table, sem = refs[2 * owners + 1 :]
        me, odd = position()
        place = dynamic_place(me, odd, owners)
        first, last = place == 0, place == owners - 1
        copies = [
            pltpu.make_async_copy(
                got[d].at[pl.ds(head + 4, 1), :], table.at[pl.ds(d, 1), :], sem.at[d]
            )
            for d in range(owners)
        ]
        for copy in copies:
            copy.start()
        for copy in copies:
            copy.wait()

        def number(d, which, field):
            return table[d, which * FIELDS + field].astype(jnp.int32)

        other = jnp.where(first, 1, jnp.where(last, 2, 0))

        def held(d, which):
            return [number(d, which, t) for t in range(NB)]

        def final(d, which):
            def lead(e, r):
                return number(d ^ e, which, NB + r)

            flip = lead(0, 2) + lead(4, 2) + lead(4, 1) + lead(6, 1) + lead(6, 0) + lead(7, 0)
            one, two = held(d ^ 7, which)
            crossed = flip % 2 == 1
            return [jnp.where(crossed, two, one), jnp.where(crossed, one, two)]

        for d in late:
            place_in(d, held(d, 0), got[d], lattice)

        def bring(chosen, i):
            for d in range(owners):
                for t, (kz, y) in enumerate(seats(held(d, other))):
                    for p in chosen:
                        lattice[p, kz, pl.ds(y + i * PLANE_ROWS, PLANE_ROWS), :] = got[d][
                            pl.ds(p * share + i * PLANE + t, PLANE_ROWS, stride=NB), :
                        ]

        @pl.when(first)
        def _():
            bring(UPWARD, 0)

        @pl.when(last)
        def _():
            bring(DOWNWARD, planes - 1)

        lane = lax.broadcasted_iota(jnp.int32, (rows, LANES), 1)
        row = lax.broadcasted_iota(jnp.int32, (rows, LANES), 0)

        def passed(pair, p):
            cx, cy, cz = VELOCITIES[p]
            if cy:
                pair = [shift_y(value, cy, lane, row, block) for value in pair]
            if cz:
                pair = [shift_z(pair[kz], pair[1 - kz], cz, lane) for kz in range(NB)]
            return pair

        for p in range(Q):
            pair = passed([lattice[p, kz] for kz in range(NB)], p)
            for kz in range(NB):
                ready[p, kz] = pair[kz]
        for kz in range(NB):
            for start in range(0, rows, 16):
                here = pl.ds(start, 16)
                after = collide(
                    [ready[p, kz, here, :] for p in range(Q)], lattice[Q, kz, here, :] > 0.5
                )
                for p in range(Q):
                    lattice[p, kz, here, :] = after[p]
        for p in range(Q):
            pair = passed([lattice[p, kz] for kz in range(NB)], p)
            for kz in range(NB):
                ready[p, kz] = pair[kz]
        for d in range(owners):
            for t, (kz, y) in enumerate(seats(final(d, 0))):
                for p in range(Q):
                    outs[d][pl.ds(p * share + t, block, stride=NB), :] = ready[
                        p, kz, pl.ds(y, block), :
                    ]

        def bring_back(chosen, i):
            for d in range(owners):
                for t, (kz, y) in enumerate(seats(final(d, other))):
                    for p in chosen:
                        outs[d][
                            pl.ds(p * share + i * PLANE + t, PLANE_ROWS, stride=NB), :
                        ] = ready[p, kz, pl.ds(y + i * PLANE_ROWS, PLANE_ROWS), :]

        @pl.when(last)
        def _():
            bring_back(UPWARD, planes - 1)

        @pl.when(first)
        def _():
            bring_back(DOWNWARD, 0)

    def crossing_kernel(*refs):
        got = by_owner(refs[:owners], order_out)
        near, far, up, down = refs[owners:]
        me, odd = position()
        for d in range(owners):
            place = dynamic_place(me ^ d, odd, owners)

            @pl.when(place == owners - 1)
            def _():
                for n, p in enumerate(UPWARD):
                    up[pl.ds(n * PLANE, PLANE), :] = got[d][
                        pl.ds(p * share + share - PLANE, PLANE), :
                    ]

            @pl.when(place == 0)
            def _():
                for n, p in enumerate(DOWNWARD):
                    down[pl.ds(n * PLANE, PLANE), :] = got[d][pl.ds(p * share, PLANE), :]

        for out in (up, down):
            out[pl.ds(faces, 4), :] = jnp.zeros((4, LANES), f32)
        send_sides(odd, up, down, near, far)

    ends = [(p, 0) for p in UPWARD] + [(p, WHOLE - 8) for p in DOWNWARD]

    def unpack_kernel(*refs):
        got, (out, edge, main, sem) = by_owner(refs[:owners], order_out), refs[owners:]
        me, odd = position()
        for d in range(owners):
            place = dynamic_place(me ^ d, odd, owners)
            here = pl.multiple_of(place * share, min(share, 8))
            for p in range(Q):
                cx = VELOCITIES[p][0]
                main[p, pl.ds(8 + here + cx * PLANE, share), :] = got[d][
                    pl.ds(p * share, share), :
                ]
        copy = pltpu.make_async_copy(main.at[:, pl.ds(8, WHOLE), :], out, sem.at[0])
        copy.start()
        for n, (p, start) in enumerate(ends):
            edge[n] = main[p, pl.ds(8 + start, 8), :]
        copy.wait()

    def finish_kernel(_, edge, far, near, out, patch, sem):
        below, above = sides(position()[1], near, far)
        for n in range(len(ends)):
            patch[n] = edge[n]
        for n in range(len(UPWARD)):
            patch[n, pl.ds(0, PLANE), :] = below[n * PLANE : (n + 1) * PLANE]
            patch[len(UPWARD) + n, pl.ds(8 - PLANE, PLANE), :] = above[n * PLANE : (n + 1) * PLANE]
        copies = [
            pltpu.make_async_copy(patch.at[n], out.at[p, pl.ds(start, 8), :], sem.at[n])
            for n, (p, start) in enumerate(ends)
        ]
        for copy in copies:
            copy.start()
        for copy in copies:
            copy.wait()

    def shape(*dims):
        return jax.ShapeDtypeStruct(dims, f32)

    def call(
        kernel,
        name,
        out_shape,
        inputs,
        cost,
        scratch=(),
        spec=VMEM_SPEC,
        limit=40,
        aliases=None,
        out_specs=None,
    ):
        outs = out_specs or jax.tree.map(lambda _: VMEM_SPEC, out_shape)
        specs = spec if isinstance(spec, tuple) else (spec,) * len(inputs)
        return pl.pallas_call(
            kernel,
            out_shape=out_shape,
            in_specs=specs,
            out_specs=outs,
            scratch_shapes=list(scratch),
            input_output_aliases=aliases or {},
            compiler_params=pltpu.CompilerParams(vmem_limit_bytes=limit * 1024 * 1024),
            cost_estimate=pl.CostEstimate(flops=cost, bytes_accessed=cost, transcendentals=0),
            name=name,
        )(*inputs)

    def exchange(parts, order):
        return [parts[0]] + [
            lax.ppermute(parts[n], "gx", [(g, g ^ order[n]) for g in range(owners)])
            for n in range(1, owners)
        ]

    def hop(near, far):
        ahead = [(s + 1) % slabs if s % 2 == 0 else (s - 1) % slabs for s in range(slabs)]
        behind = [(s - 1) % slabs if s % 2 == 0 else (s + 1) % slabs for s in range(slabs)]
        far = lax.ppermute(far, "gy", list(enumerate(behind)))
        return lax.ppermute(near, "gy", list(enumerate(ahead))), far

    def padded(count):
        return shape(count, 8 + WHOLE + 8, LANES)

    whole_lattice = (Q + 1, NB, rows, LANES)
    small, large = 100_000, 4_000_000

    def shards(populations, solid_mask, slot_blocks, swap_slots):
        tiles = B * B * B // LANES
        pops = populations[0].transpose(1, 0, 2).reshape(Q, NB, tiles, LANES)
        pops = pops.transpose(0, 2, 1, 3).reshape(Q, WHOLE, LANES)
        mask = solid_mask[0].reshape(NB, tiles, LANES).transpose(1, 0, 2).reshape(WHOLE, LANES)
        swaps = swap_slots[0, 0].T
        in_place = pl.BlockSpec(memory_space=pltpu.HBM)
        near, far, own = call(
            edge_kernel,
            "edge_planes",
            (shape(rows_hop, LANES), shape(rows_hop, LANES), shape(8, LANES)),
            (pops, mask, slot_blocks, swaps),
            small,
            (
                pltpu.VMEM((rows_hop, LANES), f32),
                pltpu.VMEM((rows_hop, LANES), f32),
                pltpu.VMEM((2, Q, 8, LANES), f32),
                pltpu.VMEM((2, 8, LANES), jnp.int32),
                pltpu.VMEM(slot_blocks.shape, jnp.int32),
                pltpu.VMEM(swaps.shape, jnp.int32),
                pltpu.SemaphoreType.DMA((6,)),
            ),
            in_place,
            62,
        )
        near, far = hop(near, far)
        post = call(
            collide_kernel,
            "first_collision",
            padded(Q + 1),
            (pops, mask),
            large,
        )
        parts = call(
            pack_kernel,
            "pack_planes",
            (shape(rows_in, LANES),) * owners,
            (post, own, far, near),
            large,
        )
        got = exchange(parts, order_in)
        lattice = call(
            early_kernel,
            "place_early",
            shape(*whole_lattice),
            [got[order_in.index(d)] for d in early],
            large,
            (pltpu.SMEM((len(early), LANES), f32), pltpu.SemaphoreType.DMA((len(early),))),
        )
        *parts, _ = call(
            middle_kernel,
            "second_step",
            (shape(rows_out, LANES),) * owners + (shape(*whole_lattice),),
            (*got, lattice),
            large,
            (
                pltpu.VMEM(whole_lattice, f32),
                pltpu.SMEM((owners, LANES), f32),
                pltpu.SemaphoreType.DMA((owners,)),
            ),
            aliases={owners: owners},
        )
        home = exchange(parts, order_out)
        near, far = call(
            crossing_kernel,
            "crossing_planes",
            (shape(rows_hop, LANES),) * 2,
            home,
            small,
            (pltpu.VMEM((rows_hop, LANES), f32),) * 2,
        )
        near, far = hop(near, far)
        out, edge = call(
            unpack_kernel,
            "unpack_planes",
            (shape(Q, WHOLE, LANES), shape(len(ends), 8, LANES)),
            home,
            large,
            (pltpu.VMEM((Q, 8 + WHOLE + 8, LANES), f32), pltpu.SemaphoreType.DMA((1,))),
            out_specs=(in_place, VMEM_SPEC),
        )
        out = call(
            finish_kernel,
            "finish",
            shape(Q, WHOLE, LANES),
            (out, edge, far, near),
            small,
            (pltpu.VMEM((len(ends), 8, LANES), f32), pltpu.SemaphoreType.DMA((len(ends),))),
            spec=(in_place, VMEM_SPEC, VMEM_SPEC, VMEM_SPEC),
            aliases={0: 0},
            out_specs=in_place,
        )
        out = out.reshape(Q, tiles, NB, LANES).transpose(0, 2, 1, 3)
        return out.reshape(Q, NB, B * B * B).transpose(1, 0, 2)[None]

    return shards


def solution(mesh):
    return jax.shard_map(
        build(mesh),
        mesh=mesh,
        in_specs=(
            P("gy", "gx", None, None),
            P("gy", "gx", None),
            P("gy", "gx"),
            P("gy", "gx", None, None),
        ),
        out_specs=P("gy", "gx", None, None),
        check_vma=False,
    )
```
